32 devices in a mesh: member: 8 (over z, x), wave: 4 (over y, core).
Axes of the slice: x: 2, y: 2, z: 4, core: 2. Of those that a mesh axis runs over, the one named last changes fastest.
Arguments:
- state: float32 [8, 32, 32, 640], P('member', 'wave'), may hold values from -6 to 6
- legendre: bfloat16 [32, 640, 640], P('wave'), may hold values from -0.25 to 0.25
- lat_weights: float32 [640], replicated, may hold values from 0.5 to 2
- region: int32 [4], replicated, may hold values from 0 to 2560, as said below
- sources: int32 [8], replicated, may hold values from 0 to 7, as said below
Outputs:
- new_states: float32 [8, 32, 32, 640], P('member', 'wave')
- scores: float32 [8], P('member')
The draws below stay inside these ranges and needn't reach their ends.
Inputs may be any that keep to these rules, and one draw needn't show every extreme that they name: region[0] < region[1] bound the latitudes and region[2] < region[3] the longitudes of the region; each band covers at least half of its grid dimension; the longitude band ends at the last longitude, region[3] = 2560. `sources`: some member is the source of at least 2 slots.
All inputs are finite; a program needn't handle non-finite values.
Results may differ from the reference program's by a relative error of at most 0.0059.
Values may be sent and summed in bfloat16 or wider, within the bound.
A program may use at most 128 MiB of HBM per device.

```python
import math
import jax
import jax.numpy as jnp
from jax import lax

NDEG = 640
NLAT = 640
NLON = 2560
LEV = 8
MW = 32
ROWS = 32
MEMBERS = 8


def draw_region(key, part):
    keys = jax.random.split(jax.random.fold_in(key, 11), 3)
    lat_low = jax.random.randint(keys[0], (), 0, NLAT // 8)
    lat_high = NLAT - jax.random.randint(keys[1], (), 0, NLAT // 8)
    lon_low = jax.random.randint(keys[2], (), 0, NLON // 2)
    lon_high = jnp.int32(NLON) + 0 * lon_low
    return jnp.stack([lat_low, lat_high, lon_low, lon_high]).astype(jnp.int32)


def draw_sources(key, part):
    keys = jax.random.split(jax.random.fold_in(key, 7), 2)
    picks = jax.random.randint(keys[0], (MEMBERS,), 0, MEMBERS)
    favored = jax.random.randint(keys[1], (), 0, MEMBERS)
    slots = jnp.arange(MEMBERS)
    offset = (slots - favored) % MEMBERS
    picks = jnp.where((offset >= 1) & (offset <= MEMBERS // 4), favored, picks)
    picks = jnp.where(offset == MEMBERS // 4 + 1, 0, picks)
    picks = jnp.where(offset == MEMBERS // 4 + 2, MEMBERS - 1, picks)
    picks = jnp.where(offset == MEMBERS // 2 + 1, (favored + 1) % MEMBERS, picks)
    return picks.astype(jnp.int32)


def levels(key, extent, pieces, smallest, high):
    def one(dim, parts):
        steps = jax.random.uniform(jax.random.fold_in(jax.random.fold_in(key, 6), dim), (parts,), jnp.float32, smallest / len(pieces), high / len(pieces))
        return jnp.repeat(jnp.exp(steps), extent[dim] // parts).reshape((-1,) + (1,) * (len(extent) - dim - 1))

    loudness = one(*pieces[0])
    for cut in pieces[1:]:
        loudness = loudness * one(*cut)
    return loudness


def noise(rng, extent, spread, reach, pieces=(), dtype=jnp.bfloat16):
    result = spread * jax.random.normal(rng, extent, jnp.float32)
    if pieces:
        result = result * levels(rng, extent, pieces, -0.22, 0.18)
    return jnp.clip(result, -reach, reach).astype(dtype)


def setup_inputs(seed: int = 0) -> dict:
    key_list = jax.random.split(jax.random.key(seed), 6)
    state = noise(key_list[0], (MEMBERS, MW, ROWS, NDEG), 1.0, 6.0, ((0, 8), (1, 4)), jnp.float32)
    legendre = noise(key_list[1], (MW, NDEG, NLAT), NDEG ** -0.5, 0.25, ((0, 4),))
    lat_weights = jnp.clip(jnp.exp(jax.random.uniform(key_list[2], (NLAT,), jnp.float32, math.log(0.5), math.log(2.0))), 0.5, 2.0)
    region = draw_region(jax.random.fold_in(key_list[5], 71), 0)
    sources = draw_sources(jax.random.fold_in(key_list[5], 71), 0)
    return dict(state=state, legendre=legendre, lat_weights=lat_weights, region=region, sources=sources)


advect_rate = 2.0


def fourier_table(waves_total, points):
    wave_index = lax.broadcasted_iota(jnp.int32, (waves_total, points), 0)
    column_index = lax.broadcasted_iota(jnp.int32, (waves_total, points), 1)
    angles = ((wave_index * column_index) % points).astype(jnp.float32) * (2.0 * jnp.pi / points)
    return jnp.stack([jnp.cos(angles), -jnp.sin(angles)], axis=1).astype(jnp.bfloat16)


def advance(state_one, legendre, lat_weights, region, fourier):
    spectral = lax.optimization_barrier(state_one.astype(jnp.bfloat16)).astype(jnp.float32)
    legendre_wide = legendre.astype(jnp.float32)
    fourier_wide = fourier.astype(jnp.float32)
    fourier_coef = jnp.einsum('mrn,mnl->mrl', spectral, legendre_wide).astype(jnp.bfloat16)
    fourier_coef = lax.optimization_barrier(fourier_coef).astype(jnp.float32).reshape(MW, 2, 2 * LEV, NLAT)
    gridded = (2.0 * MW) ** -0.5 * jnp.einsum('mckl,mcx->klx', fourier_coef, fourier_wide)
    wind_grid = gridded[:LEV]
    temper_grid = gridded[LEV:]
    weights_column = lat_weights[None, :, None]
    fluxes = jnp.concatenate([0.5 * wind_grid * wind_grid, wind_grid * temper_grid], axis=0) * weights_column
    fluxes = lax.optimization_barrier(fluxes.astype(jnp.bfloat16)).astype(jnp.float32)
    lat_index = lax.broadcasted_iota(jnp.int32, (NLAT, 1), 0)
    lon_index = lax.broadcasted_iota(jnp.int32, (1, NLON), 1)
    lat_inside = (lat_index >= region[0]) & (lat_index < region[1])
    in_region = lat_inside & (lon_index >= region[2]) & (lon_index < region[3])
    lowest = temper_grid[LEV - 1]
    region_total = jnp.sum(jnp.where(in_region, lat_weights[:, None] * lowest * lowest, jnp.float32(0.0)))
    region_weight = jnp.sum(jnp.where(lat_inside[:, 0], lat_weights, jnp.float32(0.0))) * (region[3] - region[2]).astype(jnp.float32)
    score_value = region_total / region_weight
    flux_coef = (NLON ** -0.5 * jnp.einsum('klx,mcx->mckl', fluxes, fourier_wide)).astype(jnp.bfloat16)
    flux_coef = lax.optimization_barrier(flux_coef).astype(jnp.float32)
    tendency = jnp.einsum('mckl,mnl->mckn', flux_coef, legendre_wide)
    wave_ids = lax.broadcasted_iota(jnp.int32, (MW, 1, 1), 0).astype(jnp.float32)
    advection = advect_rate * wave_ids / MW
    degree_ids = lax.broadcasted_iota(jnp.int32, (1, 1, NDEG), 2).astype(jnp.float32)
    damping = 1.0 + ((degree_ids + 1.0) / NDEG) ** 2
    spectral_split = state_one.reshape(MW, 2, 2 * LEV, NDEG)
    real_part = (spectral_split[:, 0] + advection * tendency[:, 1]) / damping
    imag_part = (spectral_split[:, 1] - advection * tendency[:, 0]) / damping
    stepped = jnp.stack([real_part, imag_part], axis=1).reshape(MW, ROWS, NDEG)
    return stepped, score_value


def reference(state, legendre, lat_weights, region, sources):
    fourier = fourier_table(MW, NLON)
    stepped, scores = lax.map(lambda single: advance(single, legendre, lat_weights, region, fourier), state)
    new_states = jnp.take(stepped, sources, axis=0)
    return new_states, scores
```

```python
import jax
import jax.numpy as jnp
import numpy as np
from jax import lax
from jax.sharding import PartitionSpec as P

NLON = 2560


advect_rate = 2.0


def wave_table(waves_total, points):
    wave_index = np.arange(waves_total)[:, None]
    angles = (wave_index * np.arange(points)[None, :] % points) * (2.0 * np.pi / points)
    return np.stack([np.cos(angles), -np.sin(angles)], axis=1)


def split_table(table):
    high = table.astype(jnp.bfloat16)
    low = (table - high.astype(np.float64)).astype(jnp.bfloat16)
    return high, low


def quadrature_points(waves_total):
    return (3 * (waves_total - 1)) // 128 * 128 + 128


def on_device(state, legendre, lat_weights, region, sources):
    wave_count = lax.axis_size("wave")
    waves_local = legendre.shape[0]
    waves_total = waves_local * wave_count
    degrees = legendre.shape[1]
    latitudes = legendre.shape[2]
    lat_rows = latitudes // wave_count
    state_rows = state.shape[2]
    level_count = state_rows // 4
    points = quadrature_points(waves_total)
    table_high, table_low = split_table(wave_table(waves_total, points))
    spectral = state[0]
    fourier_coef = jnp.einsum(
        "mrn,mnl->mrl", spectral.astype(jnp.bfloat16), legendre, preferred_element_type=jnp.float32
    )
    fourier_coef = fourier_coef.astype(jnp.bfloat16).reshape(
        waves_local, 2, 2 * level_count, latitudes
    )
    synthesis_scale = (2.0 * waves_total) ** (-0.5)
    coef = lax.all_to_all(fourier_coef, "wave", split_axis=3, concat_axis=0, tiled=True)
    gridded = synthesis_scale * jnp.einsum(
        "mckl,mcx->klx",
        jnp.concatenate([coef, coef], axis=1),
        jnp.concatenate([table_high, table_low], axis=1),
        preferred_element_type=jnp.float32,
    )
    lat_start = lax.axis_index("wave") * lat_rows
    local_weights = lax.dynamic_slice_in_dim(lat_weights, lat_start, lat_rows)
    wind_grid = gridded[:level_count]
    temper_grid = gridded[level_count:]
    fluxes = (
        jnp.concatenate([0.5 * wind_grid * wind_grid, wind_grid * temper_grid], axis=0)
        * local_weights[None, :, None]
    )
    fluxes = fluxes.astype(jnp.bfloat16)
    fourier = wave_table(waves_total, NLON).reshape(2 * waves_total, NLON).astype(jnp.bfloat16)
    lon_index = lax.broadcasted_iota(jnp.int32, (1, NLON), 1)
    lon_inside = (lon_index >= region[2]) & (lon_index < region[3])
    gram = jnp.einsum(
        "px,qx->pq",
        jnp.where(lon_inside, fourier, jnp.zeros((), jnp.bfloat16)),
        fourier,
        preferred_element_type=jnp.float32,
    )
    lowest = coef[:, :, -1].reshape(2 * waves_total, lat_rows).astype(jnp.float32)
    gram_lowest = jnp.dot(gram, lowest, precision=lax.Precision.HIGHEST)
    lat_index = lat_start + lax.broadcasted_iota(jnp.int32, (lat_rows,), 0)
    in_band = (lat_index >= region[0]) & (lat_index < region[1])
    region_part = jnp.sum(
        jnp.where(in_band, local_weights, 0.0)[None, :] * lowest * gram_lowest
    ) / (2.0 * waves_total)
    region_total = lax.psum(region_part, "wave")
    every_lat = lax.broadcasted_iota(jnp.int32, (latitudes,), 0)
    lat_inside = (every_lat >= region[0]) & (every_lat < region[1])
    region_weight = jnp.sum(jnp.where(lat_inside, lat_weights, 0.0)) * (
        region[3] - region[2]
    ).astype(jnp.float32)
    scores = (region_total / region_weight).reshape(1)
    analysis_scale = NLON ** (-0.5) * (NLON / points)
    flux_high = jnp.einsum("klx,mcx->mckl", fluxes, table_high, preferred_element_type=jnp.float32)
    flux_low = jnp.einsum("klx,mcx->mckl", fluxes, table_low, preferred_element_type=jnp.float32)
    flux_coef = (analysis_scale * (flux_high + flux_low)).astype(jnp.bfloat16)
    tendency = jnp.einsum(
        "mckl,mnl->mckn",
        lax.all_to_all(flux_coef, "wave", split_axis=0, concat_axis=3, tiled=True),
        legendre,
        preferred_element_type=jnp.float32,
    )
    wave_ids = lax.axis_index("wave") * waves_local + lax.broadcasted_iota(
        jnp.int32, (waves_local, 1, 1), 0
    )
    advection = advect_rate * wave_ids.astype(jnp.float32) / waves_total
    degree_ids = lax.broadcasted_iota(jnp.int32, (1, 1, degrees), 2).astype(jnp.float32)
    damping = 1.0 + ((degree_ids + 1.0) / degrees) ** 2
    spectral_split = spectral.reshape(waves_local, 2, 2 * level_count, degrees)
    real_part = (spectral_split[:, 0] + advection * tendency[:, 1]) / damping
    imag_part = (spectral_split[:, 1] - advection * tendency[:, 0]) / damping
    stepped = jnp.stack([real_part, imag_part], axis=1).reshape(1, waves_local, state_rows, degrees)
    source_member = sources[lax.axis_index("member")]
    shards = lax.all_gather(stepped.astype(jnp.bfloat16), "member", axis=0, tiled=True)
    cloned = lax.dynamic_slice_in_dim(shards, source_member, 1, axis=0).astype(jnp.float32)
    return (cloned, scores)


def solution(mesh):
    in_specs = (P("member", "wave", None, None), P("wave", None, None), P(), P(), P())
    out_specs = (P("member", "wave", None, None), P("member"))
    return jax.shard_map(
        on_device, mesh=mesh, in_specs=in_specs, out_specs=out_specs, check_vma=False
    )
```

```python
import functools

import jax
import jax.numpy as jnp
import numpy as np
from jax import lax
from jax.experimental import pallas as pl
from jax.experimental.pallas import tpu as pltpu
from jax.sharding import PartitionSpec as P

NLON = 2560


advect_rate = 2.0


def wave_table(waves_total, points):
    wave_index = np.arange(waves_total)[:, None]
    angles = (wave_index * np.arange(points)[None, :] % points) * (2.0 * np.pi / points)
    return np.stack([np.cos(angles), -np.sin(angles)], axis=1)


def split_table(table):
    high = table.astype(jnp.bfloat16)
    low = (table - high.astype(np.float64)).astype(jnp.bfloat16)
    return high, low


def quadrature_points(waves_total):
    return (3 * (waves_total - 1)) // 128 * 128 + 128


def on_device(state, legendre, lat_weights, region, sources):
    wave_count = lax.axis_size("wave")
    waves_local = legendre.shape[0]
    waves_total = waves_local * wave_count
    degrees = legendre.shape[1]
    latitudes = legendre.shape[2]
    lat_rows = latitudes // wave_count
    state_rows = state.shape[2]
    level_count = state_rows // 4
    points = quadrature_points(waves_total)
    table_high, table_low = split_table(wave_table(waves_total, points))
    spectral = state[0]
    fourier_coef = jnp.einsum(
        "mrn,mnl->mrl", spectral.astype(jnp.bfloat16), legendre, preferred_element_type=jnp.float32
    )
    fourier_coef = fourier_coef.astype(jnp.bfloat16).reshape(
        waves_local, 2, 2 * level_count, latitudes
    )
    synthesis_scale = (2.0 * waves_total) ** (-0.5)
    coef = lax.all_to_all(fourier_coef, "wave", split_axis=3, concat_axis=0, tiled=True)
    gridded = synthesis_scale * jnp.einsum(
        "mckl,mcx->klx",
        jnp.concatenate([coef, coef], axis=1),
        jnp.concatenate([table_high, table_low], axis=1),
        preferred_element_type=jnp.float32,
    )
    lat_start = lax.axis_index("wave") * lat_rows
    local_weights = lax.dynamic_slice_in_dim(lat_weights, lat_start, lat_rows)
    wind_grid = gridded[:level_count]
    temper_grid = gridded[level_count:]
    fluxes = (
        jnp.concatenate([0.5 * wind_grid * wind_grid, wind_grid * temper_grid], axis=0)
        * local_weights[None, :, None]
    )
    fluxes = fluxes.astype(jnp.bfloat16)
    fourier = wave_table(waves_total, NLON).reshape(2 * waves_total, NLON).astype(jnp.bfloat16)
    lon_index = lax.broadcasted_iota(jnp.int32, (1, NLON), 1)
    lon_inside = (lon_index >= region[2]) & (lon_index < region[3])
    gram = jnp.einsum(
        "px,qx->pq",
        jnp.where(lon_inside, fourier, jnp.zeros((), jnp.bfloat16)),
        fourier,
        preferred_element_type=jnp.float32,
    )
    lowest = coef[:, :, -1].reshape(2 * waves_total, lat_rows).astype(jnp.float32)
    gram_lowest = jnp.dot(gram, lowest, precision=lax.Precision.HIGHEST)
    lat_index = lat_start + lax.broadcasted_iota(jnp.int32, (lat_rows,), 0)
    in_band = (lat_index >= region[0]) & (lat_index < region[1])
    region_part = jnp.sum(
        jnp.where(in_band, local_weights, 0.0)[None, :] * lowest * gram_lowest
    ) / (2.0 * waves_total)
    region_total = lax.psum(region_part, "wave")
    every_lat = lax.broadcasted_iota(jnp.int32, (latitudes,), 0)
    lat_inside = (every_lat >= region[0]) & (every_lat < region[1])
    region_weight = jnp.sum(jnp.where(lat_inside, lat_weights, 0.0)) * (
        region[3] - region[2]
    ).astype(jnp.float32)
    scores = (region_total / region_weight).reshape(1)
    analysis_scale = NLON ** (-0.5) * (NLON / points)
    flux_high = jnp.einsum("klx,mcx->mckl", fluxes, table_high, preferred_element_type=jnp.float32)
    flux_low = jnp.einsum("klx,mcx->mckl", fluxes, table_low, preferred_element_type=jnp.float32)
    flux_coef = (analysis_scale * (flux_high + flux_low)).astype(jnp.bfloat16)
    tendency = jnp.einsum(
        "mckl,mnl->mckn",
        lax.all_to_all(flux_coef, "wave", split_axis=0, concat_axis=3, tiled=True),
        legendre,
        preferred_element_type=jnp.float32,
    )
    wave_ids = lax.axis_index("wave") * waves_local + lax.broadcasted_iota(
        jnp.int32, (waves_local, 1, 1), 0
    )
    advection = advect_rate * wave_ids.astype(jnp.float32) / waves_total
    degree_ids = lax.broadcasted_iota(jnp.int32, (1, 1, degrees), 2).astype(jnp.float32)
    damping = 1.0 + ((degree_ids + 1.0) / degrees) ** 2
    spectral_split = spectral.reshape(waves_local, 2, 2 * level_count, degrees)
    real_part = (spectral_split[:, 0] + advection * tendency[:, 1]) / damping
    imag_part = (spectral_split[:, 1] - advection * tendency[:, 0]) / damping
    stepped = jnp.stack([real_part, imag_part], axis=1).reshape(1, waves_local, state_rows, degrees)
    source_member = sources[lax.axis_index("member")]
    shards = lax.all_gather(stepped.astype(jnp.bfloat16), "member", axis=0, tiled=True)
    cloned = lax.dynamic_slice_in_dim(shards, source_member, 1, axis=0).astype(jnp.float32)
    return (cloned, scores)


MESH = pl.DeviceIdType.MESH
WAVES = 4
CHUNKS = 4
PAIR = 2
ROWS = 32
CHUNK_ROWS = PAIR * ROWS
PART_ROWS = CHUNK_ROWS // WAVES
OWNED_ROWS = CHUNKS * PART_ROWS


def order_tables(levels):
    held = levels // WAVES
    forward = np.zeros((CHUNK_ROWS, CHUNK_ROWS))
    backward = np.zeros((CHUNK_ROWS, CHUNK_ROWS))
    for m in range(PAIR):
        for c in range(2):
            for f in range(2):
                for k in range(levels):
                    plain = ((m * 2 + c) * 2 + f) * levels + k
                    owner = ((((k // held) * PAIR + m) * 2 + c) * 2 + f) * held + k % held
                    crossed = ((((k // held) * PAIR + m) * 2 + (1 - c)) * 2 + f) * held + k % held
                    forward[owner, plain] = 1.0
                    backward[plain, crossed] = 1.0 - 2.0 * c
    return forward.astype(jnp.bfloat16), backward.astype(jnp.bfloat16)


def grid_tables(table):
    waves, _, points = table.shape
    wide = np.einsum("mcx,fg,kl->lgxmcfk", table, np.eye(2), np.eye(2))
    return split_table(wide.reshape(4 * points, 8 * waves))


def step_kernel(
    state_ref, legendre_ref, weights_ref, region_ref, sources_ref, synth_ref, analysis_ref,
    forward_ref, backward_ref, pick_ref, fourier_ref,
    out_ref, score_ref,
    leg, sent, held, flux, back_sent, back, score_buf, cross, crossed,
    pool0, pool1, pool2, pool3,
    leg_sem, go_send, go_recv, ret_send, ret_recv, score_send, score_recv,
    pass_send, pass_recv, cross_send, cross_recv,
    *, scale, analysis_scale, waves_total,
):
    pools = [pool0, pool1, pool2, pool3]
    me = lax.axis_index("wave")
    slot = lax.axis_index("member")
    z = slot // 2
    x = slot % 2
    half = z // 2
    inner = z % 2 != half % 2
    z_mate = (z + 1 - 2 * (z % 2)) * 2 + x
    x_mate = z * 2 + 1 - x
    far_inner = (2 - half) * 2 + x
    far_outer = (3 - 3 * half) * 2 + x
    here = slot - half * 4
    z_here = z_mate - half * 4
    points = synth_ref.shape[1] // 4
    degrees = state_ref.shape[1]
    lat_count = weights_ref.shape[1]

    loads = [
        pltpu.make_async_copy(legendre_ref.at[m], leg.at[m], leg_sem.at[m])
        for m in range(CHUNKS * PAIR)
    ]
    for load in loads:
        load.start()

    barrier = pltpu.get_barrier_semaphore()
    for d in range(1, WAVES):
        pl.semaphore_signal(
            barrier, inc=1, device_id={"wave": (me + d) % WAVES}, device_id_type=MESH
        )
    for mate in (z_mate, x_mate, far_inner):
        pl.semaphore_signal(barrier, inc=1, device_id={"member": mate}, device_id_type=MESH)

    @pl.when(inner)
    def _():
        pl.semaphore_signal(barrier, inc=1, device_id={"member": far_outer}, device_id_type=MESH)
        pl.semaphore_wait(barrier, 7)

    @pl.when(jnp.logical_not(inner))
    def _():
        pl.semaphore_wait(barrier, 6)

    def wave_copy(source, target, target_row, c, d, send_sem, recv_sem):
        to = (me + d) % WAVES
        return pltpu.make_async_remote_copy(
            src_ref=source.at[pl.ds(pl.multiple_of(to * OWNED_ROWS + c * PART_ROWS, PART_ROWS), PART_ROWS)],
            dst_ref=target.at[pl.ds(pl.multiple_of(target_row, PART_ROWS), PART_ROWS)],
            send_sem=send_sem.at[d - 1, c],
            recv_sem=recv_sem.at[d - 1, c],
            device_id={"wave": to},
            device_id_type=MESH,
        )

    my_rows = me * OWNED_ROWS
    go = []
    for c in range(CHUNKS):
        parts = []
        for m in range(c * PAIR, (c + 1) * PAIR):
            loads[m].wait()
            parts.append(
                jnp.dot(
                    state_ref[m * ROWS : (m + 1) * ROWS].astype(jnp.bfloat16),
                    leg[m],
                    preferred_element_type=jnp.float32,
                )
            )
        coef = jnp.concatenate(parts, axis=0).astype(jnp.bfloat16)
        ordered = jnp.dot(
            forward_ref[...], coef, preferred_element_type=jnp.float32
        ).astype(jnp.bfloat16)
        for w in range(WAVES):
            sent[w * OWNED_ROWS + c * PART_ROWS : w * OWNED_ROWS + (c + 1) * PART_ROWS] = ordered[
                w * PART_ROWS : (w + 1) * PART_ROWS
            ]
        for d in (2, 1, 3):
            copy = wave_copy(sent, held, my_rows + c * PART_ROWS, c, d, go_send, go_recv)
            copy.start()
            go.append(copy)
    mine = pl.ds(pl.multiple_of(my_rows, OWNED_ROWS), OWNED_ROWS)
    held[mine] = sent[mine]

    low, high = region_ref[2], region_ref[3]
    lon = lax.broadcasted_iota(jnp.int32, (1, fourier_ref.shape[1]), 1)
    lon_inside = jnp.where((lon >= low) & (lon < high), 1.0, 0.0)
    fourier = fourier_ref[...]
    gram = lax.dot_general(
        (fourier.astype(jnp.float32) * lon_inside).astype(jnp.bfloat16),
        fourier,
        (((1,), (1,)), ((), ())),
        preferred_element_type=jnp.float32,
    )
    gram_high = gram.astype(jnp.bfloat16)
    gram_low = (gram - gram_high.astype(jnp.float32)).astype(jnp.bfloat16)
    lat = lax.broadcasted_iota(jnp.int32, (1, lat_count), 1)
    weights = weights_ref[...]
    region_weights = jnp.where((lat >= region_ref[0]) & (lat < region_ref[1]), weights, 0.0)
    weight_sum = jnp.sum(region_weights, axis=1, keepdims=True) * (high - low).astype(jnp.float32)

    for copy in go:
        copy.wait_recv()

    coefs = held[...]
    scaled = weights * (scale * scale)
    for k in range(2):
        rows = slice(k * 2 * points, (k + 1) * 2 * points)
        grid = jnp.dot(
            synth_ref[0, rows], coefs, preferred_element_type=jnp.float32
        ) + jnp.dot(synth_ref[1, rows], coefs, preferred_element_type=jnp.float32)
        wind = grid[:points]
        weighted = wind * scaled
        flux[k * 2 * points : (k * 2 + 1) * points] = (0.5 * weighted * wind).astype(jnp.bfloat16)
        flux[(k * 2 + 1) * points : (k * 2 + 2) * points] = (weighted * grid[points:]).astype(
            jnp.bfloat16
        )
    fluxes = flux[...]
    back_sent[...] = (
        analysis_scale
        * (
            jnp.dot(analysis_ref[0], fluxes, preferred_element_type=jnp.float32)
            + jnp.dot(analysis_ref[1], fluxes, preferred_element_type=jnp.float32)
        )
    ).astype(jnp.bfloat16)
    ret = []
    for c in range(CHUNKS):
        for d in (2, 1, 3):
            copy = wave_copy(back_sent, back, my_rows + c * PART_ROWS, c, d, ret_send, ret_recv)
            copy.start()
            ret.append(copy)
    back[mine] = back_sent[mine]

    lowest = jnp.dot(pick_ref[...], coefs, preferred_element_type=jnp.float32)
    lowest_half = lowest.astype(jnp.bfloat16)
    spread = jnp.dot(gram_high, lowest_half, preferred_element_type=jnp.float32) + jnp.dot(
        gram_low, lowest_half, preferred_element_type=jnp.float32
    )
    squares = jnp.sum(lowest * spread, axis=0, keepdims=True) * (region_weights * (scale * scale))
    score = jnp.sum(squares, axis=1, keepdims=True) / weight_sum
    score = score * jnp.where(me == WAVES - 1, 1.0, 0.0)
    score_buf[me] = jnp.broadcast_to(score, score_buf.shape[1:])
    score_copies = []
    for d in range(1, WAVES):
        copy = pltpu.make_async_remote_copy(
            src_ref=score_buf.at[me],
            dst_ref=score_buf.at[me],
            send_sem=score_send.at[d - 1],
            recv_sem=score_recv.at[d - 1],
            device_id={"wave": (me + d) % WAVES},
            device_id_type=MESH,
        )
        copy.start()
        score_copies.append(copy)

    def member_copy(source, target, to, send_sem, recv_sem):
        return pltpu.make_async_remote_copy(
            src_ref=source, dst_ref=target, send_sem=send_sem, recv_sem=recv_sem,
            device_id={"member": to}, device_id_type=MESH,
        )

    def pass_copy(c, kind):
        which = z_here if kind == 2 else here
        block = pools[c].at[which]
        return member_copy(
            block, block, z_mate if kind == 0 else x_mate, pass_send.at[kind, c], pass_recv.at[kind, c]
        )

    def cross_copy(c, far):
        return member_copy(
            cross.at[c, far],
            crossed.at[c],
            far_outer if far else far_inner,
            cross_send.at[far, c],
            cross_recv.at[c],
        )

    def half_index(member_slot):
        return jnp.clip(sources_ref[member_slot] - half * 4, 0, 3)

    inner_pick = half_index(far_inner)
    outer_pick = half_index(far_outer)

    def forward_pass(c):
        pass_copy(c, 0).wait_recv()
        pass_copy(c, 2).start()

    def send_across(c):
        pass_copy(c, 1).wait_recv()
        pass_copy(c, 2).wait_recv()

        @pl.when(inner)
        def _():
            cross[c, 1] = pools[c][outer_pick]
            cross_copy(c, 1).start()
            cross[c, 0] = pools[c][inner_pick]
            cross_copy(c, 0).start()

    degree = lax.broadcasted_iota(jnp.int32, (1, degrees), 1).astype(jnp.float32)
    keep = 1.0 / (1.0 + ((degree + 1.0) / degrees) ** 2)
    for c in range(CHUNKS):
        for copy in ret[c * (WAVES - 1) : (c + 1) * (WAVES - 1)]:
            copy.wait_recv()
        arrived = jnp.concatenate(
            [
                back[w * OWNED_ROWS + c * PART_ROWS : w * OWNED_ROWS + (c + 1) * PART_ROWS]
                for w in range(WAVES)
            ],
            axis=0,
        )
        plain = jnp.dot(
            backward_ref[...], arrived, preferred_element_type=jnp.float32
        ).astype(jnp.bfloat16)
        for i in range(PAIR):
            m = c * PAIR + i
            tendency = lax.dot_general(
                plain[i * ROWS : (i + 1) * ROWS],
                leg[m],
                (((1,), (1,)), ((), ())),
                preferred_element_type=jnp.float32,
            )
            wave_id = (me * (CHUNKS * PAIR) + m).astype(jnp.float32)
            advection = wave_id * (advect_rate / waves_total)
            stepped = (state_ref[m * ROWS : (m + 1) * ROWS] + advection * tendency) * keep
            pools[c][here, i * ROWS : (i + 1) * ROWS] = stepped.astype(jnp.bfloat16)
        pass_copy(c, 0).start()
        pass_copy(c, 1).start()
        if c >= 1:
            forward_pass(c - 1)
        if c >= 3:
            send_across(c - 3)
    forward_pass(CHUNKS - 1)
    for c in range(CHUNKS - 3, CHUNKS):
        send_across(c)

    for copy in score_copies:
        copy.wait()
    score_ref[...] = score_buf[0] + score_buf[1] + score_buf[2] + score_buf[3]
    for copy in go + ret:
        copy.wait_send()

    origin = sources_ref[slot] - half * 4
    near = (origin >= 0) & (origin < 4)
    choice = jnp.clip(origin, 0, 3)
    for c in range(CHUNKS):
        cross_copy(c, 0).wait_recv()
        out_ref[c * CHUNK_ROWS : (c + 1) * CHUNK_ROWS] = jnp.where(
            near, pools[c][choice], crossed[c]
        )
    for c in range(CHUNKS):
        for kind in range(3):
            pass_copy(c, kind).wait_send()

    @pl.when(inner)
    def _():
        for c in range(CHUNKS):
            for far in range(2):
                cross_copy(c, far).wait_send()


def in_one_kernel(state, legendre, lat_weights, region, sources):
    waves_local, degrees, latitudes = legendre.shape
    waves_total = waves_local * WAVES
    points = quadrature_points(waves_total)
    levels = state.shape[2] // 4
    synth_high, synth_low = grid_tables(wave_table(waves_total, points))
    forward, backward = order_tables(levels)
    pick = np.zeros((2 * waves_total, 8 * waves_total))
    pick[np.arange(2 * waves_total), np.arange(2 * waves_total) * 4 + 3] = 1.0
    fourier = wave_table(waves_total, NLON).reshape(2 * waves_total, NLON).astype(jnp.bfloat16)
    vmem = pl.BlockSpec(memory_space=pltpu.VMEM)
    smem = pl.BlockSpec(memory_space=pltpu.SMEM)
    rows = waves_local * ROWS
    block = (rows, degrees)
    dma = pltpu.SemaphoreType.DMA
    cloned, scores = pl.pallas_call(
        functools.partial(
            step_kernel,
            scale=(2.0 * waves_total) ** -0.5,
            analysis_scale=NLON**-0.5 * (NLON / points),
            waves_total=waves_total,
        ),
        out_shape=(
            jax.ShapeDtypeStruct(block, jnp.bfloat16),
            jax.ShapeDtypeStruct((8, 128), jnp.float32),
        ),
        in_specs=[vmem, pl.BlockSpec(memory_space=pl.ANY), vmem, smem, smem] + [vmem] * 6,
        out_specs=(vmem, vmem),
        scratch_shapes=[
            pltpu.VMEM(legendre.shape, jnp.bfloat16),
            pltpu.VMEM((rows, latitudes), jnp.bfloat16),
            pltpu.VMEM((rows, latitudes), jnp.bfloat16),
            pltpu.VMEM((4 * points, latitudes), jnp.bfloat16),
            pltpu.VMEM((rows, latitudes), jnp.bfloat16),
            pltpu.VMEM((rows, latitudes), jnp.bfloat16),
            pltpu.VMEM((WAVES, 8, 128), jnp.float32),
            pltpu.VMEM((CHUNKS, 2, CHUNK_ROWS, degrees), jnp.bfloat16),
            pltpu.VMEM((CHUNKS, CHUNK_ROWS, degrees), jnp.bfloat16),
        ]
        + [pltpu.VMEM((4, CHUNK_ROWS, degrees), jnp.bfloat16)] * CHUNKS
        + [
            dma((waves_local,)),
            dma((WAVES - 1, CHUNKS)),
            dma((WAVES - 1, CHUNKS)),
            dma((WAVES - 1, CHUNKS)),
            dma((WAVES - 1, CHUNKS)),
            dma((WAVES - 1,)),
            dma((WAVES - 1,)),
            dma((3, CHUNKS)),
            dma((3, CHUNKS)),
            dma((2, CHUNKS)),
            dma((CHUNKS,)),
        ],
        compiler_params=pltpu.CompilerParams(
            collective_id=0, has_side_effects=True, vmem_limit_bytes=48 * 1024 * 1024
        ),
    )(
        state.reshape(block),
        legendre,
        lat_weights.reshape(1, latitudes),
        region,
        sources,
        jnp.asarray(np.stack([synth_high, synth_low])),
        jnp.asarray(np.stack([synth_high.T, synth_low.T])),
        jnp.asarray(forward),
        jnp.asarray(backward),
        jnp.asarray(pick.astype(jnp.bfloat16)),
        jnp.asarray(fourier),
    )
    return (cloned.astype(jnp.float32).reshape(state.shape), scores[0, :1])


def solution(mesh):
    in_specs = (P("member", "wave", None, None), P("wave", None, None), P(), P(), P())
    out_specs = (P("member", "wave", None, None), P("member"))

    def run(state, legendre, lat_weights, region, sources):
        shape = (state.shape[1] // mesh.shape["wave"], state.shape[2], state.shape[3], legendre.shape[2])
        fits = mesh.shape["wave"] == 4 and mesh.shape["member"] == 8 and shape == (8, 32, 640, 640)
        return jax.shard_map(
            in_one_kernel if fits else on_device,
            mesh=mesh,
            in_specs=in_specs,
            out_specs=out_specs,
            check_vma=False,
        )(state, legendre, lat_weights, region, sources)

    return run
```

```python
import functools

import jax
import jax.numpy as jnp
import numpy as np
from jax import lax
from jax.experimental import pallas as pl
from jax.experimental.pallas import tpu as pltpu
from jax.sharding import PartitionSpec as P

NLON = 2560


advect_rate = 2.0


def wave_table(waves_total, points):
    wave_index = np.arange(waves_total)[:, None]
    angles = (wave_index * np.arange(points)[None, :] % points) * (2.0 * np.pi / points)
    return np.stack([np.cos(angles), -np.sin(angles)], axis=1)


def split_table(table):
    high = table.astype(jnp.bfloat16)
    low = (table - high.astype(np.float64)).astype(jnp.bfloat16)
    return high, low


def quadrature_points(waves_total):
    return (3 * (waves_total - 1)) // 128 * 128 + 128


def on_device(state, legendre, lat_weights, region, sources):
    wave_count = lax.axis_size("wave")
    waves_local = legendre.shape[0]
    waves_total = waves_local * wave_count
    degrees = legendre.shape[1]
    latitudes = legendre.shape[2]
    lat_rows = latitudes // wave_count
    state_rows = state.shape[2]
    level_count = state_rows // 4
    points = quadrature_points(waves_total)
    table_high, table_low = split_table(wave_table(waves_total, points))
    spectral = state[0]
    fourier_coef = jnp.einsum(
        "mrn,mnl->mrl", spectral.astype(jnp.bfloat16), legendre, preferred_element_type=jnp.float32
    )
    fourier_coef = fourier_coef.astype(jnp.bfloat16).reshape(
        waves_local, 2, 2 * level_count, latitudes
    )
    synthesis_scale = (2.0 * waves_total) ** (-0.5)
    coef = lax.all_to_all(fourier_coef, "wave", split_axis=3, concat_axis=0, tiled=True)
    gridded = synthesis_scale * jnp.einsum(
        "mckl,mcx->klx",
        jnp.concatenate([coef, coef], axis=1),
        jnp.concatenate([table_high, table_low], axis=1),
        preferred_element_type=jnp.float32,
    )
    lat_start = lax.axis_index("wave") * lat_rows
    local_weights = lax.dynamic_slice_in_dim(lat_weights, lat_start, lat_rows)
    wind_grid = gridded[:level_count]
    temper_grid = gridded[level_count:]
    fluxes = (
        jnp.concatenate([0.5 * wind_grid * wind_grid, wind_grid * temper_grid], axis=0)
        * local_weights[None, :, None]
    )
    fluxes = fluxes.astype(jnp.bfloat16)
    fourier = wave_table(waves_total, NLON).reshape(2 * waves_total, NLON).astype(jnp.bfloat16)
    lon_index = lax.broadcasted_iota(jnp.int32, (1, NLON), 1)
    lon_inside = (lon_index >= region[2]) & (lon_index < region[3])
    gram = jnp.einsum(
        "px,qx->pq",
        jnp.where(lon_inside, fourier, jnp.zeros((), jnp.bfloat16)),
        fourier,
        preferred_element_type=jnp.float32,
    )
    lowest = coef[:, :, -1].reshape(2 * waves_total, lat_rows).astype(jnp.float32)
    gram_lowest = jnp.dot(gram, lowest, precision=lax.Precision.HIGHEST)
    lat_index = lat_start + lax.broadcasted_iota(jnp.int32, (lat_rows,), 0)
    in_band = (lat_index >= region[0]) & (lat_index < region[1])
    region_part = jnp.sum(
        jnp.where(in_band, local_weights, 0.0)[None, :] * lowest * gram_lowest
    ) / (2.0 * waves_total)
    region_total = lax.psum(region_part, "wave")
    every_lat = lax.broadcasted_iota(jnp.int32, (latitudes,), 0)
    lat_inside = (every_lat >= region[0]) & (every_lat < region[1])
    region_weight = jnp.sum(jnp.where(lat_inside, lat_weights, 0.0)) * (
        region[3] - region[2]
    ).astype(jnp.float32)
    scores = (region_total / region_weight).reshape(1)
    analysis_scale = NLON ** (-0.5) * (NLON / points)
    flux_high = jnp.einsum("klx,mcx->mckl", fluxes, table_high, preferred_element_type=jnp.float32)
    flux_low = jnp.einsum("klx,mcx->mckl", fluxes, table_low, preferred_element_type=jnp.float32)
    flux_coef = (analysis_scale * (flux_high + flux_low)).astype(jnp.bfloat16)
    tendency = jnp.einsum(
        "mckl,mnl->mckn",
        lax.all_to_all(flux_coef, "wave", split_axis=0, concat_axis=3, tiled=True),
        legendre,
        preferred_element_type=jnp.float32,
    )
    wave_ids = lax.axis_index("wave") * waves_local + lax.broadcasted_iota(
        jnp.int32, (waves_local, 1, 1), 0
    )
    advection = advect_rate * wave_ids.astype(jnp.float32) / waves_total
    degree_ids = lax.broadcasted_iota(jnp.int32, (1, 1, degrees), 2).astype(jnp.float32)
    damping = 1.0 + ((degree_ids + 1.0) / degrees) ** 2
    spectral_split = spectral.reshape(waves_local, 2, 2 * level_count, degrees)
    real_part = (spectral_split[:, 0] + advection * tendency[:, 1]) / damping
    imag_part = (spectral_split[:, 1] - advection * tendency[:, 0]) / damping
    stepped = jnp.stack([real_part, imag_part], axis=1).reshape(1, waves_local, state_rows, degrees)
    source_member = sources[lax.axis_index("member")]
    shards = lax.all_gather(stepped.astype(jnp.bfloat16), "member", axis=0, tiled=True)
    cloned = lax.dynamic_slice_in_dim(shards, source_member, 1, axis=0).astype(jnp.float32)
    return (cloned, scores)


MESH = pl.DeviceIdType.MESH
WAVES = 4
CHUNKS = 4
PAIR = 2
ROWS = 32
CHUNK_ROWS = PAIR * ROWS
PART_ROWS = CHUNK_ROWS // WAVES
OWNED_ROWS = CHUNKS * PART_ROWS


def order_tables(levels):
    held = levels // WAVES
    forward = np.zeros((CHUNK_ROWS, CHUNK_ROWS))
    backward = np.zeros((CHUNK_ROWS, CHUNK_ROWS))
    for m in range(PAIR):
        for c in range(2):
            for f in range(2):
                for k in range(levels):
                    plain = ((m * 2 + c) * 2 + f) * levels + k
                    owner = ((((k // held) * PAIR + m) * 2 + c) * 2 + f) * held + k % held
                    crossed = ((((k // held) * PAIR + m) * 2 + (1 - c)) * 2 + f) * held + k % held
                    forward[owner, plain] = 1.0
                    backward[plain, crossed] = 1.0 - 2.0 * c
    return forward.astype(jnp.bfloat16), backward.astype(jnp.bfloat16)


def grid_tables(table):
    waves, _, points = table.shape
    wide = np.einsum("mcx,fg,kl->lgxmcfk", table, np.eye(2), np.eye(2))
    return split_table(wide.reshape(4 * points, 8 * waves))


def step_kernel(
    state_hbm, legendre_ref, weights_ref, region_ref, sources_ref, synth_hbm, analysis_hbm,
    forward_hbm, backward_hbm, pick_hbm, fourier_hbm,
    out_ref, score_ref,
    state_ref, synth_ref, analysis_ref, forward_ref, backward_ref, pick_ref, fourier_ref,
    leg, sent, held, flux, back_sent, back, score_buf, cross, crossed,
    pool0, pool1, pool2, pool3,
    state_sem, table_sem, leg_sem, go_send, go_recv, ret_send, ret_recv, score_send, score_recv,
    pass_send, pass_recv, cross_send, cross_recv,
    *, scale, analysis_scale, waves_total,
):
    pools = [pool0, pool1, pool2, pool3]
    me = lax.axis_index("wave")
    slot = lax.axis_index("member")
    z = slot // 2
    x = slot % 2
    half = z // 2
    inner = z % 2 != half % 2
    z_mate = (z + 1 - 2 * (z % 2)) * 2 + x
    x_mate = z * 2 + 1 - x
    far_inner = (2 - half) * 2 + x
    far_outer = (3 - 3 * half) * 2 + x
    here = slot - half * 4
    z_here = z_mate - half * 4
    points = synth_ref.shape[1] // 4
    degrees = state_ref.shape[1]
    lat_count = weights_ref.shape[0]

    loads = [
        pltpu.make_async_copy(legendre_ref.at[m], leg.at[m], leg_sem.at[m])
        for m in range(CHUNKS * PAIR)
    ]
    state_loads = [
        pltpu.make_async_copy(
            state_hbm.at[pl.ds(c * CHUNK_ROWS, CHUNK_ROWS)],
            state_ref.at[pl.ds(c * CHUNK_ROWS, CHUNK_ROWS)],
            state_sem.at[c],
        )
        for c in range(CHUNKS)
    ]
    table_pairs = [
        (forward_hbm, forward_ref),
        (fourier_hbm, fourier_ref),
        (synth_hbm, synth_ref),
        (analysis_hbm, analysis_ref),
        (pick_hbm, pick_ref),
        (backward_hbm, backward_ref),
    ]
    table_loads = [
        pltpu.make_async_copy(pair[0], pair[1], table_sem.at[i])
        for i, pair in enumerate(table_pairs)
    ]
    table_loads[0].start()
    for c in range(CHUNKS):
        state_loads[c].start()
        for load in loads[c * PAIR : (c + 1) * PAIR]:
            load.start()
    for load in table_loads[1:]:
        load.start()

    barrier = pltpu.get_barrier_semaphore()
    for d in range(1, WAVES):
        pl.semaphore_signal(
            barrier, inc=1, device_id={"wave": (me + d) % WAVES}, device_id_type=MESH
        )
    for mate in (z_mate, x_mate, far_inner):
        pl.semaphore_signal(barrier, inc=1, device_id={"member": mate}, device_id_type=MESH)

    @pl.when(inner)
    def _():
        pl.semaphore_signal(barrier, inc=1, device_id={"member": far_outer}, device_id_type=MESH)

    def wave_copy(source, target, target_row, c, d, send_sem, recv_sem):
        to = (me + d) % WAVES
        return pltpu.make_async_remote_copy(
            src_ref=source.at[pl.ds(pl.multiple_of(to * OWNED_ROWS + c * PART_ROWS, PART_ROWS), PART_ROWS)],
            dst_ref=target.at[pl.ds(pl.multiple_of(target_row, PART_ROWS), PART_ROWS)],
            send_sem=send_sem.at[d - 1, c],
            recv_sem=recv_sem.at[d - 1, c],
            device_id={"wave": to},
            device_id_type=MESH,
        )

    my_rows = me * OWNED_ROWS
    go = []
    for c in range(CHUNKS):
        parts = []
        state_loads[c].wait()
        if c == 0:
            table_loads[0].wait()
        for m in range(c * PAIR, (c + 1) * PAIR):
            loads[m].wait()
            parts.append(
                jnp.dot(
                    state_ref[m * ROWS : (m + 1) * ROWS].astype(jnp.bfloat16),
                    leg[m],
                    preferred_element_type=jnp.float32,
                )
            )
        coef = jnp.concatenate(parts, axis=0).astype(jnp.bfloat16)
        ordered = jnp.dot(
            forward_ref[...], coef, preferred_element_type=jnp.float32
        ).astype(jnp.bfloat16)
        for w in range(WAVES):
            sent[w * OWNED_ROWS + c * PART_ROWS : w * OWNED_ROWS + (c + 1) * PART_ROWS] = ordered[
                w * PART_ROWS : (w + 1) * PART_ROWS
            ]
        if c == 0:

            @pl.when(inner)
            def _():
                pl.semaphore_wait(barrier, 7)

            @pl.when(jnp.logical_not(inner))
            def _():
                pl.semaphore_wait(barrier, 6)

        for d in (2, 1, 3):
            copy = wave_copy(sent, held, my_rows + c * PART_ROWS, c, d, go_send, go_recv)
            copy.start()
            go.append(copy)
    mine = pl.ds(pl.multiple_of(my_rows, OWNED_ROWS), OWNED_ROWS)
    held[mine] = sent[mine]

    for load in table_loads[1:]:
        load.wait()
    low, high = region_ref[2], region_ref[3]
    lon = lax.broadcasted_iota(jnp.int32, (1, fourier_ref.shape[1]), 1)
    lon_inside = jnp.where((lon >= low) & (lon < high), 1.0, 0.0)
    fourier = fourier_ref[...]
    gram = lax.dot_general(
        (fourier.astype(jnp.float32) * lon_inside).astype(jnp.bfloat16),
        fourier,
        (((1,), (1,)), ((), ())),
        preferred_element_type=jnp.float32,
    )
    gram_high = gram.astype(jnp.bfloat16)
    gram_low = (gram - gram_high.astype(jnp.float32)).astype(jnp.bfloat16)
    lat = lax.broadcasted_iota(jnp.int32, (1, lat_count), 1)
    weights = weights_ref[...].reshape(1, lat_count)
    region_weights = jnp.where((lat >= region_ref[0]) & (lat < region_ref[1]), weights, 0.0)
    weight_sum = jnp.sum(region_weights, axis=1, keepdims=True) * (high - low).astype(jnp.float32)

    for copy in go:
        copy.wait_recv()

    coefs = held[...]
    scaled = weights * (scale * scale)
    for k in range(2):
        rows = slice(k * 2 * points, (k + 1) * 2 * points)
        grid = jnp.dot(
            synth_ref[0, rows], coefs, preferred_element_type=jnp.float32
        ) + jnp.dot(synth_ref[1, rows], coefs, preferred_element_type=jnp.float32)
        wind = grid[:points]
        weighted = wind * scaled
        flux[k * 2 * points : (k * 2 + 1) * points] = (0.5 * weighted * wind).astype(jnp.bfloat16)
        flux[(k * 2 + 1) * points : (k * 2 + 2) * points] = (weighted * grid[points:]).astype(
            jnp.bfloat16
        )
    fluxes = flux[...]
    back_sent[...] = (
        analysis_scale
        * (
            jnp.dot(analysis_ref[0], fluxes, preferred_element_type=jnp.float32)
            + jnp.dot(analysis_ref[1], fluxes, preferred_element_type=jnp.float32)
        )
    ).astype(jnp.bfloat16)
    ret = []
    for c in range(CHUNKS):
        for d in (2, 1, 3):
            copy = wave_copy(back_sent, back, my_rows + c * PART_ROWS, c, d, ret_send, ret_recv)
            copy.start()
            ret.append(copy)
    back[mine] = back_sent[mine]

    lowest = jnp.dot(pick_ref[...], coefs, preferred_element_type=jnp.float32)
    lowest_half = lowest.astype(jnp.bfloat16)
    spread = jnp.dot(gram_high, lowest_half, preferred_element_type=jnp.float32) + jnp.dot(
        gram_low, lowest_half, preferred_element_type=jnp.float32
    )
    squares = jnp.sum(lowest * spread, axis=0, keepdims=True) * (region_weights * (scale * scale))
    score = jnp.sum(squares, axis=1, keepdims=True) / weight_sum
    score = score * jnp.where(me == WAVES - 1, 1.0, 0.0)
    score_buf[me] = jnp.broadcast_to(score, score_buf.shape[1:])
    score_copies = []
    for d in range(1, WAVES):
        copy = pltpu.make_async_remote_copy(
            src_ref=score_buf.at[me],
            dst_ref=score_buf.at[me],
            send_sem=score_send.at[d - 1],
            recv_sem=score_recv.at[d - 1],
            device_id={"wave": (me + d) % WAVES},
            device_id_type=MESH,
        )
        copy.start()
        score_copies.append(copy)

    def member_copy(source, target, to, send_sem, recv_sem):
        return pltpu.make_async_remote_copy(
            src_ref=source, dst_ref=target, send_sem=send_sem, recv_sem=recv_sem,
            device_id={"member": to}, device_id_type=MESH,
        )

    def pass_copy(c, kind):
        which = z_here if kind == 2 else here
        block = pools[c].at[which]
        return member_copy(
            block, block, z_mate if kind == 0 else x_mate, pass_send.at[kind, c], pass_recv.at[kind, c]
        )

    def cross_copy(c, far):
        return member_copy(
            cross.at[c, far],
            crossed.at[c],
            far_outer if far else far_inner,
            cross_send.at[far, c],
            cross_recv.at[c],
        )

    def half_index(member_slot):
        return jnp.clip(sources_ref[member_slot] - half * 4, 0, 3)

    inner_pick = half_index(far_inner)
    outer_pick = half_index(far_outer)

    def forward_pass(c):
        pass_copy(c, 0).wait_recv()
        pass_copy(c, 2).start()

    def send_across(c):
        pass_copy(c, 1).wait_recv()
        pass_copy(c, 2).wait_recv()

        @pl.when(inner)
        def _():
            cross[c, 1] = pools[c][outer_pick]
            cross_copy(c, 1).start()
            cross[c, 0] = pools[c][inner_pick]
            cross_copy(c, 0).start()

    degree = lax.broadcasted_iota(jnp.int32, (1, degrees), 1).astype(jnp.float32)
    keep = 1.0 / (1.0 + ((degree + 1.0) / degrees) ** 2)
    for c in range(CHUNKS):
        for copy in ret[c * (WAVES - 1) : (c + 1) * (WAVES - 1)]:
            copy.wait_recv()
        arrived = jnp.concatenate(
            [
                back[w * OWNED_ROWS + c * PART_ROWS : w * OWNED_ROWS + (c + 1) * PART_ROWS]
                for w in range(WAVES)
            ],
            axis=0,
        )
        plain = jnp.dot(
            backward_ref[...], arrived, preferred_element_type=jnp.float32
        ).astype(jnp.bfloat16)
        for i in range(PAIR):
            m = c * PAIR + i
            tendency = lax.dot_general(
                plain[i * ROWS : (i + 1) * ROWS],
                leg[m],
                (((1,), (1,)), ((), ())),
                preferred_element_type=jnp.float32,
            )
            wave_id = (me * (CHUNKS * PAIR) + m).astype(jnp.float32)
            advection = wave_id * (advect_rate / waves_total)
            stepped = (state_ref[m * ROWS : (m + 1) * ROWS] + advection * tendency) * keep
            pools[c][here, i * ROWS : (i + 1) * ROWS] = stepped.astype(jnp.bfloat16)
        pass_copy(c, 0).start()
        pass_copy(c, 1).start()
        if c >= 1:
            forward_pass(c - 1)
        if c >= 3:
            send_across(c - 3)
    forward_pass(CHUNKS - 1)
    for c in range(CHUNKS - 3, CHUNKS):
        send_across(c)

    for copy in score_copies:
        copy.wait()
    score_ref[...] = score_buf[0] + score_buf[1] + score_buf[2] + score_buf[3]
    for copy in go + ret:
        copy.wait_send()

    origin = sources_ref[slot] - half * 4
    near = (origin >= 0) & (origin < 4)
    choice = jnp.clip(origin, 0, 3)
    for c in range(CHUNKS):
        cross_copy(c, 0).wait_recv()
        out_ref[c * CHUNK_ROWS : (c + 1) * CHUNK_ROWS] = jnp.where(
            near, pools[c][choice], crossed[c]
        )
    for c in range(CHUNKS):
        for kind in range(3):
            pass_copy(c, kind).wait_send()

    @pl.when(inner)
    def _():
        for c in range(CHUNKS):
            for far in range(2):
                cross_copy(c, far).wait_send()


def in_one_kernel(state, legendre, lat_weights, region, sources):
    waves_local, degrees, latitudes = legendre.shape
    waves_total = waves_local * WAVES
    points = quadrature_points(waves_total)
    levels = state.shape[2] // 4
    synth_high, synth_low = grid_tables(wave_table(waves_total, points))
    forward, backward = order_tables(levels)
    pick = np.zeros((2 * waves_total, 8 * waves_total))
    pick[np.arange(2 * waves_total), np.arange(2 * waves_total) * 4 + 3] = 1.0
    fourier = wave_table(waves_total, NLON).reshape(2 * waves_total, NLON).astype(jnp.bfloat16)
    tables = [
        jnp.asarray(np.stack([synth_high, synth_low])),
        jnp.asarray(np.stack([synth_high.T, synth_low.T])),
        jnp.asarray(forward),
        jnp.asarray(backward),
        jnp.asarray(pick.astype(jnp.bfloat16)),
        jnp.asarray(fourier),
    ]
    vmem = pl.BlockSpec(memory_space=pltpu.VMEM)
    smem = pl.BlockSpec(memory_space=pltpu.SMEM)
    hbm = pl.BlockSpec(memory_space=pl.ANY)
    rows = waves_local * ROWS
    block = (rows, degrees)
    dma = pltpu.SemaphoreType.DMA
    cloned, scores = pl.pallas_call(
        functools.partial(
            step_kernel,
            scale=(2.0 * waves_total) ** -0.5,
            analysis_scale=NLON**-0.5 * (NLON / points),
            waves_total=waves_total,
        ),
        out_shape=(
            jax.ShapeDtypeStruct(block, jnp.bfloat16),
            jax.ShapeDtypeStruct((8, 128), jnp.float32),
        ),
        in_specs=[hbm, hbm, vmem, smem, smem] + [hbm] * 6,
        out_specs=(vmem, vmem),
        scratch_shapes=[pltpu.VMEM(block, jnp.float32)]
        + [pltpu.VMEM(table.shape, table.dtype) for table in tables]
        + [
            pltpu.VMEM(legendre.shape, jnp.bfloat16),
            pltpu.VMEM((rows, latitudes), jnp.bfloat16),
            pltpu.VMEM((rows, latitudes), jnp.bfloat16),
            pltpu.VMEM((4 * points, latitudes), jnp.bfloat16),
            pltpu.VMEM((rows, latitudes), jnp.bfloat16),
            pltpu.VMEM((rows, latitudes), jnp.bfloat16),
            pltpu.VMEM((WAVES, 8, 128), jnp.float32),
            pltpu.VMEM((CHUNKS, 2, CHUNK_ROWS, degrees), jnp.bfloat16),
            pltpu.VMEM((CHUNKS, CHUNK_ROWS, degrees), jnp.bfloat16),
        ]
        + [pltpu.VMEM((4, CHUNK_ROWS, degrees), jnp.bfloat16)] * CHUNKS
        + [
            dma((CHUNKS,)),
            dma((len(tables),)),
            dma((waves_local,)),
            dma((WAVES - 1, CHUNKS)),
            dma((WAVES - 1, CHUNKS)),
            dma((WAVES - 1, CHUNKS)),
            dma((WAVES - 1, CHUNKS)),
            dma((WAVES - 1,)),
            dma((WAVES - 1,)),
            dma((3, CHUNKS)),
            dma((3, CHUNKS)),
            dma((2, CHUNKS)),
            dma((CHUNKS,)),
        ],
        compiler_params=pltpu.CompilerParams(
            collective_id=0, has_side_effects=True, vmem_limit_bytes=56 * 1024 * 1024
        ),
    )(
        state.reshape(block),
        legendre,
        lat_weights,
        region,
        sources,
        *tables,
    )
    return (cloned.astype(jnp.float32).reshape(state.shape), scores[0, :1])


def solution(mesh):
    in_specs = (P("member", "wave", None, None), P("wave", None, None), P(), P(), P())
    out_specs = (P("member", "wave", None, None), P("member"))

    def run(state, legendre, lat_weights, region, sources):
        shape = (state.shape[1] // mesh.shape["wave"], state.shape[2], state.shape[3], legendre.shape[2])
        fits = mesh.shape["wave"] == 4 and mesh.shape["member"] == 8 and shape == (8, 32, 640, 640)
        return jax.shard_map(
            in_one_kernel if fits else on_device,
            mesh=mesh,
            in_specs=in_specs,
            out_specs=out_specs,
            check_vma=False,
        )(state, legendre, lat_weights, region, sources)

    return run
```

```python
import functools

import jax
import jax.numpy as jnp
import numpy as np
from jax import lax
from jax.experimental import pallas as pl
from jax.experimental.pallas import tpu as pltpu
from jax.sharding import PartitionSpec as P

NLON = 2560


advect_rate = 2.0


def wave_table(waves_total, points):
    wave_index = np.arange(waves_total)[:, None]
    angles = (wave_index * np.arange(points)[None, :] % points) * (2.0 * np.pi / points)
    return np.stack([np.cos(angles), -np.sin(angles)], axis=1)


def split_table(table):
    high = table.astype(jnp.bfloat16)
    low = (table - high.astype(np.float64)).astype(jnp.bfloat16)
    return high, low


def quadrature_points(waves_total):
    return (3 * (waves_total - 1)) // 128 * 128 + 128


def on_device(state, legendre, lat_weights, region, sources):
    wave_count = lax.axis_size("wave")
    waves_local = legendre.shape[0]
    waves_total = waves_local * wave_count
    degrees = legendre.shape[1]
    latitudes = legendre.shape[2]
    lat_rows = latitudes // wave_count
    state_rows = state.shape[2]
    level_count = state_rows // 4
    points = quadrature_points(waves_total)
    table_high, table_low = split_table(wave_table(waves_total, points))
    spectral = state[0]
    fourier_coef = jnp.einsum(
        "mrn,mnl->mrl", spectral.astype(jnp.bfloat16), legendre, preferred_element_type=jnp.float32
    )
    fourier_coef = fourier_coef.astype(jnp.bfloat16).reshape(
        waves_local, 2, 2 * level_count, latitudes
    )
    synthesis_scale = (2.0 * waves_total) ** (-0.5)
    coef = lax.all_to_all(fourier_coef, "wave", split_axis=3, concat_axis=0, tiled=True)
    gridded = synthesis_scale * jnp.einsum(
        "mckl,mcx->klx",
        jnp.concatenate([coef, coef], axis=1),
        jnp.concatenate([table_high, table_low], axis=1),
        preferred_element_type=jnp.float32,
    )
    lat_start = lax.axis_index("wave") * lat_rows
    local_weights = lax.dynamic_slice_in_dim(lat_weights, lat_start, lat_rows)
    wind_grid = gridded[:level_count]
    temper_grid = gridded[level_count:]
    fluxes = (
        jnp.concatenate([0.5 * wind_grid * wind_grid, wind_grid * temper_grid], axis=0)
        * local_weights[None, :, None]
    )
    fluxes = fluxes.astype(jnp.bfloat16)
    fourier = wave_table(waves_total, NLON).reshape(2 * waves_total, NLON).astype(jnp.bfloat16)
    lon_index = lax.broadcasted_iota(jnp.int32, (1, NLON), 1)
    lon_inside = (lon_index >= region[2]) & (lon_index < region[3])
    gram = jnp.einsum(
        "px,qx->pq",
        jnp.where(lon_inside, fourier, jnp.zeros((), jnp.bfloat16)),
        fourier,
        preferred_element_type=jnp.float32,
    )
    lowest = coef[:, :, -1].reshape(2 * waves_total, lat_rows).astype(jnp.float32)
    gram_lowest = jnp.dot(gram, lowest, precision=lax.Precision.HIGHEST)
    lat_index = lat_start + lax.broadcasted_iota(jnp.int32, (lat_rows,), 0)
    in_band = (lat_index >= region[0]) & (lat_index < region[1])
    region_part = jnp.sum(
        jnp.where(in_band, local_weights, 0.0)[None, :] * lowest * gram_lowest
    ) / (2.0 * waves_total)
    region_total = lax.psum(region_part, "wave")
    every_lat = lax.broadcasted_iota(jnp.int32, (latitudes,), 0)
    lat_inside = (every_lat >= region[0]) & (every_lat < region[1])
    region_weight = jnp.sum(jnp.where(lat_inside, lat_weights, 0.0)) * (
        region[3] - region[2]
    ).astype(jnp.float32)
    scores = (region_total / region_weight).reshape(1)
    analysis_scale = NLON ** (-0.5) * (NLON / points)
    flux_high = jnp.einsum("klx,mcx->mckl", fluxes, table_high, preferred_element_type=jnp.float32)
    flux_low = jnp.einsum("klx,mcx->mckl", fluxes, table_low, preferred_element_type=jnp.float32)
    flux_coef = (analysis_scale * (flux_high + flux_low)).astype(jnp.bfloat16)
    tendency = jnp.einsum(
        "mckl,mnl->mckn",
        lax.all_to_all(flux_coef, "wave", split_axis=0, concat_axis=3, tiled=True),
        legendre,
        preferred_element_type=jnp.float32,
    )
    wave_ids = lax.axis_index("wave") * waves_local + lax.broadcasted_iota(
        jnp.int32, (waves_local, 1, 1), 0
    )
    advection = advect_rate * wave_ids.astype(jnp.float32) / waves_total
    degree_ids = lax.broadcasted_iota(jnp.int32, (1, 1, degrees), 2).astype(jnp.float32)
    damping = 1.0 + ((degree_ids + 1.0) / degrees) ** 2
    spectral_split = spectral.reshape(waves_local, 2, 2 * level_count, degrees)
    real_part = (spectral_split[:, 0] + advection * tendency[:, 1]) / damping
    imag_part = (spectral_split[:, 1] - advection * tendency[:, 0]) / damping
    stepped = jnp.stack([real_part, imag_part], axis=1).reshape(1, waves_local, state_rows, degrees)
    source_member = sources[lax.axis_index("member")]
    shards = lax.all_gather(stepped.astype(jnp.bfloat16), "member", axis=0, tiled=True)
    cloned = lax.dynamic_slice_in_dim(shards, source_member, 1, axis=0).astype(jnp.float32)
    return (cloned, scores)


MESH = pl.DeviceIdType.MESH
WAVES = 4
CHUNKS = 4
STEPS = 8
PAIR = 2
ROWS = 32
CHUNK_ROWS = PAIR * ROWS
PART_ROWS = CHUNK_ROWS // WAVES
OWNED_ROWS = CHUNKS * PART_ROWS


def order_tables(levels):
    held = levels // WAVES
    forward = np.zeros((CHUNK_ROWS, CHUNK_ROWS))
    backward = np.zeros((CHUNK_ROWS, CHUNK_ROWS))
    for m in range(PAIR):
        for c in range(2):
            for f in range(2):
                for k in range(levels):
                    plain = ((m * 2 + c) * 2 + f) * levels + k
                    owner = ((((k // held) * PAIR + m) * 2 + c) * 2 + f) * held + k % held
                    crossed = ((((k // held) * PAIR + m) * 2 + (1 - c)) * 2 + f) * held + k % held
                    forward[owner, plain] = 1.0
                    backward[plain, crossed] = 1.0 - 2.0 * c
    return forward.astype(jnp.bfloat16), backward.astype(jnp.bfloat16)


def step_kernel(
    state_hbm, legendre_ref, weights_ref, region_ref, sources_ref, table_hbm,
    out_ref, score_ref,
    state_ref, table_ref, synth_ref, analysis_ref, low_ref, low_sent, low_held,
    chosen, leg, sent, held, flux, back_sent, back, cross, crossed,
    *rest, scale, analysis_scale, waves_total, points,
):
    pools = rest[:STEPS]
    (
        state_sem, table_sem, leg_sem, go_send, go_recv, ret_send, ret_recv, score_send, score_recv,
        pass_send, pass_recv, cross_send, cross_recv,
    ) = rest[STEPS:]
    me = lax.axis_index("wave")
    slot = lax.axis_index("member")
    z = slot // 2
    x = slot % 2
    half = z // 2
    inner = z % 2 != half % 2
    z_mate = (z + 1 - 2 * (z % 2)) * 2 + x
    x_mate = z * 2 + 1 - x
    far_inner = (2 - half) * 2 + x
    far_outer = (3 - 3 * half) * 2 + x
    here = slot - half * 4
    z_here = z_mate - half * 4
    degrees = state_ref.shape[1]
    lat_count = weights_ref.shape[0]
    f32 = jnp.float32
    bf16 = jnp.bfloat16
    low_level = ROWS // 4 - 1

    loads = [
        pltpu.make_async_copy(legendre_ref.at[m], leg.at[m], leg_sem.at[m]) for m in range(STEPS)
    ]
    state_loads = [
        pltpu.make_async_copy(
            state_hbm.at[pl.ds(c * CHUNK_ROWS, CHUNK_ROWS)],
            state_ref.at[pl.ds(c * CHUNK_ROWS, CHUNK_ROWS)],
            state_sem.at[c],
        )
        for c in range(CHUNKS)
    ]
    table_load = pltpu.make_async_copy(table_hbm, table_ref, table_sem)
    for load in state_loads + [table_load] + loads:
        load.start()

    barrier = pltpu.get_barrier_semaphore()
    for d in range(1, WAVES):
        pl.semaphore_signal(
            barrier, inc=1, device_id={"wave": (me + d) % WAVES}, device_id_type=MESH
        )
    for mate in (z_mate, x_mate, far_inner):
        pl.semaphore_signal(barrier, inc=1, device_id={"member": mate}, device_id_type=MESH)

    @pl.when(inner)
    def _():
        pl.semaphore_signal(barrier, inc=1, device_id={"member": far_outer}, device_id_type=MESH)

    for c in range(CHUNKS):
        state_loads[c].wait()
        for m in range(c * PAIR, (c + 1) * PAIR):
            pools[m][here] = state_ref[m * ROWS : (m + 1) * ROWS].astype(bf16)

    @pl.when(inner)
    def _():
        pl.semaphore_wait(barrier, 7)

    @pl.when(jnp.logical_not(inner))
    def _():
        pl.semaphore_wait(barrier, 6)

    def member_copy(source, target, to, send_sem, recv_sem):
        return pltpu.make_async_remote_copy(
            src_ref=source, dst_ref=target, send_sem=send_sem, recv_sem=recv_sem,
            device_id={"member": to}, device_id_type=MESH,
        )

    def pass_copy(c, kind):
        block = pools[c].at[z_here if kind == 2 else here]
        return member_copy(
            block, block, z_mate if kind == 0 else x_mate, pass_send.at[kind, c], pass_recv.at[kind, c]
        )

    def cross_copy(c, far):
        return member_copy(
            cross.at[c, far],
            crossed.at[c],
            far_outer if far else far_inner,
            cross_send.at[far, c],
            cross_recv.at[c],
        )

    def half_index(member_slot):
        return jnp.clip(sources_ref[member_slot] - half * 4, 0, 3)

    inner_pick = half_index(far_inner)
    outer_pick = half_index(far_outer)
    origin = sources_ref[slot] - half * 4
    near = (origin >= 0) & (origin < 4)
    choice = jnp.clip(origin, 0, 3)

    for c in range(STEPS):
        pass_copy(c, 0).start()
        if c < 2:
            pass_copy(c, 1).start()

    def forward_pass(c):
        pass_copy(c, 0).wait_recv()
        pass_copy(c, 2).start()
        if c + 2 < STEPS:
            pass_copy(c + 2, 1).start()

    def send_across(c):
        pass_copy(c, 1).wait_recv()
        pass_copy(c, 2).wait_recv()

        @pl.when(inner)
        def _():
            cross[c, 1] = pools[c][outer_pick]
            cross_copy(c, 1).start()
            cross[c, 0] = pools[c][inner_pick]
            cross_copy(c, 0).start()

    def lowest_coef(m):
        loads[m].wait()
        coef = jnp.dot(
            state_ref[m * ROWS : (m + 1) * ROWS].astype(bf16), leg[m], preferred_element_type=f32
        )
        for c in range(2):
            row = c * (ROWS // 2) + ROWS // 4 + low_level
            low_ref[m * 2 + c : m * 2 + c + 1] = coef[row : row + 1]

    def wave_copy(source, target, target_row, c, d, send_sem, recv_sem):
        to = (me + d) % WAVES
        return pltpu.make_async_remote_copy(
            src_ref=source.at[pl.ds(pl.multiple_of(to * OWNED_ROWS + c * PART_ROWS, PART_ROWS), PART_ROWS)],
            dst_ref=target.at[pl.ds(pl.multiple_of(target_row, PART_ROWS), PART_ROWS)],
            send_sem=send_sem.at[d - 1, c],
            recv_sem=recv_sem.at[d - 1, c],
            device_id={"wave": to},
            device_id_type=MESH,
        )

    def low_copy(d):
        return pltpu.make_async_remote_copy(
            src_ref=low_sent,
            dst_ref=low_held.at[pl.ds(pl.multiple_of(me * 16, 16), 16)],
            send_sem=score_send.at[d - 1],
            recv_sem=score_recv.at[d - 1],
            device_id={"wave": (me + d) % WAVES},
            device_id_type=MESH,
        )

    my_rows = me * OWNED_ROWS
    mine = pl.ds(pl.multiple_of(my_rows, OWNED_ROWS), OWNED_ROWS)
    columns = fourier_columns = table_ref.shape[1] - 4 * 128
    go = []
    coef_parts = []

    def take_source(c):
        cross_copy(c, 0).wait_recv()
        block = jnp.where(near, pools[c][choice], crossed[c])
        chosen[c * ROWS : (c + 1) * ROWS] = block
        coef_parts.append(jnp.dot(block, leg[c], preferred_element_type=f32))
        if c % PAIR != PAIR - 1:
            return
        pair = c // PAIR
        coef = jnp.concatenate(coef_parts[-PAIR:], axis=0).astype(bf16)
        forward = table_ref[:, columns + 256 : columns + 256 + CHUNK_ROWS]
        ordered = jnp.dot(forward, coef, preferred_element_type=f32).astype(bf16)
        for w in range(WAVES):
            first = w * OWNED_ROWS + pair * PART_ROWS
            sent[first : first + PART_ROWS] = ordered[w * PART_ROWS : (w + 1) * PART_ROWS]
        for d in (2, 1, 3):
            copy = wave_copy(sent, held, my_rows + pair * PART_ROWS, pair, d, go_send, go_recv)
            copy.start()
            go.append(copy)

    table_load.wait()
    coef_rows = 4 * 2 * waves_total
    owner_of = lax.broadcasted_iota(jnp.int32, (2 * waves_total, coef_rows), 0)
    column = lax.broadcasted_iota(jnp.int32, (2 * waves_total, coef_rows), 1)
    widen = jnp.where(column // 4 == owner_of, 1.0, 0.0).astype(bf16)
    tall_owner = lax.broadcasted_iota(jnp.int32, (coef_rows, 2 * waves_total), 1)
    tall_row = lax.broadcasted_iota(jnp.int32, (coef_rows, 2 * waves_total), 0)
    lengthen = jnp.where(tall_row // 4 == tall_owner, 1.0, 0.0).astype(bf16)
    synth_column = lax.broadcasted_iota(jnp.int32, (points, coef_rows), 1) % 4
    analysis_row = lax.broadcasted_iota(jnp.int32, (coef_rows, points), 0) % 4
    for part in range(2):
        waves = table_ref[:, columns + part * 128 : columns + part * 128 + points]
        wide = lax.dot_general(
            waves, widen, (((0,), (0,)), ((), ())), preferred_element_type=f32
        )
        tall = jnp.dot(lengthen, waves, preferred_element_type=f32)
        for k in range(2):
            for f in range(2):
                at = slice((k * 2 + f) * points, (k * 2 + f + 1) * points)
                synth_ref[part, at] = jnp.where(synth_column == f * 2 + k, wide, 0.0).astype(bf16)
                analysis_ref[part, :, at] = jnp.where(
                    analysis_row == f * 2 + k, tall, 0.0
                ).astype(bf16)

    low, high = region_ref[2], region_ref[3]
    lon = lax.broadcasted_iota(jnp.int32, (1, fourier_columns), 1)
    lon_inside = jnp.where((lon >= low) & (lon < high), 1.0, 0.0)
    fourier = table_ref[:, :fourier_columns]
    gram = lax.dot_general(
        (fourier.astype(f32) * lon_inside).astype(bf16),
        fourier,
        (((1,), (1,)), ((), ())),
        preferred_element_type=f32,
    )
    gram_high = gram.astype(bf16)
    gram_low = (gram - gram_high.astype(f32)).astype(bf16)
    lat = lax.broadcasted_iota(jnp.int32, (1, lat_count), 1)
    weights = weights_ref[...].reshape(1, lat_count)
    region_weights = jnp.where((lat >= region_ref[0]) & (lat < region_ref[1]), weights, 0.0)
    weight_sum = jnp.sum(region_weights, axis=1, keepdims=True) * (high - low).astype(f32)

    for t in range(STEPS + 4):
        if t < STEPS:
            forward_pass(t)
            lowest_coef(t)
        if t == STEPS - 1:
            low_sent[...] = low_ref[...].astype(bf16)
            low_held[pl.ds(pl.multiple_of(me * 16, 16), 16)] = low_sent[...]
            for d in range(1, WAVES):
                low_copy(d).start()
        if 1 <= t <= STEPS:
            send_across(t - 1)
        if t >= 4:
            take_source(t - 4)
    held[mine] = sent[mine]

    for copy in go:
        copy.wait_recv()

    coefs = held[...]
    scaled = weights * (scale * scale)
    for k in range(2):
        rows = slice(k * 2 * points, (k + 1) * 2 * points)
        grid = jnp.dot(synth_ref[0, rows], coefs, preferred_element_type=f32) + jnp.dot(
            synth_ref[1, rows], coefs, preferred_element_type=f32
        )
        wind = grid[:points]
        weighted = wind * scaled
        flux[k * 2 * points : (k * 2 + 1) * points] = (0.5 * weighted * wind).astype(bf16)
        flux[(k * 2 + 1) * points : (k * 2 + 2) * points] = (weighted * grid[points:]).astype(bf16)
    fluxes = flux[...]
    back_sent[...] = (
        analysis_scale
        * (
            jnp.dot(analysis_ref[0], fluxes, preferred_element_type=f32)
            + jnp.dot(analysis_ref[1], fluxes, preferred_element_type=f32)
        )
    ).astype(bf16)
    ret = []
    for c in range(CHUNKS):
        for d in (2, 1, 3):
            copy = wave_copy(back_sent, back, my_rows + c * PART_ROWS, c, d, ret_send, ret_recv)
            copy.start()
            ret.append(copy)
    back[mine] = back_sent[mine]

    for d in range(1, WAVES):
        low_copy(d).wait()
    lowest = low_held[...]
    spread = jnp.dot(gram_high, lowest, preferred_element_type=f32) + jnp.dot(
        gram_low, lowest, preferred_element_type=f32
    )
    squares = jnp.sum(lowest.astype(f32) * spread, axis=0, keepdims=True) * (
        region_weights * (scale * scale)
    )
    score = jnp.sum(squares, axis=1, keepdims=True) / weight_sum
    score_ref[...] = jnp.broadcast_to(score, score_ref.shape)

    degree = lax.broadcasted_iota(jnp.int32, (1, degrees), 1).astype(f32)
    keep = 1.0 / (1.0 + ((degree + 1.0) / degrees) ** 2)
    backward = table_ref[:, columns + 384 : columns + 384 + CHUNK_ROWS]
    for c in range(CHUNKS):
        for copy in ret[c * (WAVES - 1) : (c + 1) * (WAVES - 1)]:
            copy.wait_recv()
        arrived = jnp.concatenate(
            [
                back[w * OWNED_ROWS + c * PART_ROWS : w * OWNED_ROWS + (c + 1) * PART_ROWS]
                for w in range(WAVES)
            ],
            axis=0,
        )
        plain = jnp.dot(backward, arrived, preferred_element_type=f32).astype(bf16)
        for i in range(PAIR):
            m = c * PAIR + i
            tendency = lax.dot_general(
                plain[i * ROWS : (i + 1) * ROWS],
                leg[m],
                (((1,), (1,)), ((), ())),
                preferred_element_type=f32,
            )
            wave_id = (me * STEPS + m).astype(f32)
            advection = wave_id * (advect_rate / waves_total)
            source = chosen[m * ROWS : (m + 1) * ROWS].astype(f32)
            out_ref[m * ROWS : (m + 1) * ROWS] = (source + advection * tendency) * keep

    for copy in go + ret:
        copy.wait_send()
    for c in range(STEPS):
        for kind in range(3):
            pass_copy(c, kind).wait_send()

    @pl.when(inner)
    def _():
        for c in range(STEPS):
            for far in range(2):
                cross_copy(c, far).wait_send()


def in_one_kernel(state, legendre, lat_weights, region, sources):
    waves_local, degrees, latitudes = legendre.shape
    waves_total = waves_local * WAVES
    points = quadrature_points(waves_total)
    table_high, table_low = split_table(wave_table(waves_total, points))
    fourier = wave_table(waves_total, NLON).astype(jnp.bfloat16)
    forward, backward = order_tables(state.shape[2] // 4)
    unused = np.zeros((CHUNK_ROWS, 128 - CHUNK_ROWS), jnp.bfloat16)
    flat = [t.reshape(2 * waves_total, -1) for t in (fourier, table_high, table_low)]
    table = np.concatenate(flat + [forward, unused, backward, unused], axis=1)
    vmem = pl.BlockSpec(memory_space=pltpu.VMEM)
    smem = pl.BlockSpec(memory_space=pltpu.SMEM)
    hbm = pl.BlockSpec(memory_space=pl.ANY)
    rows = waves_local * ROWS
    block = (rows, degrees)
    grid_rows = (rows, latitudes)
    dma = pltpu.SemaphoreType.DMA
    bf16 = jnp.bfloat16
    stepped, scores = pl.pallas_call(
        functools.partial(
            step_kernel,
            scale=(2.0 * waves_total) ** -0.5,
            analysis_scale=NLON**-0.5 * (NLON / points),
            waves_total=waves_total,
            points=points,
        ),
        out_shape=(
            jax.ShapeDtypeStruct(block, jnp.float32),
            jax.ShapeDtypeStruct((8, 128), jnp.float32),
        ),
        in_specs=[hbm, hbm, vmem, smem, smem, hbm],
        out_specs=(vmem, vmem),
        scratch_shapes=[
            pltpu.VMEM(block, jnp.float32),
            pltpu.VMEM(table.shape, bf16),
            pltpu.VMEM((2, 4 * points, 8 * waves_total), bf16),
            pltpu.VMEM((2, 8 * waves_total, 4 * points), bf16),
            pltpu.VMEM((2 * waves_local, latitudes), jnp.float32),
            pltpu.VMEM((2 * waves_local, latitudes), bf16),
            pltpu.VMEM((2 * waves_total, latitudes), bf16),
            pltpu.VMEM(block, bf16),
            pltpu.VMEM(legendre.shape, bf16),
            pltpu.VMEM(grid_rows, bf16),
            pltpu.VMEM(grid_rows, bf16),
            pltpu.VMEM((4 * points, latitudes), bf16),
            pltpu.VMEM(grid_rows, bf16),
            pltpu.VMEM(grid_rows, bf16),
            pltpu.VMEM((STEPS, 2, ROWS, degrees), bf16),
            pltpu.VMEM((STEPS, ROWS, degrees), bf16),
        ]
        + [pltpu.VMEM((4, ROWS, degrees), bf16)] * STEPS
        + [
            dma((CHUNKS,)),
            dma,
            dma((STEPS,)),
            dma((WAVES - 1, CHUNKS)),
            dma((WAVES - 1, CHUNKS)),
            dma((WAVES - 1, CHUNKS)),
            dma((WAVES - 1, CHUNKS)),
            dma((WAVES - 1,)),
            dma((WAVES - 1,)),
            dma((3, STEPS)),
            dma((3, STEPS)),
            dma((2, STEPS)),
            dma((STEPS,)),
        ],
        compiler_params=pltpu.CompilerParams(
            collective_id=0, has_side_effects=True, vmem_limit_bytes=48 * 1024 * 1024
        ),
    )(state.reshape(block), legendre, lat_weights, region, sources, jnp.asarray(table))
    return (stepped.reshape(state.shape), scores[0, :1])


def solution(mesh):
    in_specs = (P("member", "wave", None, None), P("wave", None, None), P(), P(), P())
    out_specs = (P("member", "wave", None, None), P("member"))

    def run(state, legendre, lat_weights, region, sources):
        shape = (state.shape[1] // mesh.shape["wave"], state.shape[2], state.shape[3], legendre.shape[2])
        fits = mesh.shape["wave"] == 4 and mesh.shape["member"] == 8 and shape == (8, 32, 640, 640)
        return jax.shard_map(
            in_one_kernel if fits else on_device,
            mesh=mesh,
            in_specs=in_specs,
            out_specs=out_specs,
            check_vma=False,
        )(state, legendre, lat_weights, region, sources)

    return run
```

```python
import functools

import jax
import jax.numpy as jnp
import numpy as np
from jax import lax
from jax.experimental import pallas as pl
from jax.experimental.pallas import tpu as pltpu
from jax.sharding import PartitionSpec as P

NLON = 2560


advect_rate = 2.0


def wave_table(waves_total, points):
    wave_index = np.arange(waves_total)[:, None]
    angles = (wave_index * np.arange(points)[None, :] % points) * (2.0 * np.pi / points)
    return np.stack([np.cos(angles), -np.sin(angles)], axis=1)


def split_table(table):
    high = table.astype(jnp.bfloat16)
    low = (table - high.astype(np.float64)).astype(jnp.bfloat16)
    return high, low


def quadrature_points(waves_total):
    return (3 * (waves_total - 1)) // 128 * 128 + 128


def on_device(state, legendre, lat_weights, region, sources):
    wave_count = lax.axis_size("wave")
    waves_local = legendre.shape[0]
    waves_total = waves_local * wave_count
    degrees = legendre.shape[1]
    latitudes = legendre.shape[2]
    lat_rows = latitudes // wave_count
    state_rows = state.shape[2]
    level_count = state_rows // 4
    points = quadrature_points(waves_total)
    table_high, table_low = split_table(wave_table(waves_total, points))
    spectral = state[0]
    fourier_coef = jnp.einsum(
        "mrn,mnl->mrl", spectral.astype(jnp.bfloat16), legendre, preferred_element_type=jnp.float32
    )
    fourier_coef = fourier_coef.astype(jnp.bfloat16).reshape(
        waves_local, 2, 2 * level_count, latitudes
    )
    synthesis_scale = (2.0 * waves_total) ** (-0.5)
    coef = lax.all_to_all(fourier_coef, "wave", split_axis=3, concat_axis=0, tiled=True)
    gridded = synthesis_scale * jnp.einsum(
        "mckl,mcx->klx",
        jnp.concatenate([coef, coef], axis=1),
        jnp.concatenate([table_high, table_low], axis=1),
        preferred_element_type=jnp.float32,
    )
    lat_start = lax.axis_index("wave") * lat_rows
    local_weights = lax.dynamic_slice_in_dim(lat_weights, lat_start, lat_rows)
    wind_grid = gridded[:level_count]
    temper_grid = gridded[level_count:]
    fluxes = (
        jnp.concatenate([0.5 * wind_grid * wind_grid, wind_grid * temper_grid], axis=0)
        * local_weights[None, :, None]
    )
    fluxes = fluxes.astype(jnp.bfloat16)
    fourier = wave_table(waves_total, NLON).reshape(2 * waves_total, NLON).astype(jnp.bfloat16)
    lon_index = lax.broadcasted_iota(jnp.int32, (1, NLON), 1)
    lon_inside = (lon_index >= region[2]) & (lon_index < region[3])
    gram = jnp.einsum(
        "px,qx->pq",
        jnp.where(lon_inside, fourier, jnp.zeros((), jnp.bfloat16)),
        fourier,
        preferred_element_type=jnp.float32,
    )
    lowest = coef[:, :, -1].reshape(2 * waves_total, lat_rows).astype(jnp.float32)
    gram_lowest = jnp.dot(gram, lowest, precision=lax.Precision.HIGHEST)
    lat_index = lat_start + lax.broadcasted_iota(jnp.int32, (lat_rows,), 0)
    in_band = (lat_index >= region[0]) & (lat_index < region[1])
    region_part = jnp.sum(
        jnp.where(in_band, local_weights, 0.0)[None, :] * lowest * gram_lowest
    ) / (2.0 * waves_total)
    region_total = lax.psum(region_part, "wave")
    every_lat = lax.broadcasted_iota(jnp.int32, (latitudes,), 0)
    lat_inside = (every_lat >= region[0]) & (every_lat < region[1])
    region_weight = jnp.sum(jnp.where(lat_inside, lat_weights, 0.0)) * (
        region[3] - region[2]
    ).astype(jnp.float32)
    scores = (region_total / region_weight).reshape(1)
    analysis_scale = NLON ** (-0.5) * (NLON / points)
    flux_high = jnp.einsum("klx,mcx->mckl", fluxes, table_high, preferred_element_type=jnp.float32)
    flux_low = jnp.einsum("klx,mcx->mckl", fluxes, table_low, preferred_element_type=jnp.float32)
    flux_coef = (analysis_scale * (flux_high + flux_low)).astype(jnp.bfloat16)
    tendency = jnp.einsum(
        "mckl,mnl->mckn",
        lax.all_to_all(flux_coef, "wave", split_axis=0, concat_axis=3, tiled=True),
        legendre,
        preferred_element_type=jnp.float32,
    )
    wave_ids = lax.axis_index("wave") * waves_local + lax.broadcasted_iota(
        jnp.int32, (waves_local, 1, 1), 0
    )
    advection = advect_rate * wave_ids.astype(jnp.float32) / waves_total
    degree_ids = lax.broadcasted_iota(jnp.int32, (1, 1, degrees), 2).astype(jnp.float32)
    damping = 1.0 + ((degree_ids + 1.0) / degrees) ** 2
    spectral_split = spectral.reshape(waves_local, 2, 2 * level_count, degrees)
    real_part = (spectral_split[:, 0] + advection * tendency[:, 1]) / damping
    imag_part = (spectral_split[:, 1] - advection * tendency[:, 0]) / damping
    stepped = jnp.stack([real_part, imag_part], axis=1).reshape(1, waves_local, state_rows, degrees)
    source_member = sources[lax.axis_index("member")]
    shards = lax.all_gather(stepped.astype(jnp.bfloat16), "member", axis=0, tiled=True)
    cloned = lax.dynamic_slice_in_dim(shards, source_member, 1, axis=0).astype(jnp.float32)
    return (cloned, scores)


MESH = pl.DeviceIdType.MESH
WAVES = 4
CHUNKS = 2
PAIR = 4
ROWS = 32
SET_ROWS = ROWS // 2
LOCAL_WAVES = CHUNKS * PAIR
CHUNK_ROWS = PAIR * SET_ROWS
PART_ROWS = CHUNK_ROWS // WAVES
OWNED_ROWS = CHUNKS * PART_ROWS
STEPS = 4


def order_tables():
    forward = np.zeros((CHUNK_ROWS, CHUNK_ROWS))
    backward = np.zeros((CHUNK_ROWS, CHUNK_ROWS))
    for m in range(PAIR):
        for c in range(2):
            for f in range(2):
                for k in range(WAVES):
                    plain = ((m * 2 + c) * 2 + f) * WAVES + k
                    forward[((k * PAIR + m) * 2 + c) * 2 + f, plain] = 1.0
                    backward[plain, ((k * PAIR + m) * 2 + 1 - c) * 2 + f] = 1.0 - 2.0 * c
    return forward.astype(jnp.bfloat16), backward.astype(jnp.bfloat16)


def step_kernel(
    state_hbm, legendre_ref, weights_ref, region_ref, sources_ref, table_hbm,
    out_ref, score_ref,
    state_ref, set_ref, table_ref, synth_ref, analysis_ref, low_ref, low_sent, low_held,
    chosen, leg, sent, held, flux, back_sent, back, cross, crossed,
    *rest, scale, analysis_scale, waves_total, points,
):
    pools = rest[: 2 * STEPS]
    (
        state_sem, table_sem, leg_sem, go_send, go_recv, ret_send, ret_recv, score_send, score_recv,
        pass_send, pass_recv, cross_send, cross_recv,
    ) = rest[2 * STEPS :]
    me = lax.axis_index("wave")
    slot = lax.axis_index("member")
    z = slot // 2
    x = slot % 2
    half = z // 2
    inner = z % 2 != half % 2
    z_mate = (z + 1 - 2 * (z % 2)) * 2 + x
    x_mate = z * 2 + 1 - x
    far_inner = (2 - half) * 2 + x
    far_outer = (3 - 3 * half) * 2 + x
    here = slot - half * 4
    z_here = z_mate - half * 4
    degrees = state_ref.shape[1]
    lat_count = weights_ref.shape[0]
    f32 = jnp.float32
    bf16 = jnp.bfloat16
    levels = ROWS // 4

    loads = [
        pltpu.make_async_copy(legendre_ref.at[m], leg.at[m], leg_sem.at[m]) for m in range(LOCAL_WAVES)
    ]
    state_loads = [
        pltpu.make_async_copy(
            state_hbm.at[pl.ds(c * PAIR * ROWS, PAIR * ROWS)],
            state_ref.at[pl.ds(c * PAIR * ROWS, PAIR * ROWS)],
            state_sem.at[c],
        )
        for c in range(CHUNKS)
    ]
    table_load = pltpu.make_async_copy(table_hbm, table_ref, table_sem)
    for load in state_loads + [table_load] + loads:
        load.start()

    barrier = pltpu.get_barrier_semaphore()
    for d in range(1, WAVES):
        pl.semaphore_signal(
            barrier, inc=1, device_id={"wave": (me + d) % WAVES}, device_id_type=MESH
        )
    for mate in (z_mate, x_mate, far_inner):
        pl.semaphore_signal(barrier, inc=1, device_id={"member": mate}, device_id_type=MESH)

    @pl.when(inner)
    def _():
        pl.semaphore_signal(barrier, inc=1, device_id={"member": far_outer}, device_id_type=MESH)

    for c in range(CHUNKS):
        state_loads[c].wait()
        for m in range(c * PAIR, (c + 1) * PAIR):
            for group in range(4):
                for early in range(2):
                    first = m * SET_ROWS + group * WAVES
                    source = m * ROWS + group * levels + (1 - early) * WAVES
                    set_ref[1 - early, first : first + WAVES] = state_ref[source : source + WAVES]
        for g in range(c * 2, c * 2 + 2):
            pools[g][here] = set_ref[0, g * ROWS : (g + 1) * ROWS].astype(bf16)

    @pl.when(inner)
    def _():
        pl.semaphore_wait(barrier, 7)

    @pl.when(jnp.logical_not(inner))
    def _():
        pl.semaphore_wait(barrier, 6)

    def member_copy(source, target, to, send_sem, recv_sem):
        return pltpu.make_async_remote_copy(
            src_ref=source, dst_ref=target, send_sem=send_sem, recv_sem=recv_sem,
            device_id={"member": to}, device_id_type=MESH,
        )

    def pass_copy(c, kind):
        block = pools[c].at[z_here if kind == 2 else here]
        return member_copy(
            block, block, z_mate if kind == 0 else x_mate, pass_send.at[kind, c], pass_recv.at[kind, c]
        )

    def cross_copy(c, far):
        return member_copy(
            cross.at[c, far],
            crossed.at[c],
            far_outer if far else far_inner,
            cross_send.at[far, c],
            cross_recv.at[c],
        )

    def half_index(member_slot):
        return jnp.clip(sources_ref[member_slot] - half * 4, 0, 3)

    inner_pick = half_index(far_inner)
    outer_pick = half_index(far_outer)
    origin = sources_ref[slot] - half * 4
    near = (origin >= 0) & (origin < 4)
    choice = jnp.clip(origin, 0, 3)

    def begin_pass(c):
        pass_copy(c, 0).start()
        if c % STEPS < 2:
            pass_copy(c, 1).start()

    for c in range(STEPS):
        begin_pass(c)

    def forward_pass(c):
        pass_copy(c, 0).wait_recv()
        pass_copy(c, 2).start()
        if c % STEPS + 2 < STEPS:
            pass_copy(c + 2, 1).start()

    def send_across(c):
        pass_copy(c, 1).wait_recv()
        pass_copy(c, 2).wait_recv()

        @pl.when(inner)
        def _():
            cross[c, 1] = pools[c][outer_pick]
            cross_copy(c, 1).start()
            cross[c, 0] = pools[c][inner_pick]
            cross_copy(c, 0).start()

    def wave_copy(source, target, h, c, d, send_sem, recv_sem):
        to = (me + d) % WAVES
        return pltpu.make_async_remote_copy(
            src_ref=source.at[h, pl.ds(pl.multiple_of(to * OWNED_ROWS + c * PART_ROWS, PART_ROWS), PART_ROWS)],
            dst_ref=target.at[h, pl.ds(pl.multiple_of(me * OWNED_ROWS + c * PART_ROWS, PART_ROWS), PART_ROWS)],
            send_sem=send_sem.at[h, d - 1, c],
            recv_sem=recv_sem.at[h, d - 1, c],
            device_id={"wave": to},
            device_id_type=MESH,
        )

    def low_copy(d):
        return pltpu.make_async_remote_copy(
            src_ref=low_sent,
            dst_ref=low_held.at[pl.ds(pl.multiple_of(me * 16, 16), 16)],
            send_sem=score_send.at[d - 1],
            recv_sem=score_recv.at[d - 1],
            device_id={"wave": (me + d) % WAVES},
            device_id_type=MESH,
        )

    my_rows = me * OWNED_ROWS
    mine = pl.ds(pl.multiple_of(my_rows, OWNED_ROWS), OWNED_ROWS)
    columns = fourier_columns = table_ref.shape[1] - 4 * 128

    def go_copy(h, c, d):
        return wave_copy(sent, held, h, c, d, go_send, go_recv)

    def ret_copy(h, c, d):
        return wave_copy(back_sent, back, h, c, d, ret_send, ret_recv)

    def transform(h, c):
        parts = []
        for m in range(c * PAIR, (c + 1) * PAIR):
            rows = slice(m * SET_ROWS, (m + 1) * SET_ROWS)
            if h == 1:
                loads[m].wait()
                block = set_ref[1, rows].astype(bf16)
            else:
                block = chosen[rows]
            part = jnp.dot(block, leg[m], preferred_element_type=f32)
            parts.append(part)
            if h == 1:
                for real in range(2):
                    row = (real + 1) * (SET_ROWS // 2) - 1
                    low_ref[m * 2 + real : m * 2 + real + 1] = part[row : row + 1]
        coef = jnp.concatenate(parts, axis=0).astype(bf16)
        forward = table_ref[:, columns + 256 : columns + 256 + CHUNK_ROWS]
        ordered = jnp.dot(forward, coef, preferred_element_type=f32).astype(bf16)
        for w in range(WAVES):
            first = w * OWNED_ROWS + c * PART_ROWS
            sent[h, first : first + PART_ROWS] = ordered[w * PART_ROWS : (w + 1) * PART_ROWS]
        for d in (2, 1, 3):
            go_copy(h, c, d).start()

    def take_source(g):
        cross_copy(g, 0).wait_recv()
        return jnp.where(near, pools[g][choice], crossed[g])

    table_load.wait()
    transform(1, 0)
    forward_pass(0)
    transform(1, 1)
    low_sent[...] = low_ref[...].astype(bf16)
    low_held[pl.ds(pl.multiple_of(me * 16, 16), 16)] = low_sent[...]
    for d in range(1, WAVES):
        low_copy(d).start()
    held[1, mine] = sent[1, mine]
    forward_pass(1)
    forward_pass(2)
    send_across(0)

    coef_rows = 4 * waves_total
    owner_of = lax.broadcasted_iota(jnp.int32, (2 * waves_total, coef_rows), 0)
    column = lax.broadcasted_iota(jnp.int32, (2 * waves_total, coef_rows), 1)
    widen = jnp.where(column // 2 == owner_of, 1.0, 0.0).astype(bf16)
    tall_owner = lax.broadcasted_iota(jnp.int32, (coef_rows, 2 * waves_total), 1)
    tall_row = lax.broadcasted_iota(jnp.int32, (coef_rows, 2 * waves_total), 0)
    lengthen = jnp.where(tall_row // 2 == tall_owner, 1.0, 0.0).astype(bf16)
    synth_column = lax.broadcasted_iota(jnp.int32, (points, coef_rows), 1) % 2
    analysis_row = lax.broadcasted_iota(jnp.int32, (coef_rows, points), 0) % 2
    for part in range(2):
        waves = table_ref[:, columns + part * 128 : columns + part * 128 + points]
        wide = lax.dot_general(
            waves, widen, (((0,), (0,)), ((), ())), preferred_element_type=f32
        )
        tall = jnp.dot(lengthen, waves, preferred_element_type=f32)
        for f in range(2):
            at = slice(f * points, (f + 1) * points)
            synth_ref[at, part * coef_rows : (part + 1) * coef_rows] = jnp.where(
                synth_column == f, wide, 0.0
            ).astype(bf16)
            analysis_ref[part, :, at] = jnp.where(analysis_row == f, tall, 0.0).astype(bf16)
    forward_pass(3)
    send_across(1)

    low, high = region_ref[2], region_ref[3]
    lon = lax.broadcasted_iota(jnp.int32, (1, fourier_columns), 1)
    lon_inside = jnp.where((lon >= low) & (lon < high), 1.0, 0.0)
    fourier = table_ref[:, :fourier_columns]
    gram = lax.dot_general(
        (fourier.astype(f32) * lon_inside).astype(bf16),
        fourier,
        (((1,), (1,)), ((), ())),
        preferred_element_type=f32,
    )
    gram_high = gram.astype(bf16)
    gram_low = (gram - gram_high.astype(f32)).astype(bf16)
    lat = lax.broadcasted_iota(jnp.int32, (1, lat_count), 1)
    weights = weights_ref[...].reshape(1, lat_count)
    region_weights = jnp.where((lat >= region_ref[0]) & (lat < region_ref[1]), weights, 0.0)
    weight_sum = jnp.sum(region_weights, axis=1, keepdims=True) * (high - low).astype(f32)

    send_across(2)
    scaled = weights * (scale * scale)

    def grid_phase(h):
        for c in range(CHUNKS):
            for d in (2, 1, 3):
                go_copy(h, c, d).wait_recv()
        coefs = held[h]
        grid = jnp.dot(
            synth_ref[...], jnp.concatenate([coefs, coefs], axis=0), preferred_element_type=f32
        )
        wind = grid[:points]
        weighted = wind * scaled
        flux[h, :points] = (0.5 * weighted * wind).astype(bf16)
        flux[h, points:] = (weighted * grid[points:]).astype(bf16)
        fluxes = flux[h]
        back_sent[h] = (
            analysis_scale
            * (
                jnp.dot(analysis_ref[0], fluxes, preferred_element_type=f32)
                + jnp.dot(analysis_ref[1], fluxes, preferred_element_type=f32)
            )
        ).astype(bf16)
        for c in range(CHUNKS):
            for d in (2, 1, 3):
                ret_copy(h, c, d).start()
        back[h, mine] = back_sent[h, mine]

    grid_phase(1)
    send_across(3)
    for c in range(CHUNKS):
        for g in range(c * 2, c * 2 + 2):
            chosen[g * ROWS : (g + 1) * ROWS] = take_source(g)
        transform(0, c)
    held[0, mine] = sent[0, mine]

    for d in range(1, WAVES):
        low_copy(d).wait()
    lowest = low_held[...]
    spread = jnp.dot(gram_high, lowest, preferred_element_type=f32) + jnp.dot(
        gram_low, lowest, preferred_element_type=f32
    )
    squares = jnp.sum(lowest.astype(f32) * spread, axis=0, keepdims=True) * (
        region_weights * (scale * scale)
    )
    score = jnp.sum(squares, axis=1, keepdims=True) / weight_sum
    score_ref[...] = jnp.broadcast_to(score, score_ref.shape)

    degree = lax.broadcasted_iota(jnp.int32, (1, degrees), 1).astype(f32)
    keep = 1.0 / (1.0 + ((degree + 1.0) / degrees) ** 2)
    backward = table_ref[:, columns + 384 : columns + 384 + CHUNK_ROWS]
    def tendencies(h, c):
        for d in (2, 1, 3):
            ret_copy(h, c, d).wait_recv()
        arrived = jnp.concatenate(
            [
                back[h, w * OWNED_ROWS + c * PART_ROWS : w * OWNED_ROWS + (c + 1) * PART_ROWS]
                for w in range(WAVES)
            ],
            axis=0,
        )
        plain = jnp.dot(backward, arrived, preferred_element_type=f32).astype(bf16)
        for i in range(PAIR):
            m = c * PAIR + i
            rows = slice(m * SET_ROWS, (m + 1) * SET_ROWS)
            tendency = lax.dot_general(
                plain[i * SET_ROWS : (i + 1) * SET_ROWS],
                leg[m],
                (((1,), (1,)), ((), ())),
                preferred_element_type=f32,
            )
            wave_id = (me * LOCAL_WAVES + m).astype(f32)
            advection = wave_id * (advect_rate / waves_total)
            source = set_ref[1, rows] if h == 1 else chosen[rows].astype(f32)
            stepped = (source + advection * tendency) * keep
            if h == 1:
                g = STEPS + m // 2
                pools[g][here, (m % 2) * SET_ROWS : (m % 2 + 1) * SET_ROWS] = stepped.astype(bf16)
                if m % 2 == 1:
                    begin_pass(g)
            else:
                put_rows(m, 0, stepped)

    def put_rows(m, late, values):
        for group in range(4):
            first = m * ROWS + group * levels + late * WAVES
            out_ref[first : first + WAVES] = values[group * WAVES : (group + 1) * WAVES]

    tendencies(1, 0)
    tendencies(1, 1)
    forward_pass(STEPS)
    forward_pass(STEPS + 1)
    grid_phase(0)
    forward_pass(STEPS + 2)
    forward_pass(STEPS + 3)
    for g in range(STEPS, 2 * STEPS):
        send_across(g)
    tendencies(0, 0)
    tendencies(0, 1)
    for g in range(STEPS, 2 * STEPS):
        block = take_source(g).astype(f32)
        for i in range(2):
            put_rows((g - STEPS) * 2 + i, 1, block[i * SET_ROWS : (i + 1) * SET_ROWS])

    for h in range(2):
        for c in range(CHUNKS):
            for d in (2, 1, 3):
                go_copy(h, c, d).wait_send()
                ret_copy(h, c, d).wait_send()
    for c in range(2 * STEPS):
        for kind in range(3):
            pass_copy(c, kind).wait_send()

    @pl.when(inner)
    def _():
        for c in range(2 * STEPS):
            for far in range(2):
                cross_copy(c, far).wait_send()


def in_one_kernel(state, legendre, lat_weights, region, sources):
    waves_local, degrees, latitudes = legendre.shape
    waves_total = waves_local * WAVES
    points = quadrature_points(waves_total)
    table_high, table_low = split_table(wave_table(waves_total, points))
    fourier = wave_table(waves_total, NLON).astype(jnp.bfloat16)
    forward, backward = order_tables()
    unused = np.zeros((CHUNK_ROWS, 128 - CHUNK_ROWS), jnp.bfloat16)
    flat = [t.reshape(2 * waves_total, -1) for t in (fourier, table_high, table_low)]
    table = np.concatenate(flat + [forward, unused, backward, unused], axis=1)
    vmem = pl.BlockSpec(memory_space=pltpu.VMEM)
    smem = pl.BlockSpec(memory_space=pltpu.SMEM)
    hbm = pl.BlockSpec(memory_space=pl.ANY)
    rows = waves_local * ROWS
    block = (rows, degrees)
    grid_rows = (2, 4 * waves_total, latitudes)
    dma = pltpu.SemaphoreType.DMA
    bf16 = jnp.bfloat16
    stepped, scores = pl.pallas_call(
        functools.partial(
            step_kernel,
            scale=(2.0 * waves_total) ** -0.5,
            analysis_scale=NLON**-0.5 * (NLON / points),
            waves_total=waves_total,
            points=points,
        ),
        out_shape=(
            jax.ShapeDtypeStruct(block, jnp.float32),
            jax.ShapeDtypeStruct((8, 128), jnp.float32),
        ),
        in_specs=[hbm, hbm, vmem, smem, smem, hbm],
        out_specs=(vmem, vmem),
        scratch_shapes=[
            pltpu.VMEM(block, jnp.float32),
            pltpu.VMEM((2, rows // 2, degrees), jnp.float32),
            pltpu.VMEM(table.shape, bf16),
            pltpu.VMEM((2 * points, 8 * waves_total), bf16),
            pltpu.VMEM((2, 4 * waves_total, 2 * points), bf16),
            pltpu.VMEM((2 * waves_local, latitudes), jnp.float32),
            pltpu.VMEM((2 * waves_local, latitudes), bf16),
            pltpu.VMEM((2 * waves_total, latitudes), bf16),
            pltpu.VMEM((rows // 2, degrees), bf16),
            pltpu.VMEM(legendre.shape, bf16),
            pltpu.VMEM(grid_rows, bf16),
            pltpu.VMEM(grid_rows, bf16),
            pltpu.VMEM((2, 2 * points, latitudes), bf16),
            pltpu.VMEM(grid_rows, bf16),
            pltpu.VMEM(grid_rows, bf16),
            pltpu.VMEM((2 * STEPS, 2, ROWS, degrees), bf16),
            pltpu.VMEM((2 * STEPS, ROWS, degrees), bf16),
        ]
        + [pltpu.VMEM((4, ROWS, degrees), bf16)] * (2 * STEPS)
        + [
            dma((CHUNKS,)),
            dma,
            dma((LOCAL_WAVES,)),
            dma((2, WAVES - 1, CHUNKS)),
            dma((2, WAVES - 1, CHUNKS)),
            dma((2, WAVES - 1, CHUNKS)),
            dma((2, WAVES - 1, CHUNKS)),
            dma((WAVES - 1,)),
            dma((WAVES - 1,)),
            dma((3, 2 * STEPS)),
            dma((3, 2 * STEPS)),
            dma((2, 2 * STEPS)),
            dma((2 * STEPS,)),
        ],
        compiler_params=pltpu.CompilerParams(
            collective_id=0, has_side_effects=True, vmem_limit_bytes=56 * 1024 * 1024
        ),
    )(state.reshape(block), legendre, lat_weights, region, sources, jnp.asarray(table))
    return (stepped.reshape(state.shape), scores[0, :1])


def solution(mesh):
    in_specs = (P("member", "wave", None, None), P("wave", None, None), P(), P(), P())
    out_specs = (P("member", "wave", None, None), P("member"))

    def run(state, legendre, lat_weights, region, sources):
        shape = (state.shape[1] // mesh.shape["wave"], state.shape[2], state.shape[3], legendre.shape[2])
        fits = mesh.shape["wave"] == 4 and mesh.shape["member"] == 8 and shape == (8, 32, 640, 640)
        return jax.shard_map(
            in_one_kernel if fits else on_device,
            mesh=mesh,
            in_specs=in_specs,
            out_specs=out_specs,
            check_vma=False,
        )(state, legendre, lat_weights, region, sources)

    return run
```

```python
import functools

import jax
import jax.numpy as jnp
import numpy as np
from jax import lax
from jax.experimental import pallas as pl
from jax.experimental.pallas import tpu as pltpu
from jax.sharding import PartitionSpec as P

NLON = 2560


advect_rate = 2.0


def wave_table(waves_total, points):
    wave_index = np.arange(waves_total)[:, None]
    angles = (wave_index * np.arange(points)[None, :] % points) * (2.0 * np.pi / points)
    return np.stack([np.cos(angles), -np.sin(angles)], axis=1)


def split_table(table):
    high = table.astype(jnp.bfloat16)
    low = (table - high.astype(np.float64)).astype(jnp.bfloat16)
    return high, low


def quadrature_points(waves_total):
    return (3 * (waves_total - 1)) // 128 * 128 + 128


def on_device(state, legendre, lat_weights, region, sources):
    wave_count = lax.axis_size("wave")
    waves_local = legendre.shape[0]
    waves_total = waves_local * wave_count
    degrees = legendre.shape[1]
    latitudes = legendre.shape[2]
    lat_rows = latitudes // wave_count
    state_rows = state.shape[2]
    level_count = state_rows // 4
    points = quadrature_points(waves_total)
    table_high, table_low = split_table(wave_table(waves_total, points))
    spectral = state[0]
    fourier_coef = jnp.einsum(
        "mrn,mnl->mrl", spectral.astype(jnp.bfloat16), legendre, preferred_element_type=jnp.float32
    )
    fourier_coef = fourier_coef.astype(jnp.bfloat16).reshape(
        waves_local, 2, 2 * level_count, latitudes
    )
    synthesis_scale = (2.0 * waves_total) ** (-0.5)
    coef = lax.all_to_all(fourier_coef, "wave", split_axis=3, concat_axis=0, tiled=True)
    gridded = synthesis_scale * jnp.einsum(
        "mckl,mcx->klx",
        jnp.concatenate([coef, coef], axis=1),
        jnp.concatenate([table_high, table_low], axis=1),
        preferred_element_type=jnp.float32,
    )
    lat_start = lax.axis_index("wave") * lat_rows
    local_weights = lax.dynamic_slice_in_dim(lat_weights, lat_start, lat_rows)
    wind_grid = gridded[:level_count]
    temper_grid = gridded[level_count:]
    fluxes = (
        jnp.concatenate([0.5 * wind_grid * wind_grid, wind_grid * temper_grid], axis=0)
        * local_weights[None, :, None]
    )
    fluxes = fluxes.astype(jnp.bfloat16)
    fourier = wave_table(waves_total, NLON).reshape(2 * waves_total, NLON).astype(jnp.bfloat16)
    lon_index = lax.broadcasted_iota(jnp.int32, (1, NLON), 1)
    lon_inside = (lon_index >= region[2]) & (lon_index < region[3])
    gram = jnp.einsum(
        "px,qx->pq",
        jnp.where(lon_inside, fourier, jnp.zeros((), jnp.bfloat16)),
        fourier,
        preferred_element_type=jnp.float32,
    )
    lowest = coef[:, :, -1].reshape(2 * waves_total, lat_rows).astype(jnp.float32)
    gram_lowest = jnp.dot(gram, lowest, precision=lax.Precision.HIGHEST)
    lat_index = lat_start + lax.broadcasted_iota(jnp.int32, (lat_rows,), 0)
    in_band = (lat_index >= region[0]) & (lat_index < region[1])
    region_part = jnp.sum(
        jnp.where(in_band, local_weights, 0.0)[None, :] * lowest * gram_lowest
    ) / (2.0 * waves_total)
    region_total = lax.psum(region_part, "wave")
    every_lat = lax.broadcasted_iota(jnp.int32, (latitudes,), 0)
    lat_inside = (every_lat >= region[0]) & (every_lat < region[1])
    region_weight = jnp.sum(jnp.where(lat_inside, lat_weights, 0.0)) * (
        region[3] - region[2]
    ).astype(jnp.float32)
    scores = (region_total / region_weight).reshape(1)
    analysis_scale = NLON ** (-0.5) * (NLON / points)
    flux_high = jnp.einsum("klx,mcx->mckl", fluxes, table_high, preferred_element_type=jnp.float32)
    flux_low = jnp.einsum("klx,mcx->mckl", fluxes, table_low, preferred_element_type=jnp.float32)
    flux_coef = (analysis_scale * (flux_high + flux_low)).astype(jnp.bfloat16)
    tendency = jnp.einsum(
        "mckl,mnl->mckn",
        lax.all_to_all(flux_coef, "wave", split_axis=0, concat_axis=3, tiled=True),
        legendre,
        preferred_element_type=jnp.float32,
    )
    wave_ids = lax.axis_index("wave") * waves_local + lax.broadcasted_iota(
        jnp.int32, (waves_local, 1, 1), 0
    )
    advection = advect_rate * wave_ids.astype(jnp.float32) / waves_total
    degree_ids = lax.broadcasted_iota(jnp.int32, (1, 1, degrees), 2).astype(jnp.float32)
    damping = 1.0 + ((degree_ids + 1.0) / degrees) ** 2
    spectral_split = spectral.reshape(waves_local, 2, 2 * level_count, degrees)
    real_part = (spectral_split[:, 0] + advection * tendency[:, 1]) / damping
    imag_part = (spectral_split[:, 1] - advection * tendency[:, 0]) / damping
    stepped = jnp.stack([real_part, imag_part], axis=1).reshape(1, waves_local, state_rows, degrees)
    source_member = sources[lax.axis_index("member")]
    shards = lax.all_gather(stepped.astype(jnp.bfloat16), "member", axis=0, tiled=True)
    cloned = lax.dynamic_slice_in_dim(shards, source_member, 1, axis=0).astype(jnp.float32)
    return (cloned, scores)


MESH = pl.DeviceIdType.MESH
WAVES = 4
CHUNKS = 2
PAIR = 4
ROWS = 32
SET_ROWS = ROWS // 2
LOCAL_WAVES = CHUNKS * PAIR
CHUNK_ROWS = PAIR * SET_ROWS
PART_ROWS = CHUNK_ROWS // WAVES
OWNED_ROWS = CHUNKS * PART_ROWS
STEPS = 4


def order_tables():
    forward = np.zeros((CHUNK_ROWS, CHUNK_ROWS))
    backward = np.zeros((CHUNK_ROWS, CHUNK_ROWS))
    for m in range(PAIR):
        for c in range(2):
            for f in range(2):
                for k in range(WAVES):
                    plain = ((m * 2 + c) * 2 + f) * WAVES + k
                    forward[((k * PAIR + m) * 2 + c) * 2 + f, plain] = 1.0
                    backward[plain, ((k * PAIR + m) * 2 + 1 - c) * 2 + f] = 1.0 - 2.0 * c
    return forward.astype(jnp.bfloat16), backward.astype(jnp.bfloat16)


def step_kernel(
    state_hbm, legendre_ref, weights_ref, region_ref, sources_ref, table_hbm,
    out_ref, score_ref,
    state_ref, set_ref, table_ref, synth_ref, analysis_ref, low_ref, low_sent, low_held,
    chosen, leg, sent, held, flux, back_sent, back, cross, crossed,
    *rest, scale, analysis_scale, waves_total, points,
):
    pools = rest[: 2 * STEPS]
    (
        state_sem, table_sem, leg_sem, go_send, go_recv, ret_send, ret_recv, score_send, score_recv,
        pass_send, pass_recv, cross_send, cross_recv,
    ) = rest[2 * STEPS :]
    me = lax.axis_index("wave")
    slot = lax.axis_index("member")
    z = slot // 2
    x = slot % 2
    half = z // 2
    inner = z % 2 != half % 2
    z_mate = (z + 1 - 2 * (z % 2)) * 2 + x
    x_mate = z * 2 + 1 - x
    far_inner = (2 - half) * 2 + x
    far_outer = (3 - 3 * half) * 2 + x
    here = slot - half * 4
    z_here = z_mate - half * 4
    degrees = state_ref.shape[1]
    lat_count = weights_ref.shape[0]
    f32 = jnp.float32
    bf16 = jnp.bfloat16
    levels = ROWS // 4

    loads = [
        pltpu.make_async_copy(legendre_ref.at[m], leg.at[m], leg_sem.at[m]) for m in range(LOCAL_WAVES)
    ]
    state_loads = [
        pltpu.make_async_copy(
            state_hbm.at[pl.ds(c * PAIR * ROWS, PAIR * ROWS)],
            state_ref.at[pl.ds(c * PAIR * ROWS, PAIR * ROWS)],
            state_sem.at[c],
        )
        for c in range(CHUNKS)
    ]
    table_load = pltpu.make_async_copy(table_hbm, table_ref, table_sem)
    for load in state_loads + [table_load] + loads:
        load.start()

    barrier = pltpu.get_barrier_semaphore()
    for d in range(1, WAVES):
        pl.semaphore_signal(
            barrier, inc=1, device_id={"wave": (me + d) % WAVES}, device_id_type=MESH
        )
    for mate in (z_mate, x_mate, far_inner):
        pl.semaphore_signal(barrier, inc=1, device_id={"member": mate}, device_id_type=MESH)

    @pl.when(inner)
    def _():
        pl.semaphore_signal(barrier, inc=1, device_id={"member": far_outer}, device_id_type=MESH)

    for c in range(CHUNKS):
        state_loads[c].wait()
        for m in range(c * PAIR, (c + 1) * PAIR):
            for group in range(4):
                for early in range(2):
                    first = m * SET_ROWS + group * WAVES
                    source = m * ROWS + group * levels + (1 - early) * WAVES
                    set_ref[1 - early, first : first + WAVES] = state_ref[source : source + WAVES]
        for g in range(c * 2, c * 2 + 2):
            pools[g][here] = set_ref[0, g * ROWS : (g + 1) * ROWS].astype(bf16)

    @pl.when(inner)
    def _():
        pl.semaphore_wait(barrier, 7)

    @pl.when(jnp.logical_not(inner))
    def _():
        pl.semaphore_wait(barrier, 6)

    def member_copy(source, target, to, send_sem, recv_sem):
        return pltpu.make_async_remote_copy(
            src_ref=source, dst_ref=target, send_sem=send_sem, recv_sem=recv_sem,
            device_id={"member": to}, device_id_type=MESH,
        )

    def pass_copy(c, kind):
        block = pools[c].at[z_here if kind == 2 else here]
        return member_copy(
            block, block, z_mate if kind == 0 else x_mate, pass_send.at[kind, c], pass_recv.at[kind, c]
        )

    def cross_copy(c, far):
        return member_copy(
            cross.at[c, far],
            crossed.at[c],
            far_outer if far else far_inner,
            cross_send.at[far, c],
            cross_recv.at[c],
        )

    def half_index(member_slot):
        return jnp.clip(sources_ref[member_slot] - half * 4, 0, 3)

    inner_pick = half_index(far_inner)
    outer_pick = half_index(far_outer)
    origin = sources_ref[slot] - half * 4
    near = (origin >= 0) & (origin < 4)
    choice = jnp.clip(origin, 0, 3)

    def begin_pass(c):
        pass_copy(c, 0).start()
        if c % STEPS < 2:
            pass_copy(c, 1).start()

    for c in range(STEPS):
        begin_pass(c)

    def forward_pass(c):
        pass_copy(c, 0).wait_recv()
        pass_copy(c, 2).start()
        if c % STEPS + 2 < STEPS:
            pass_copy(c + 2, 1).start()

    def send_across(c):
        pass_copy(c, 1).wait_recv()
        pass_copy(c, 2).wait_recv()

        @pl.when(inner)
        def _():
            cross[c, 1] = pools[c][outer_pick]
            cross_copy(c, 1).start()
            cross[c, 0] = pools[c][inner_pick]
            cross_copy(c, 0).start()

    def wave_copy(source, target, h, c, d, send_sem, recv_sem):
        to = (me + d) % WAVES
        return pltpu.make_async_remote_copy(
            src_ref=source.at[h, pl.ds(pl.multiple_of(to * OWNED_ROWS + c * PART_ROWS, PART_ROWS), PART_ROWS)],
            dst_ref=target.at[h, pl.ds(pl.multiple_of(me * OWNED_ROWS + c * PART_ROWS, PART_ROWS), PART_ROWS)],
            send_sem=send_sem.at[h, d - 1, c],
            recv_sem=recv_sem.at[h, d - 1, c],
            device_id={"wave": to},
            device_id_type=MESH,
        )

    def low_copy(d):
        return pltpu.make_async_remote_copy(
            src_ref=low_sent,
            dst_ref=low_held.at[pl.ds(pl.multiple_of(me * 16, 16), 16)],
            send_sem=score_send.at[d - 1],
            recv_sem=score_recv.at[d - 1],
            device_id={"wave": (me + d) % WAVES},
            device_id_type=MESH,
        )

    my_rows = me * OWNED_ROWS
    mine = pl.ds(pl.multiple_of(my_rows, OWNED_ROWS), OWNED_ROWS)
    columns = fourier_columns = table_ref.shape[1] - 4 * 128

    def go_copy(h, c, d):
        return wave_copy(sent, held, h, c, d, go_send, go_recv)

    def ret_copy(h, c, d):
        return wave_copy(back_sent, back, h, c, d, ret_send, ret_recv)

    def transform(h, c):
        parts = []
        for m in range(c * PAIR, (c + 1) * PAIR):
            rows = slice(m * SET_ROWS, (m + 1) * SET_ROWS)
            if h == 1:
                loads[m].wait()
                block = set_ref[1, rows].astype(bf16)
            else:
                block = chosen[rows]
            part = jnp.dot(block, leg[m], preferred_element_type=f32)
            parts.append(part)
            if h == 1:
                for real in range(2):
                    row = (real + 1) * (SET_ROWS // 2) - 1
                    low_ref[m * 2 + real : m * 2 + real + 1] = part[row : row + 1]
        coef = jnp.concatenate(parts, axis=0).astype(bf16)
        forward = table_ref[:, columns + 256 : columns + 256 + CHUNK_ROWS]
        ordered = jnp.dot(forward, coef, preferred_element_type=f32).astype(bf16)
        for w in range(WAVES):
            first = w * OWNED_ROWS + c * PART_ROWS
            sent[h, first : first + PART_ROWS] = ordered[w * PART_ROWS : (w + 1) * PART_ROWS]
        for d in (2, 1, 3):
            go_copy(h, c, d).start()

    def take_source(g):
        cross_copy(g, 0).wait_recv()
        return jnp.where(near, pools[g][choice], crossed[g])

    table_load.wait()
    transform(1, 0)
    forward_pass(0)
    transform(1, 1)
    low_sent[...] = low_ref[...].astype(bf16)
    low_held[pl.ds(pl.multiple_of(me * 16, 16), 16)] = low_sent[...]
    for d in range(1, WAVES):
        low_copy(d).start()
    held[1, mine] = sent[1, mine]
    forward_pass(1)
    forward_pass(2)
    send_across(0)

    coef_rows = 4 * waves_total
    owner_of = lax.broadcasted_iota(jnp.int32, (2 * waves_total, coef_rows), 0)
    column = lax.broadcasted_iota(jnp.int32, (2 * waves_total, coef_rows), 1)
    widen = jnp.where(column // 2 == owner_of, 1.0, 0.0).astype(bf16)
    tall_owner = lax.broadcasted_iota(jnp.int32, (coef_rows, 2 * waves_total), 1)
    tall_row = lax.broadcasted_iota(jnp.int32, (coef_rows, 2 * waves_total), 0)
    lengthen = jnp.where(tall_row // 2 == tall_owner, 1.0, 0.0).astype(bf16)
    synth_column = lax.broadcasted_iota(jnp.int32, (points, coef_rows), 1) % 2
    analysis_row = lax.broadcasted_iota(jnp.int32, (coef_rows, points), 0) % 2
    for part in range(2):
        waves = table_ref[:, columns + part * 128 : columns + part * 128 + points]
        wide = lax.dot_general(
            waves, widen, (((0,), (0,)), ((), ())), preferred_element_type=f32
        )
        tall = jnp.dot(lengthen, waves, preferred_element_type=f32)
        for f in range(2):
            at = slice(f * points, (f + 1) * points)
            synth_ref[at, part * coef_rows : (part + 1) * coef_rows] = jnp.where(
                synth_column == f, wide, 0.0
            ).astype(bf16)
            analysis_ref[part, :, at] = jnp.where(analysis_row == f, tall, 0.0).astype(bf16)
    forward_pass(3)
    send_across(1)

    low, high = region_ref[2], region_ref[3]
    lon = lax.broadcasted_iota(jnp.int32, (1, fourier_columns), 1)
    lon_inside = jnp.where((lon >= low) & (lon < high), 1.0, 0.0)
    fourier = table_ref[:, :fourier_columns]
    gram = lax.dot_general(
        (fourier.astype(f32) * lon_inside).astype(bf16),
        fourier,
        (((1,), (1,)), ((), ())),
        preferred_element_type=f32,
    )
    gram_high = gram.astype(bf16)
    gram_low = (gram - gram_high.astype(f32)).astype(bf16)
    lat = lax.broadcasted_iota(jnp.int32, (1, lat_count), 1)
    weights = weights_ref[...].reshape(1, lat_count)
    region_weights = jnp.where((lat >= region_ref[0]) & (lat < region_ref[1]), weights, 0.0)
    weight_sum = jnp.sum(region_weights, axis=1, keepdims=True) * (high - low).astype(f32)

    send_across(2)
    scaled = weights * (scale * scale)

    def grid_phase(h):
        for c in range(CHUNKS):
            for d in (2, 1, 3):
                go_copy(h, c, d).wait_recv()
        coefs = held[h]
        grid = jnp.dot(
            synth_ref[...], jnp.concatenate([coefs, coefs], axis=0), preferred_element_type=f32
        )
        wind = grid[:points]
        weighted = wind * scaled
        flux[h, :points] = (0.5 * weighted * wind).astype(bf16)
        flux[h, points:] = (weighted * grid[points:]).astype(bf16)
        fluxes = flux[h]
        back_sent[h] = (
            analysis_scale
            * (
                jnp.dot(analysis_ref[0], fluxes, preferred_element_type=f32)
                + jnp.dot(analysis_ref[1], fluxes, preferred_element_type=f32)
            )
        ).astype(bf16)
        for c in range(CHUNKS):
            for d in (2, 1, 3):
                ret_copy(h, c, d).start()
        back[h, mine] = back_sent[h, mine]

    grid_phase(1)
    send_across(3)

    def transform_sources(c):
        for g in range(c * 2, c * 2 + 2):
            chosen[g * ROWS : (g + 1) * ROWS] = take_source(g)
        transform(0, c)

    transform_sources(0)

    for d in range(1, WAVES):
        low_copy(d).wait()
    lowest = low_held[...]
    spread = jnp.dot(gram_high, lowest, preferred_element_type=f32) + jnp.dot(
        gram_low, lowest, preferred_element_type=f32
    )
    squares = jnp.sum(lowest.astype(f32) * spread, axis=0, keepdims=True) * (
        region_weights * (scale * scale)
    )
    score = jnp.sum(squares, axis=1, keepdims=True) / weight_sum
    score_ref[...] = jnp.broadcast_to(score, score_ref.shape)

    degree = lax.broadcasted_iota(jnp.int32, (1, degrees), 1).astype(f32)
    keep = 1.0 / (1.0 + ((degree + 1.0) / degrees) ** 2)
    backward = table_ref[:, columns + 384 : columns + 384 + CHUNK_ROWS]
    def tendencies(h, c):
        for d in (2, 1, 3):
            ret_copy(h, c, d).wait_recv()
        arrived = jnp.concatenate(
            [
                back[h, w * OWNED_ROWS + c * PART_ROWS : w * OWNED_ROWS + (c + 1) * PART_ROWS]
                for w in range(WAVES)
            ],
            axis=0,
        )
        plain = jnp.dot(backward, arrived, preferred_element_type=f32).astype(bf16)
        for i in range(PAIR):
            m = c * PAIR + i
            rows = slice(m * SET_ROWS, (m + 1) * SET_ROWS)
            tendency = lax.dot_general(
                plain[i * SET_ROWS : (i + 1) * SET_ROWS],
                leg[m],
                (((1,), (1,)), ((), ())),
                preferred_element_type=f32,
            )
            wave_id = (me * LOCAL_WAVES + m).astype(f32)
            advection = wave_id * (advect_rate / waves_total)
            source = set_ref[1, rows] if h == 1 else chosen[rows].astype(f32)
            stepped = (source + advection * tendency) * keep
            if h == 1:
                g = STEPS + m // 2
                pools[g][here, (m % 2) * SET_ROWS : (m % 2 + 1) * SET_ROWS] = stepped.astype(bf16)
                if m % 2 == 1:
                    begin_pass(g)
            else:
                put_rows(m, 0, stepped)

    def put_rows(m, late, values):
        for group in range(4):
            first = m * ROWS + group * levels + late * WAVES
            out_ref[first : first + WAVES] = values[group * WAVES : (group + 1) * WAVES]

    def put_cloned(g):
        block = take_source(g).astype(f32)
        for i in range(2):
            put_rows((g - STEPS) * 2 + i, 1, block[i * SET_ROWS : (i + 1) * SET_ROWS])

    tendencies(1, 0)
    tendencies(1, 1)
    forward_pass(STEPS)
    forward_pass(STEPS + 1)
    transform_sources(1)
    held[0, mine] = sent[0, mine]
    forward_pass(STEPS + 2)
    forward_pass(STEPS + 3)
    send_across(STEPS)
    send_across(STEPS + 1)
    grid_phase(0)
    send_across(STEPS + 2)
    send_across(STEPS + 3)
    tendencies(0, 0)
    put_cloned(STEPS)
    put_cloned(STEPS + 1)
    tendencies(0, 1)
    put_cloned(STEPS + 2)
    put_cloned(STEPS + 3)

    for h in range(2):
        for c in range(CHUNKS):
            for d in (2, 1, 3):
                go_copy(h, c, d).wait_send()
                ret_copy(h, c, d).wait_send()
    for c in range(2 * STEPS):
        for kind in range(3):
            pass_copy(c, kind).wait_send()

    @pl.when(inner)
    def _():
        for c in range(2 * STEPS):
            for far in range(2):
                cross_copy(c, far).wait_send()


def in_one_kernel(state, legendre, lat_weights, region, sources):
    waves_local, degrees, latitudes = legendre.shape
    waves_total = waves_local * WAVES
    points = quadrature_points(waves_total)
    table_high, table_low = split_table(wave_table(waves_total, points))
    fourier = wave_table(waves_total, NLON).astype(jnp.bfloat16)
    forward, backward = order_tables()
    unused = np.zeros((CHUNK_ROWS, 128 - CHUNK_ROWS), jnp.bfloat16)
    flat = [t.reshape(2 * waves_total, -1) for t in (fourier, table_high, table_low)]
    table = np.concatenate(flat + [forward, unused, backward, unused], axis=1)
    vmem = pl.BlockSpec(memory_space=pltpu.VMEM)
    smem = pl.BlockSpec(memory_space=pltpu.SMEM)
    hbm = pl.BlockSpec(memory_space=pl.ANY)
    rows = waves_local * ROWS
    block = (rows, degrees)
    grid_rows = (2, 4 * waves_total, latitudes)
    dma = pltpu.SemaphoreType.DMA
    bf16 = jnp.bfloat16
    stepped, scores = pl.pallas_call(
        functools.partial(
            step_kernel,
            scale=(2.0 * waves_total) ** -0.5,
            analysis_scale=NLON**-0.5 * (NLON / points),
            waves_total=waves_total,
            points=points,
        ),
        out_shape=(
            jax.ShapeDtypeStruct(block, jnp.float32),
            jax.ShapeDtypeStruct((8, 128), jnp.float32),
        ),
        in_specs=[hbm, hbm, vmem, smem, smem, hbm],
        out_specs=(vmem, vmem),
        scratch_shapes=[
            pltpu.VMEM(block, jnp.float32),
            pltpu.VMEM((2, rows // 2, degrees), jnp.float32),
            pltpu.VMEM(table.shape, bf16),
            pltpu.VMEM((2 * points, 8 * waves_total), bf16),
            pltpu.VMEM((2, 4 * waves_total, 2 * points), bf16),
            pltpu.VMEM((2 * waves_local, latitudes), jnp.float32),
            pltpu.VMEM((2 * waves_local, latitudes), bf16),
            pltpu.VMEM((2 * waves_total, latitudes), bf16),
            pltpu.VMEM((rows // 2, degrees), bf16),
            pltpu.VMEM(legendre.shape, bf16),
            pltpu.VMEM(grid_rows, bf16),
            pltpu.VMEM(grid_rows, bf16),
            pltpu.VMEM((2, 2 * points, latitudes), bf16),
            pltpu.VMEM(grid_rows, bf16),
            pltpu.VMEM(grid_rows, bf16),
            pltpu.VMEM((2 * STEPS, 2, ROWS, degrees), bf16),
            pltpu.VMEM((2 * STEPS, ROWS, degrees), bf16),
        ]
        + [pltpu.VMEM((4, ROWS, degrees), bf16)] * (2 * STEPS)
        + [
            dma((CHUNKS,)),
            dma,
            dma((LOCAL_WAVES,)),
            dma((2, WAVES - 1, CHUNKS)),
            dma((2, WAVES - 1, CHUNKS)),
            dma((2, WAVES - 1, CHUNKS)),
            dma((2, WAVES - 1, CHUNKS)),
            dma((WAVES - 1,)),
            dma((WAVES - 1,)),
            dma((3, 2 * STEPS)),
            dma((3, 2 * STEPS)),
            dma((2, 2 * STEPS)),
            dma((2 * STEPS,)),
        ],
        compiler_params=pltpu.CompilerParams(
            collective_id=0, has_side_effects=True, vmem_limit_bytes=56 * 1024 * 1024
        ),
    )(state.reshape(block), legendre, lat_weights, region, sources, jnp.asarray(table))
    return (stepped.reshape(state.shape), scores[0, :1])


def solution(mesh):
    in_specs = (P("member", "wave", None, None), P("wave", None, None), P(), P(), P())
    out_specs = (P("member", "wave", None, None), P("member"))

    def run(state, legendre, lat_weights, region, sources):
        shape = (state.shape[1] // mesh.shape["wave"], state.shape[2], state.shape[3], legendre.shape[2])
        fits = mesh.shape["wave"] == 4 and mesh.shape["member"] == 8 and shape == (8, 32, 640, 640)
        return jax.shard_map(
            in_one_kernel if fits else on_device,
            mesh=mesh,
            in_specs=in_specs,
            out_specs=out_specs,
            check_vma=False,
        )(state, legendre, lat_weights, region, sources)

    return run
```

```python
import functools

import jax
import jax.numpy as jnp
import numpy as np
from jax import lax
from jax.experimental import pallas as pl
from jax.experimental.pallas import tpu as pltpu
from jax.sharding import PartitionSpec as P

NLON = 2560


advect_rate = 2.0


def wave_table(waves_total, points):
    wave_index = np.arange(waves_total)[:, None]
    angles = (wave_index * np.arange(points)[None, :] % points) * (2.0 * np.pi / points)
    return np.stack([np.cos(angles), -np.sin(angles)], axis=1)


def split_table(table):
    high = table.astype(jnp.bfloat16)
    low = (table - high.astype(np.float64)).astype(jnp.bfloat16)
    return high, low


def quadrature_points(waves_total):
    return (3 * (waves_total - 1)) // 128 * 128 + 128


def on_device(state, legendre, lat_weights, region, sources):
    wave_count = lax.axis_size("wave")
    waves_local = legendre.shape[0]
    waves_total = waves_local * wave_count
    degrees = legendre.shape[1]
    latitudes = legendre.shape[2]
    lat_rows = latitudes // wave_count
    state_rows = state.shape[2]
    level_count = state_rows // 4
    points = quadrature_points(waves_total)
    table_high, table_low = split_table(wave_table(waves_total, points))
    spectral = state[0]
    fourier_coef = jnp.einsum(
        "mrn,mnl->mrl", spectral.astype(jnp.bfloat16), legendre, preferred_element_type=jnp.float32
    )
    fourier_coef = fourier_coef.astype(jnp.bfloat16).reshape(
        waves_local, 2, 2 * level_count, latitudes
    )
    synthesis_scale = (2.0 * waves_total) ** (-0.5)
    coef = lax.all_to_all(fourier_coef, "wave", split_axis=3, concat_axis=0, tiled=True)
    gridded = synthesis_scale * jnp.einsum(
        "mckl,mcx->klx",
        jnp.concatenate([coef, coef], axis=1),
        jnp.concatenate([table_high, table_low], axis=1),
        preferred_element_type=jnp.float32,
    )
    lat_start = lax.axis_index("wave") * lat_rows
    local_weights = lax.dynamic_slice_in_dim(lat_weights, lat_start, lat_rows)
    wind_grid = gridded[:level_count]
    temper_grid = gridded[level_count:]
    fluxes = (
        jnp.concatenate([0.5 * wind_grid * wind_grid, wind_grid * temper_grid], axis=0)
        * local_weights[None, :, None]
    )
    fluxes = fluxes.astype(jnp.bfloat16)
    fourier = wave_table(waves_total, NLON).reshape(2 * waves_total, NLON).astype(jnp.bfloat16)
    lon_index = lax.broadcasted_iota(jnp.int32, (1, NLON), 1)
    lon_inside = (lon_index >= region[2]) & (lon_index < region[3])
    gram = jnp.einsum(
        "px,qx->pq",
        jnp.where(lon_inside, fourier, jnp.zeros((), jnp.bfloat16)),
        fourier,
        preferred_element_type=jnp.float32,
    )
    lowest = coef[:, :, -1].reshape(2 * waves_total, lat_rows).astype(jnp.float32)
    gram_lowest = jnp.dot(gram, lowest, precision=lax.Precision.HIGHEST)
    lat_index = lat_start + lax.broadcasted_iota(jnp.int32, (lat_rows,), 0)
    in_band = (lat_index >= region[0]) & (lat_index < region[1])
    region_part = jnp.sum(
        jnp.where(in_band, local_weights, 0.0)[None, :] * lowest * gram_lowest
    ) / (2.0 * waves_total)
    region_total = lax.psum(region_part, "wave")
    every_lat = lax.broadcasted_iota(jnp.int32, (latitudes,), 0)
    lat_inside = (every_lat >= region[0]) & (every_lat < region[1])
    region_weight = jnp.sum(jnp.where(lat_inside, lat_weights, 0.0)) * (
        region[3] - region[2]
    ).astype(jnp.float32)
    scores = (region_total / region_weight).reshape(1)
    analysis_scale = NLON ** (-0.5) * (NLON / points)
    flux_high = jnp.einsum("klx,mcx->mckl", fluxes, table_high, preferred_element_type=jnp.float32)
    flux_low = jnp.einsum("klx,mcx->mckl", fluxes, table_low, preferred_element_type=jnp.float32)
    flux_coef = (analysis_scale * (flux_high + flux_low)).astype(jnp.bfloat16)
    tendency = jnp.einsum(
        "mckl,mnl->mckn",
        lax.all_to_all(flux_coef, "wave", split_axis=0, concat_axis=3, tiled=True),
        legendre,
        preferred_element_type=jnp.float32,
    )
    wave_ids = lax.axis_index("wave") * waves_local + lax.broadcasted_iota(
        jnp.int32, (waves_local, 1, 1), 0
    )
    advection = advect_rate * wave_ids.astype(jnp.float32) / waves_total
    degree_ids = lax.broadcasted_iota(jnp.int32, (1, 1, degrees), 2).astype(jnp.float32)
    damping = 1.0 + ((degree_ids + 1.0) / degrees) ** 2
    spectral_split = spectral.reshape(waves_local, 2, 2 * level_count, degrees)
    real_part = (spectral_split[:, 0] + advection * tendency[:, 1]) / damping
    imag_part = (spectral_split[:, 1] - advection * tendency[:, 0]) / damping
    stepped = jnp.stack([real_part, imag_part], axis=1).reshape(1, waves_local, state_rows, degrees)
    source_member = sources[lax.axis_index("member")]
    shards = lax.all_gather(stepped.astype(jnp.bfloat16), "member", axis=0, tiled=True)
    cloned = lax.dynamic_slice_in_dim(shards, source_member, 1, axis=0).astype(jnp.float32)
    return (cloned, scores)


MESH = pl.DeviceIdType.MESH
WAVES = 4
CHUNKS = 2
PAIR = 4
ROWS = 32
SET_ROWS = ROWS // 2
LOCAL_WAVES = CHUNKS * PAIR
CHUNK_ROWS = PAIR * SET_ROWS
PART_ROWS = CHUNK_ROWS // WAVES
OWNED_ROWS = CHUNKS * PART_ROWS
STEPS = 4


def order_tables():
    forward = np.zeros((CHUNK_ROWS, CHUNK_ROWS))
    backward = np.zeros((CHUNK_ROWS, CHUNK_ROWS))
    for m in range(PAIR):
        for c in range(2):
            for f in range(2):
                for k in range(WAVES):
                    plain = ((m * 2 + c) * 2 + f) * WAVES + k
                    forward[((k * PAIR + m) * 2 + c) * 2 + f, plain] = 1.0
                    backward[plain, ((k * PAIR + m) * 2 + 1 - c) * 2 + f] = 1.0 - 2.0 * c
    return forward.astype(jnp.bfloat16), backward.astype(jnp.bfloat16)


def step_kernel(
    state_hbm, legendre_ref, weights_ref, region_ref, sources_ref, table_hbm,
    out_ref, score_ref,
    state_ref, set_ref, table_ref, synth_ref, analysis_ref, low_ref, low_sent, low_held,
    chosen, leg, sent, held, flux, back_sent, back, cross, crossed,
    *rest, scale, analysis_scale, waves_total, points,
):
    pools = rest[: 2 * STEPS]
    (
        state_sem, table_sem, leg_sem, go_send, go_recv, ret_send, ret_recv, score_send, score_recv,
        pass_send, pass_recv, cross_send, cross_recv,
    ) = rest[2 * STEPS :]
    me = lax.axis_index("wave")
    slot = lax.axis_index("member")
    z = slot // 2
    x = slot % 2
    half = z // 2
    inner = z % 2 != half % 2
    z_mate = (z + 1 - 2 * (z % 2)) * 2 + x
    x_mate = z * 2 + 1 - x
    far_inner = (2 - half) * 2 + x
    far_outer = (3 - 3 * half) * 2 + x
    here = slot - half * 4
    z_here = z_mate - half * 4
    degrees = state_ref.shape[1]
    lat_count = weights_ref.shape[0]
    f32 = jnp.float32
    bf16 = jnp.bfloat16
    levels = ROWS // 4

    loads = [
        pltpu.make_async_copy(legendre_ref.at[m], leg.at[m], leg_sem.at[m]) for m in range(LOCAL_WAVES)
    ]
    state_loads = [
        pltpu.make_async_copy(
            state_hbm.at[pl.ds(c * PAIR * ROWS, PAIR * ROWS)],
            state_ref.at[pl.ds(c * PAIR * ROWS, PAIR * ROWS)],
            state_sem.at[c],
        )
        for c in range(CHUNKS)
    ]
    table_load = pltpu.make_async_copy(table_hbm, table_ref, table_sem)
    for load in state_loads + [table_load] + loads:
        load.start()

    barrier = pltpu.get_barrier_semaphore()
    for d in range(1, WAVES):
        pl.semaphore_signal(
            barrier, inc=1, device_id={"wave": (me + d) % WAVES}, device_id_type=MESH
        )
    for mate in (z_mate, x_mate, far_inner):
        pl.semaphore_signal(barrier, inc=1, device_id={"member": mate}, device_id_type=MESH)

    @pl.when(inner)
    def _():
        pl.semaphore_signal(barrier, inc=1, device_id={"member": far_outer}, device_id_type=MESH)

    for c in range(CHUNKS):
        state_loads[c].wait()
        for m in range(c * PAIR, (c + 1) * PAIR):
            for group in range(4):
                for early in range(2):
                    first = m * SET_ROWS + group * WAVES
                    source = m * ROWS + group * levels + (1 - early) * WAVES
                    set_ref[1 - early, first : first + WAVES] = state_ref[source : source + WAVES]
        for g in range(c * 2, c * 2 + 2):
            pools[g][here] = set_ref[0, g * ROWS : (g + 1) * ROWS].astype(bf16)

    @pl.when(inner)
    def _():
        pl.semaphore_wait(barrier, 7)

    @pl.when(jnp.logical_not(inner))
    def _():
        pl.semaphore_wait(barrier, 6)

    def member_copy(source, target, to, send_sem, recv_sem):
        return pltpu.make_async_remote_copy(
            src_ref=source, dst_ref=target, send_sem=send_sem, recv_sem=recv_sem,
            device_id={"member": to}, device_id_type=MESH,
        )

    def pass_copy(c, kind):
        block = pools[c].at[z_here if kind == 2 else here]
        return member_copy(
            block, block, z_mate if kind == 0 else x_mate, pass_send.at[kind, c], pass_recv.at[kind, c]
        )

    def cross_copy(c, far):
        return member_copy(
            cross.at[c, far],
            crossed.at[c],
            far_outer if far else far_inner,
            cross_send.at[far, c],
            cross_recv.at[c],
        )

    def half_index(member_slot):
        return jnp.clip(sources_ref[member_slot] - half * 4, 0, 3)

    inner_pick = half_index(far_inner)
    outer_pick = half_index(far_outer)
    origin = sources_ref[slot] - half * 4
    near = (origin >= 0) & (origin < 4)
    choice = jnp.clip(origin, 0, 3)

    def begin_pass(c):
        pass_copy(c, 0).start()
        if c % STEPS < 2:
            pass_copy(c, 1).start()

    for c in range(STEPS):
        begin_pass(c)

    def forward_pass(c):
        pass_copy(c, 0).wait_recv()
        pass_copy(c, 2).start()
        if c % STEPS + 2 < STEPS:
            pass_copy(c + 2, 1).start()

    def send_across(c):
        pass_copy(c, 1).wait_recv()
        pass_copy(c, 2).wait_recv()

        @pl.when(inner)
        def _():
            cross[c, 1] = pools[c][outer_pick]
            cross_copy(c, 1).start()
            cross[c, 0] = pools[c][inner_pick]
            cross_copy(c, 0).start()

    def wave_copy(source, target, h, c, d, send_sem, recv_sem):
        to = (me + d) % WAVES
        return pltpu.make_async_remote_copy(
            src_ref=source.at[h, pl.ds(pl.multiple_of(to * OWNED_ROWS + c * PART_ROWS, PART_ROWS), PART_ROWS)],
            dst_ref=target.at[h, pl.ds(pl.multiple_of(me * OWNED_ROWS + c * PART_ROWS, PART_ROWS), PART_ROWS)],
            send_sem=send_sem.at[h, d - 1, c],
            recv_sem=recv_sem.at[h, d - 1, c],
            device_id={"wave": to},
            device_id_type=MESH,
        )

    def low_copy(d):
        return pltpu.make_async_remote_copy(
            src_ref=low_sent,
            dst_ref=low_held.at[pl.ds(pl.multiple_of(me * 16, 16), 16)],
            send_sem=score_send.at[d - 1],
            recv_sem=score_recv.at[d - 1],
            device_id={"wave": (me + d) % WAVES},
            device_id_type=MESH,
        )

    my_rows = me * OWNED_ROWS
    mine = pl.ds(pl.multiple_of(my_rows, OWNED_ROWS), OWNED_ROWS)
    columns = fourier_columns = table_ref.shape[1] - 4 * 128

    def go_copy(h, c, d):
        return wave_copy(sent, held, h, c, d, go_send, go_recv)

    def ret_copy(h, c, d):
        return wave_copy(back_sent, back, h, c, d, ret_send, ret_recv)

    def transform(h, c):
        parts = []
        for m in range(c * PAIR, (c + 1) * PAIR):
            rows = slice(m * SET_ROWS, (m + 1) * SET_ROWS)
            if h == 1:
                loads[m].wait()
                block = set_ref[1, rows].astype(bf16)
            else:
                block = chosen[rows]
            part = jnp.dot(block, leg[m], preferred_element_type=f32)
            parts.append(part)
            if h == 1:
                for real in range(2):
                    row = (real + 1) * (SET_ROWS // 2) - 1
                    low_ref[m * 2 + real : m * 2 + real + 1] = part[row : row + 1]
        coef = jnp.concatenate(parts, axis=0).astype(bf16)
        forward = table_ref[:, columns + 256 : columns + 256 + CHUNK_ROWS]
        ordered = jnp.dot(forward, coef, preferred_element_type=f32).astype(bf16)
        for w in range(WAVES):
            first = w * OWNED_ROWS + c * PART_ROWS
            sent[h, first : first + PART_ROWS] = ordered[w * PART_ROWS : (w + 1) * PART_ROWS]
        for d in (2, 1, 3):
            go_copy(h, c, d).start()

    def take_source(g):
        cross_copy(g, 0).wait_recv()
        return jnp.where(near, pools[g][choice], crossed[g])

    table_load.wait()
    transform(1, 0)
    forward_pass(0)
    transform(1, 1)
    low_sent[...] = low_ref[...].astype(bf16)
    low_held[pl.ds(pl.multiple_of(me * 16, 16), 16)] = low_sent[...]
    for d in range(1, WAVES):
        low_copy(d).start()
    held[1, mine] = sent[1, mine]
    forward_pass(1)
    forward_pass(2)
    send_across(0)

    coef_rows = 4 * waves_total
    owner_of = lax.broadcasted_iota(jnp.int32, (2 * waves_total, coef_rows), 0)
    column = lax.broadcasted_iota(jnp.int32, (2 * waves_total, coef_rows), 1)
    widen = jnp.where(column // 2 == owner_of, 1.0, 0.0).astype(bf16)
    tall_owner = lax.broadcasted_iota(jnp.int32, (coef_rows, 2 * waves_total), 1)
    tall_row = lax.broadcasted_iota(jnp.int32, (coef_rows, 2 * waves_total), 0)
    lengthen = jnp.where(tall_row // 2 == tall_owner, 1.0, 0.0).astype(bf16)
    synth_column = lax.broadcasted_iota(jnp.int32, (points, coef_rows), 1) % 2
    analysis_row = lax.broadcasted_iota(jnp.int32, (coef_rows, points), 0) % 2
    for part in range(2):
        waves = table_ref[:, columns + part * 128 : columns + part * 128 + points]
        wide = lax.dot_general(
            waves, widen, (((0,), (0,)), ((), ())), preferred_element_type=f32
        )
        tall = jnp.dot(lengthen, waves, preferred_element_type=f32)
        for f in range(2):
            at = slice(f * points, (f + 1) * points)
            synth_ref[at, part * coef_rows : (part + 1) * coef_rows] = jnp.where(
                synth_column == f, wide, 0.0
            ).astype(bf16)
            analysis_ref[part, :, at] = jnp.where(analysis_row == f, tall, 0.0).astype(bf16)
    forward_pass(3)
    send_across(1)

    low, high = region_ref[2], region_ref[3]
    lon = lax.broadcasted_iota(jnp.int32, (1, fourier_columns), 1)
    lon_inside = jnp.where((lon >= low) & (lon < high), 1.0, 0.0)
    fourier = table_ref[:, :fourier_columns]
    gram = lax.dot_general(
        (fourier.astype(f32) * lon_inside).astype(bf16),
        fourier,
        (((1,), (1,)), ((), ())),
        preferred_element_type=f32,
    )
    gram_high = gram.astype(bf16)
    gram_low = (gram - gram_high.astype(f32)).astype(bf16)
    lat = lax.broadcasted_iota(jnp.int32, (1, lat_count), 1)
    weights = weights_ref[...].reshape(1, lat_count)
    region_weights = jnp.where((lat >= region_ref[0]) & (lat < region_ref[1]), weights, 0.0)
    weight_sum = jnp.sum(region_weights, axis=1, keepdims=True) * (high - low).astype(f32)

    send_across(2)
    scaled = weights * (scale * scale)

    def grid_phase(h):
        for c in range(CHUNKS):
            for d in (2, 1, 3):
                go_copy(h, c, d).wait_recv()
        coefs = held[h]
        grid = jnp.dot(
            synth_ref[...], jnp.concatenate([coefs, coefs], axis=0), preferred_element_type=f32
        )
        wind = grid[:points]
        weighted = wind * scaled
        flux[h, :points] = (0.5 * weighted * wind).astype(bf16)
        flux[h, points:] = (weighted * grid[points:]).astype(bf16)
        fluxes = flux[h]
        back_sent[h] = (
            analysis_scale
            * (
                jnp.dot(analysis_ref[0], fluxes, preferred_element_type=f32)
                + jnp.dot(analysis_ref[1], fluxes, preferred_element_type=f32)
            )
        ).astype(bf16)
        for c in range(CHUNKS):
            for d in (2, 1, 3):
                ret_copy(h, c, d).start()
        back[h, mine] = back_sent[h, mine]

    grid_phase(1)
    send_across(3)

    def transform_sources(c):
        for g in range(c * 2, c * 2 + 2):
            chosen[g * ROWS : (g + 1) * ROWS] = take_source(g)
        transform(0, c)

    transform_sources(0)

    for d in range(1, WAVES):
        low_copy(d).wait()
    lowest = low_held[...]
    spread = jnp.dot(gram_high, lowest, preferred_element_type=f32) + jnp.dot(
        gram_low, lowest, preferred_element_type=f32
    )
    squares = jnp.sum(lowest.astype(f32) * spread, axis=0, keepdims=True) * (
        region_weights * (scale * scale)
    )
    score = jnp.sum(squares, axis=1, keepdims=True) / weight_sum
    score_ref[...] = jnp.broadcast_to(score, score_ref.shape)

    degree = lax.broadcasted_iota(jnp.int32, (1, degrees), 1).astype(f32)
    keep = 1.0 / (1.0 + ((degree + 1.0) / degrees) ** 2)
    backward = table_ref[:, columns + 384 : columns + 384 + CHUNK_ROWS]
    lane_wave = lax.broadcasted_iota(jnp.int32, (degrees, 2 * CHUNK_ROWS), 1) % CHUNK_ROWS // SET_ROWS

    def tendencies(h, c):
        for d in (2, 1, 3):
            ret_copy(h, c, d).wait_recv()
        arrived = jnp.concatenate(
            [
                back[h, w * OWNED_ROWS + c * PART_ROWS : w * OWNED_ROWS + (c + 1) * PART_ROWS]
                for w in range(WAVES)
            ],
            axis=0,
        )
        plain = jnp.dot(backward, arrived, preferred_element_type=f32).astype(bf16)
        twice = jnp.concatenate([plain, plain], axis=0)
        for i in range(PAIR):
            product = lax.dot_general(
                leg[c * PAIR + i],
                twice,
                (((1,), (1,)), ((), ())),
                preferred_element_type=f32,
            )
            columns_of = product if i == 0 else jnp.where(lane_wave == i, product, columns_of)
        turned = columns_of.T
        for i in range(PAIR):
            m = c * PAIR + i
            rows = slice(m * SET_ROWS, (m + 1) * SET_ROWS)
            tendency = turned[i * SET_ROWS : (i + 1) * SET_ROWS]
            wave_id = (me * LOCAL_WAVES + m).astype(f32)
            advection = wave_id * (advect_rate / waves_total)
            source = set_ref[1, rows] if h == 1 else chosen[rows].astype(f32)
            stepped = (source + advection * tendency) * keep
            if h == 1:
                g = STEPS + m // 2
                pools[g][here, (m % 2) * SET_ROWS : (m % 2 + 1) * SET_ROWS] = stepped.astype(bf16)
                if m % 2 == 1:
                    begin_pass(g)
            else:
                put_rows(m, 0, stepped)

    def put_rows(m, late, values):
        for group in range(4):
            first = m * ROWS + group * levels + late * WAVES
            out_ref[first : first + WAVES] = values[group * WAVES : (group + 1) * WAVES]

    def put_cloned(g):
        block = take_source(g).astype(f32)
        for i in range(2):
            put_rows((g - STEPS) * 2 + i, 1, block[i * SET_ROWS : (i + 1) * SET_ROWS])

    tendencies(1, 0)
    tendencies(1, 1)
    forward_pass(STEPS)
    forward_pass(STEPS + 1)
    transform_sources(1)
    held[0, mine] = sent[0, mine]
    forward_pass(STEPS + 2)
    forward_pass(STEPS + 3)
    send_across(STEPS)
    send_across(STEPS + 1)
    grid_phase(0)
    send_across(STEPS + 2)
    send_across(STEPS + 3)
    tendencies(0, 0)
    put_cloned(STEPS)
    put_cloned(STEPS + 1)
    tendencies(0, 1)
    put_cloned(STEPS + 2)
    put_cloned(STEPS + 3)

    for h in range(2):
        for c in range(CHUNKS):
            for d in (2, 1, 3):
                go_copy(h, c, d).wait_send()
                ret_copy(h, c, d).wait_send()
    for c in range(2 * STEPS):
        for kind in range(3):
            pass_copy(c, kind).wait_send()

    @pl.when(inner)
    def _():
        for c in range(2 * STEPS):
            for far in range(2):
                cross_copy(c, far).wait_send()


def in_one_kernel(state, legendre, lat_weights, region, sources):
    waves_local, degrees, latitudes = legendre.shape
    waves_total = waves_local * WAVES
    points = quadrature_points(waves_total)
    table_high, table_low = split_table(wave_table(waves_total, points))
    fourier = wave_table(waves_total, NLON).astype(jnp.bfloat16)
    forward, backward = order_tables()
    unused = np.zeros((CHUNK_ROWS, 128 - CHUNK_ROWS), jnp.bfloat16)
    flat = [t.reshape(2 * waves_total, -1) for t in (fourier, table_high, table_low)]
    table = np.concatenate(flat + [forward, unused, backward, unused], axis=1)
    vmem = pl.BlockSpec(memory_space=pltpu.VMEM)
    smem = pl.BlockSpec(memory_space=pltpu.SMEM)
    hbm = pl.BlockSpec(memory_space=pl.ANY)
    rows = waves_local * ROWS
    block = (rows, degrees)
    grid_rows = (2, 4 * waves_total, latitudes)
    dma = pltpu.SemaphoreType.DMA
    bf16 = jnp.bfloat16
    stepped, scores = pl.pallas_call(
        functools.partial(
            step_kernel,
            scale=(2.0 * waves_total) ** -0.5,
            analysis_scale=NLON**-0.5 * (NLON / points),
            waves_total=waves_total,
            points=points,
        ),
        out_shape=(
            jax.ShapeDtypeStruct(block, jnp.float32),
            jax.ShapeDtypeStruct((8, 128), jnp.float32),
        ),
        in_specs=[hbm, hbm, vmem, smem, smem, hbm],
        out_specs=(vmem, vmem),
        scratch_shapes=[
            pltpu.VMEM(block, jnp.float32),
            pltpu.VMEM((2, rows // 2, degrees), jnp.float32),
            pltpu.VMEM(table.shape, bf16),
            pltpu.VMEM((2 * points, 8 * waves_total), bf16),
            pltpu.VMEM((2, 4 * waves_total, 2 * points), bf16),
            pltpu.VMEM((2 * waves_local, latitudes), jnp.float32),
            pltpu.VMEM((2 * waves_local, latitudes), bf16),
            pltpu.VMEM((2 * waves_total, latitudes), bf16),
            pltpu.VMEM((rows // 2, degrees), bf16),
            pltpu.VMEM(legendre.shape, bf16),
            pltpu.VMEM(grid_rows, bf16),
            pltpu.VMEM(grid_rows, bf16),
            pltpu.VMEM((2, 2 * points, latitudes), bf16),
            pltpu.VMEM(grid_rows, bf16),
            pltpu.VMEM(grid_rows, bf16),
            pltpu.VMEM((2 * STEPS, 2, ROWS, degrees), bf16),
            pltpu.VMEM((2 * STEPS, ROWS, degrees), bf16),
        ]
        + [pltpu.VMEM((4, ROWS, degrees), bf16)] * (2 * STEPS)
        + [
            dma((CHUNKS,)),
            dma,
            dma((LOCAL_WAVES,)),
            dma((2, WAVES - 1, CHUNKS)),
            dma((2, WAVES - 1, CHUNKS)),
            dma((2, WAVES - 1, CHUNKS)),
            dma((2, WAVES - 1, CHUNKS)),
            dma((WAVES - 1,)),
            dma((WAVES - 1,)),
            dma((3, 2 * STEPS)),
            dma((3, 2 * STEPS)),
            dma((2, 2 * STEPS)),
            dma((2 * STEPS,)),
        ],
        compiler_params=pltpu.CompilerParams(
            collective_id=0, has_side_effects=True, vmem_limit_bytes=56 * 1024 * 1024
        ),
    )(state.reshape(block), legendre, lat_weights, region, sources, jnp.asarray(table))
    return (stepped.reshape(state.shape), scores[0, :1])


def solution(mesh):
    in_specs = (P("member", "wave", None, None), P("wave", None, None), P(), P(), P())
    out_specs = (P("member", "wave", None, None), P("member"))

    def run(state, legendre, lat_weights, region, sources):
        shape = (state.shape[1] // mesh.shape["wave"], state.shape[2], state.shape[3], legendre.shape[2])
        fits = mesh.shape["wave"] == 4 and mesh.shape["member"] == 8 and shape == (8, 32, 640, 640)
        return jax.shard_map(
            in_one_kernel if fits else on_device,
            mesh=mesh,
            in_specs=in_specs,
            out_specs=out_specs,
            check_vma=False,
        )(state, legendre, lat_weights, region, sources)

    return run
```

```python
import functools

import jax
import jax.numpy as jnp
import numpy as np
from jax import lax
from jax.experimental import pallas as pl
from jax.experimental.pallas import tpu as pltpu
from jax.sharding import PartitionSpec as P

NLON = 2560


advect_rate = 2.0


def wave_table(waves_total, points):
    wave_index = np.arange(waves_total)[:, None]
    angles = (wave_index * np.arange(points)[None, :] % points) * (2.0 * np.pi / points)
    return np.stack([np.cos(angles), -np.sin(angles)], axis=1)


def split_table(table):
    high = table.astype(jnp.bfloat16)
    low = (table - high.astype(np.float64)).astype(jnp.bfloat16)
    return high, low


def quadrature_points(waves_total):
    return (3 * (waves_total - 1)) // 128 * 128 + 128


def on_device(state, legendre, lat_weights, region, sources):
    wave_count = lax.axis_size("wave")
    waves_local = legendre.shape[0]
    waves_total = waves_local * wave_count
    degrees = legendre.shape[1]
    latitudes = legendre.shape[2]
    lat_rows = latitudes // wave_count
    state_rows = state.shape[2]
    level_count = state_rows // 4
    points = quadrature_points(waves_total)
    table_high, table_low = split_table(wave_table(waves_total, points))
    spectral = state[0]
    fourier_coef = jnp.einsum(
        "mrn,mnl->mrl", spectral.astype(jnp.bfloat16), legendre, preferred_element_type=jnp.float32
    )
    fourier_coef = fourier_coef.astype(jnp.bfloat16).reshape(
        waves_local, 2, 2 * level_count, latitudes
    )
    synthesis_scale = (2.0 * waves_total) ** (-0.5)
    coef = lax.all_to_all(fourier_coef, "wave", split_axis=3, concat_axis=0, tiled=True)
    gridded = synthesis_scale * jnp.einsum(
        "mckl,mcx->klx",
        jnp.concatenate([coef, coef], axis=1),
        jnp.concatenate([table_high, table_low], axis=1),
        preferred_element_type=jnp.float32,
    )
    lat_start = lax.axis_index("wave") * lat_rows
    local_weights = lax.dynamic_slice_in_dim(lat_weights, lat_start, lat_rows)
    wind_grid = gridded[:level_count]
    temper_grid = gridded[level_count:]
    fluxes = (
        jnp.concatenate([0.5 * wind_grid * wind_grid, wind_grid * temper_grid], axis=0)
        * local_weights[None, :, None]
    )
    fluxes = fluxes.astype(jnp.bfloat16)
    fourier = wave_table(waves_total, NLON).reshape(2 * waves_total, NLON).astype(jnp.bfloat16)
    lon_index = lax.broadcasted_iota(jnp.int32, (1, NLON), 1)
    lon_inside = (lon_index >= region[2]) & (lon_index < region[3])
    gram = jnp.einsum(
        "px,qx->pq",
        jnp.where(lon_inside, fourier, jnp.zeros((), jnp.bfloat16)),
        fourier,
        preferred_element_type=jnp.float32,
    )
    lowest = coef[:, :, -1].reshape(2 * waves_total, lat_rows).astype(jnp.float32)
    gram_lowest = jnp.dot(gram, lowest, precision=lax.Precision.HIGHEST)
    lat_index = lat_start + lax.broadcasted_iota(jnp.int32, (lat_rows,), 0)
    in_band = (lat_index >= region[0]) & (lat_index < region[1])
    region_part = jnp.sum(
        jnp.where(in_band, local_weights, 0.0)[None, :] * lowest * gram_lowest
    ) / (2.0 * waves_total)
    region_total = lax.psum(region_part, "wave")
    every_lat = lax.broadcasted_iota(jnp.int32, (latitudes,), 0)
    lat_inside = (every_lat >= region[0]) & (every_lat < region[1])
    region_weight = jnp.sum(jnp.where(lat_inside, lat_weights, 0.0)) * (
        region[3] - region[2]
    ).astype(jnp.float32)
    scores = (region_total / region_weight).reshape(1)
    analysis_scale = NLON ** (-0.5) * (NLON / points)
    flux_high = jnp.einsum("klx,mcx->mckl", fluxes, table_high, preferred_element_type=jnp.float32)
    flux_low = jnp.einsum("klx,mcx->mckl", fluxes, table_low, preferred_element_type=jnp.float32)
    flux_coef = (analysis_scale * (flux_high + flux_low)).astype(jnp.bfloat16)
    tendency = jnp.einsum(
        "mckl,mnl->mckn",
        lax.all_to_all(flux_coef, "wave", split_axis=0, concat_axis=3, tiled=True),
        legendre,
        preferred_element_type=jnp.float32,
    )
    wave_ids = lax.axis_index("wave") * waves_local + lax.broadcasted_iota(
        jnp.int32, (waves_local, 1, 1), 0
    )
    advection = advect_rate * wave_ids.astype(jnp.float32) / waves_total
    degree_ids = lax.broadcasted_iota(jnp.int32, (1, 1, degrees), 2).astype(jnp.float32)
    damping = 1.0 + ((degree_ids + 1.0) / degrees) ** 2
    spectral_split = spectral.reshape(waves_local, 2, 2 * level_count, degrees)
    real_part = (spectral_split[:, 0] + advection * tendency[:, 1]) / damping
    imag_part = (spectral_split[:, 1] - advection * tendency[:, 0]) / damping
    stepped = jnp.stack([real_part, imag_part], axis=1).reshape(1, waves_local, state_rows, degrees)
    source_member = sources[lax.axis_index("member")]
    shards = lax.all_gather(stepped.astype(jnp.bfloat16), "member", axis=0, tiled=True)
    cloned = lax.dynamic_slice_in_dim(shards, source_member, 1, axis=0).astype(jnp.float32)
    return (cloned, scores)


MESH = pl.DeviceIdType.MESH
WAVES = 4
CHUNKS = 2
PAIR = 4
ROWS = 32
SET_ROWS = ROWS // 2
LOCAL_WAVES = CHUNKS * PAIR
CHUNK_ROWS = PAIR * SET_ROWS
PART_ROWS = CHUNK_ROWS // WAVES
OWNED_ROWS = CHUNKS * PART_ROWS
STEPS = 4


def order_tables():
    forward = np.zeros((CHUNK_ROWS, CHUNK_ROWS))
    backward = np.zeros((CHUNK_ROWS, CHUNK_ROWS))
    for m in range(PAIR):
        for c in range(2):
            for f in range(2):
                for k in range(WAVES):
                    plain = ((m * 2 + c) * 2 + f) * WAVES + k
                    forward[((k * PAIR + m) * 2 + c) * 2 + f, plain] = 1.0
                    backward[plain, ((k * PAIR + m) * 2 + 1 - c) * 2 + f] = 1.0 - 2.0 * c
    return forward.astype(jnp.bfloat16), backward.astype(jnp.bfloat16)


def step_kernel(
    state_hbm, legendre_ref, weights_ref, region_ref, sources_ref, table_hbm,
    out_ref, score_ref,
    state_ref, set_ref, table_ref, synth_ref, analysis_ref, low_ref, low_sent, low_held,
    chosen, leg, sent, held, flux, back_sent, back, cross, crossed,
    *rest, scale, analysis_scale, waves_total, points,
):
    pools = rest[: 2 * STEPS]
    (
        state_sem, table_sem, leg_sem, go_send, go_recv, ret_send, ret_recv, score_send, score_recv,
        pass_send, pass_recv, cross_send, cross_recv,
    ) = rest[2 * STEPS :]
    me = lax.axis_index("wave")
    slot = lax.axis_index("member")
    z = slot // 2
    x = slot % 2
    half = z // 2
    inner = z % 2 != half % 2
    z_mate = (z + 1 - 2 * (z % 2)) * 2 + x
    x_mate = z * 2 + 1 - x
    far_inner = (2 - half) * 2 + x
    far_outer = (3 - 3 * half) * 2 + x
    here = slot - half * 4
    z_here = z_mate - half * 4
    degrees = state_ref.shape[1]
    lat_count = weights_ref.shape[0]
    f32 = jnp.float32
    bf16 = jnp.bfloat16
    levels = ROWS // 4

    loads = [
        pltpu.make_async_copy(legendre_ref.at[m], leg.at[m], leg_sem.at[m]) for m in range(LOCAL_WAVES)
    ]
    state_loads = [
        pltpu.make_async_copy(
            state_hbm.at[pl.ds(c * PAIR * ROWS, PAIR * ROWS)],
            state_ref.at[pl.ds(c * PAIR * ROWS, PAIR * ROWS)],
            state_sem.at[c],
        )
        for c in range(CHUNKS)
    ]
    table_load = pltpu.make_async_copy(table_hbm, table_ref, table_sem)
    for load in state_loads + [table_load] + loads:
        load.start()

    barrier = pltpu.get_barrier_semaphore()
    for d in range(1, WAVES):
        pl.semaphore_signal(
            barrier, inc=1, device_id={"wave": (me + d) % WAVES}, device_id_type=MESH
        )
    for mate in (z_mate, x_mate, far_inner):
        pl.semaphore_signal(barrier, inc=1, device_id={"member": mate}, device_id_type=MESH)

    @pl.when(inner)
    def _():
        pl.semaphore_signal(barrier, inc=1, device_id={"member": far_outer}, device_id_type=MESH)

    for c in range(CHUNKS):
        state_loads[c].wait()
        for m in range(c * PAIR, (c + 1) * PAIR):
            for group in range(4):
                for early in range(2):
                    first = m * SET_ROWS + group * WAVES
                    source = m * ROWS + group * levels + (1 - early) * WAVES
                    set_ref[1 - early, first : first + WAVES] = state_ref[source : source + WAVES]
        for g in range(c * 2, c * 2 + 2):
            pools[g][here] = set_ref[0, g * ROWS : (g + 1) * ROWS].astype(bf16)

    columns = fourier_columns = table_ref.shape[1] - 4 * 128
    table_load.wait()
    coef_rows = 4 * waves_total
    owner_of = lax.broadcasted_iota(jnp.int32, (2 * waves_total, coef_rows), 0)
    column = lax.broadcasted_iota(jnp.int32, (2 * waves_total, coef_rows), 1)
    widen = jnp.where(column // 2 == owner_of, 1.0, 0.0).astype(bf16)
    tall_owner = lax.broadcasted_iota(jnp.int32, (coef_rows, 2 * waves_total), 1)
    tall_row = lax.broadcasted_iota(jnp.int32, (coef_rows, 2 * waves_total), 0)
    lengthen = jnp.where(tall_row // 2 == tall_owner, 1.0, 0.0).astype(bf16)
    synth_column = lax.broadcasted_iota(jnp.int32, (points, coef_rows), 1) % 2
    analysis_row = lax.broadcasted_iota(jnp.int32, (coef_rows, points), 0) % 2
    for part in range(2):
        waves = table_ref[:, columns + part * 128 : columns + part * 128 + points]
        wide = lax.dot_general(
            waves, widen, (((0,), (0,)), ((), ())), preferred_element_type=f32
        )
        tall = jnp.dot(lengthen, waves, preferred_element_type=f32)
        for f in range(2):
            at = slice(f * points, (f + 1) * points)
            synth_ref[at, part * coef_rows : (part + 1) * coef_rows] = jnp.where(
                synth_column == f, wide, 0.0
            ).astype(bf16)
            analysis_ref[part, :, at] = jnp.where(analysis_row == f, tall, 0.0).astype(bf16)
    low, high = region_ref[2], region_ref[3]
    lon = lax.broadcasted_iota(jnp.int32, (1, fourier_columns), 1)
    lon_inside = jnp.where((lon >= low) & (lon < high), 1.0, 0.0)
    fourier = table_ref[:, :fourier_columns]
    gram = lax.dot_general(
        (fourier.astype(f32) * lon_inside).astype(bf16),
        fourier,
        (((1,), (1,)), ((), ())),
        preferred_element_type=f32,
    )
    gram_high = gram.astype(bf16)
    gram_low = (gram - gram_high.astype(f32)).astype(bf16)
    lat = lax.broadcasted_iota(jnp.int32, (1, lat_count), 1)
    weights = weights_ref[...].reshape(1, lat_count)
    region_weights = jnp.where((lat >= region_ref[0]) & (lat < region_ref[1]), weights, 0.0)
    weight_sum = jnp.sum(region_weights, axis=1, keepdims=True) * (high - low).astype(f32)

    @pl.when(inner)
    def _():
        pl.semaphore_wait(barrier, 7)

    @pl.when(jnp.logical_not(inner))
    def _():
        pl.semaphore_wait(barrier, 6)

    def member_copy(source, target, to, send_sem, recv_sem):
        return pltpu.make_async_remote_copy(
            src_ref=source, dst_ref=target, send_sem=send_sem, recv_sem=recv_sem,
            device_id={"member": to}, device_id_type=MESH,
        )

    def pass_copy(c, kind):
        block = pools[c].at[z_here if kind == 2 else here]
        return member_copy(
            block, block, z_mate if kind == 0 else x_mate, pass_send.at[kind, c], pass_recv.at[kind, c]
        )

    def cross_copy(c, far):
        return member_copy(
            cross.at[c, far],
            crossed.at[c],
            far_outer if far else far_inner,
            cross_send.at[far, c],
            cross_recv.at[c],
        )

    def half_index(member_slot):
        return jnp.clip(sources_ref[member_slot] - half * 4, 0, 3)

    inner_pick = half_index(far_inner)
    outer_pick = half_index(far_outer)
    origin = sources_ref[slot] - half * 4
    near = (origin >= 0) & (origin < 4)
    choice = jnp.clip(origin, 0, 3)

    def begin_pass(c):
        pass_copy(c, 0).start()
        if c % STEPS < 2:
            pass_copy(c, 1).start()

    for c in range(STEPS):
        begin_pass(c)

    def forward_pass(c):
        pass_copy(c, 0).wait_recv()
        pass_copy(c, 2).start()
        if c % STEPS + 2 < STEPS:
            pass_copy(c + 2, 1).start()

    def send_across(c):
        pass_copy(c, 1).wait_recv()
        pass_copy(c, 2).wait_recv()

        @pl.when(inner)
        def _():
            cross[c, 1] = pools[c][outer_pick]
            cross_copy(c, 1).start()
            cross[c, 0] = pools[c][inner_pick]
            cross_copy(c, 0).start()

    def wave_copy(source, target, h, c, d, send_sem, recv_sem):
        to = (me + d) % WAVES
        return pltpu.make_async_remote_copy(
            src_ref=source.at[h, pl.ds(pl.multiple_of(to * OWNED_ROWS + c * PART_ROWS, PART_ROWS), PART_ROWS)],
            dst_ref=target.at[h, pl.ds(pl.multiple_of(me * OWNED_ROWS + c * PART_ROWS, PART_ROWS), PART_ROWS)],
            send_sem=send_sem.at[h, d - 1, c],
            recv_sem=recv_sem.at[h, d - 1, c],
            device_id={"wave": to},
            device_id_type=MESH,
        )

    def low_copy(d):
        return pltpu.make_async_remote_copy(
            src_ref=low_sent,
            dst_ref=low_held.at[pl.ds(pl.multiple_of(me * 16, 16), 16)],
            send_sem=score_send.at[d - 1],
            recv_sem=score_recv.at[d - 1],
            device_id={"wave": (me + d) % WAVES},
            device_id_type=MESH,
        )

    my_rows = me * OWNED_ROWS
    mine = pl.ds(pl.multiple_of(my_rows, OWNED_ROWS), OWNED_ROWS)

    def go_copy(h, c, d):
        return wave_copy(sent, held, h, c, d, go_send, go_recv)

    def ret_copy(h, c, d):
        return wave_copy(back_sent, back, h, c, d, ret_send, ret_recv)

    def transform(h, c):
        parts = []
        for m in range(c * PAIR, (c + 1) * PAIR):
            rows = slice(m * SET_ROWS, (m + 1) * SET_ROWS)
            if h == 1:
                loads[m].wait()
                block = set_ref[1, rows].astype(bf16)
            else:
                block = chosen[rows]
            part = jnp.dot(block, leg[m], preferred_element_type=f32)
            parts.append(part)
            if h == 1:
                for real in range(2):
                    row = (real + 1) * (SET_ROWS // 2) - 1
                    low_ref[m * 2 + real : m * 2 + real + 1] = part[row : row + 1]
        coef = jnp.concatenate(parts, axis=0).astype(bf16)
        forward = table_ref[:, columns + 256 : columns + 256 + CHUNK_ROWS]
        ordered = jnp.dot(forward, coef, preferred_element_type=f32).astype(bf16)
        for w in range(WAVES):
            first = w * OWNED_ROWS + c * PART_ROWS
            sent[h, first : first + PART_ROWS] = ordered[w * PART_ROWS : (w + 1) * PART_ROWS]
        for d in (2, 1, 3):
            go_copy(h, c, d).start()

    def take_source(g):
        cross_copy(g, 0).wait_recv()
        return jnp.where(near, pools[g][choice], crossed[g])

    transform(1, 0)
    forward_pass(0)
    transform(1, 1)
    low_sent[...] = low_ref[...].astype(bf16)
    low_held[pl.ds(pl.multiple_of(me * 16, 16), 16)] = low_sent[...]
    for d in range(1, WAVES):
        low_copy(d).start()
    held[1, mine] = sent[1, mine]
    forward_pass(1)
    forward_pass(2)
    send_across(0)

    forward_pass(3)
    send_across(1)
    send_across(2)
    scaled = weights * (scale * scale)

    def grid_phase(h):
        for c in range(CHUNKS):
            for d in (2, 1, 3):
                go_copy(h, c, d).wait_recv()
        coefs = held[h]
        grid = jnp.dot(
            synth_ref[...], jnp.concatenate([coefs, coefs], axis=0), preferred_element_type=f32
        )
        wind = grid[:points]
        weighted = wind * scaled
        flux[h, :points] = (0.5 * weighted * wind).astype(bf16)
        flux[h, points:] = (weighted * grid[points:]).astype(bf16)
        fluxes = flux[h]
        back_sent[h] = (
            analysis_scale
            * (
                jnp.dot(analysis_ref[0], fluxes, preferred_element_type=f32)
                + jnp.dot(analysis_ref[1], fluxes, preferred_element_type=f32)
            )
        ).astype(bf16)
        for c in range(CHUNKS):
            for d in (2, 1, 3):
                ret_copy(h, c, d).start()
        back[h, mine] = back_sent[h, mine]

    grid_phase(1)
    send_across(3)

    def transform_sources(c):
        for g in range(c * 2, c * 2 + 2):
            chosen[g * ROWS : (g + 1) * ROWS] = take_source(g)
        transform(0, c)

    transform_sources(0)

    for d in range(1, WAVES):
        low_copy(d).wait()
    lowest = low_held[...]
    spread = jnp.dot(gram_high, lowest, preferred_element_type=f32) + jnp.dot(
        gram_low, lowest, preferred_element_type=f32
    )
    squares = jnp.sum(lowest.astype(f32) * spread, axis=0, keepdims=True) * (
        region_weights * (scale * scale)
    )
    score = jnp.sum(squares, axis=1, keepdims=True) / weight_sum
    score_ref[...] = jnp.broadcast_to(score, score_ref.shape)

    degree = lax.broadcasted_iota(jnp.int32, (1, degrees), 1).astype(f32)
    keep = 1.0 / (1.0 + ((degree + 1.0) / degrees) ** 2)
    backward = table_ref[:, columns + 384 : columns + 384 + CHUNK_ROWS]
    def tendencies(h, c):
        for d in (2, 1, 3):
            ret_copy(h, c, d).wait_recv()
        arrived = jnp.concatenate(
            [
                back[h, w * OWNED_ROWS + c * PART_ROWS : w * OWNED_ROWS + (c + 1) * PART_ROWS]
                for w in range(WAVES)
            ],
            axis=0,
        )
        plain = jnp.dot(backward, arrived, preferred_element_type=f32).astype(bf16)
        for i in range(PAIR):
            m = c * PAIR + i
            rows = slice(m * SET_ROWS, (m + 1) * SET_ROWS)
            tendency = lax.dot_general(
                plain[i * SET_ROWS : (i + 1) * SET_ROWS],
                leg[m],
                (((1,), (1,)), ((), ())),
                preferred_element_type=f32,
            )
            wave_id = (me * LOCAL_WAVES + m).astype(f32)
            advection = wave_id * (advect_rate / waves_total)
            source = set_ref[1, rows] if h == 1 else chosen[rows].astype(f32)
            stepped = (source + advection * tendency) * keep
            if h == 1:
                g = STEPS + m // 2
                pools[g][here, (m % 2) * SET_ROWS : (m % 2 + 1) * SET_ROWS] = stepped.astype(bf16)
                if m % 2 == 1:
                    begin_pass(g)
            else:
                put_rows(m, 0, stepped)

    def put_rows(m, late, values):
        for group in range(4):
            first = m * ROWS + group * levels + late * WAVES
            out_ref[first : first + WAVES] = values[group * WAVES : (group + 1) * WAVES]

    def put_cloned(g):
        block = take_source(g).astype(f32)
        for i in range(2):
            put_rows((g - STEPS) * 2 + i, 1, block[i * SET_ROWS : (i + 1) * SET_ROWS])

    tendencies(1, 0)
    tendencies(1, 1)
    forward_pass(STEPS)
    forward_pass(STEPS + 1)
    transform_sources(1)
    held[0, mine] = sent[0, mine]
    forward_pass(STEPS + 2)
    forward_pass(STEPS + 3)
    send_across(STEPS)
    send_across(STEPS + 1)
    grid_phase(0)
    send_across(STEPS + 2)
    send_across(STEPS + 3)
    tendencies(0, 0)
    put_cloned(STEPS)
    put_cloned(STEPS + 1)
    tendencies(0, 1)
    put_cloned(STEPS + 2)
    put_cloned(STEPS + 3)

    for h in range(2):
        for c in range(CHUNKS):
            for d in (2, 1, 3):
                go_copy(h, c, d).wait_send()
                ret_copy(h, c, d).wait_send()
    for c in range(2 * STEPS):
        for kind in range(3):
            pass_copy(c, kind).wait_send()

    @pl.when(inner)
    def _():
        for c in range(2 * STEPS):
            for far in range(2):
                cross_copy(c, far).wait_send()


def in_one_kernel(state, legendre, lat_weights, region, sources):
    waves_local, degrees, latitudes = legendre.shape
    waves_total = waves_local * WAVES
    points = quadrature_points(waves_total)
    table_high, table_low = split_table(wave_table(waves_total, points))
    fourier = wave_table(waves_total, NLON).astype(jnp.bfloat16)
    forward, backward = order_tables()
    unused = np.zeros((CHUNK_ROWS, 128 - CHUNK_ROWS), jnp.bfloat16)
    flat = [t.reshape(2 * waves_total, -1) for t in (fourier, table_high, table_low)]
    table = np.concatenate(flat + [forward, unused, backward, unused], axis=1)
    vmem = pl.BlockSpec(memory_space=pltpu.VMEM)
    smem = pl.BlockSpec(memory_space=pltpu.SMEM)
    hbm = pl.BlockSpec(memory_space=pl.ANY)
    rows = waves_local * ROWS
    block = (rows, degrees)
    grid_rows = (2, 4 * waves_total, latitudes)
    dma = pltpu.SemaphoreType.DMA
    bf16 = jnp.bfloat16
    stepped, scores = pl.pallas_call(
        functools.partial(
            step_kernel,
            scale=(2.0 * waves_total) ** -0.5,
            analysis_scale=NLON**-0.5 * (NLON / points),
            waves_total=waves_total,
            points=points,
        ),
        out_shape=(
            jax.ShapeDtypeStruct(block, jnp.float32),
            jax.ShapeDtypeStruct((8, 128), jnp.float32),
        ),
        in_specs=[hbm, hbm, vmem, smem, smem, hbm],
        out_specs=(vmem, vmem),
        scratch_shapes=[
            pltpu.VMEM(block, jnp.float32),
            pltpu.VMEM((2, rows // 2, degrees), jnp.float32),
            pltpu.VMEM(table.shape, bf16),
            pltpu.VMEM((2 * points, 8 * waves_total), bf16),
            pltpu.VMEM((2, 4 * waves_total, 2 * points), bf16),
            pltpu.VMEM((2 * waves_local, latitudes), jnp.float32),
            pltpu.VMEM((2 * waves_local, latitudes), bf16),
            pltpu.VMEM((2 * waves_total, latitudes), bf16),
            pltpu.VMEM((rows // 2, degrees), bf16),
            pltpu.VMEM(legendre.shape, bf16),
            pltpu.VMEM(grid_rows, bf16),
            pltpu.VMEM(grid_rows, bf16),
            pltpu.VMEM((2, 2 * points, latitudes), bf16),
            pltpu.VMEM(grid_rows, bf16),
            pltpu.VMEM(grid_rows, bf16),
            pltpu.VMEM((2 * STEPS, 2, ROWS, degrees), bf16),
            pltpu.VMEM((2 * STEPS, ROWS, degrees), bf16),
        ]
        + [pltpu.VMEM((4, ROWS, degrees), bf16)] * (2 * STEPS)
        + [
            dma((CHUNKS,)),
            dma,
            dma((LOCAL_WAVES,)),
            dma((2, WAVES - 1, CHUNKS)),
            dma((2, WAVES - 1, CHUNKS)),
            dma((2, WAVES - 1, CHUNKS)),
            dma((2, WAVES - 1, CHUNKS)),
            dma((WAVES - 1,)),
            dma((WAVES - 1,)),
            dma((3, 2 * STEPS)),
            dma((3, 2 * STEPS)),
            dma((2, 2 * STEPS)),
            dma((2 * STEPS,)),
        ],
        compiler_params=pltpu.CompilerParams(
            collective_id=0, has_side_effects=True, vmem_limit_bytes=56 * 1024 * 1024
        ),
    )(state.reshape(block), legendre, lat_weights, region, sources, jnp.asarray(table))
    return (stepped.reshape(state.shape), scores[0, :1])


def solution(mesh):
    in_specs = (P("member", "wave", None, None), P("wave", None, None), P(), P(), P())
    out_specs = (P("member", "wave", None, None), P("member"))

    def run(state, legendre, lat_weights, region, sources):
        shape = (state.shape[1] // mesh.shape["wave"], state.shape[2], state.shape[3], legendre.shape[2])
        fits = mesh.shape["wave"] == 4 and mesh.shape["member"] == 8 and shape == (8, 32, 640, 640)
        return jax.shard_map(
            in_one_kernel if fits else on_device,
            mesh=mesh,
            in_specs=in_specs,
            out_specs=out_specs,
            check_vma=False,
        )(state, legendre, lat_weights, region, sources)

    return run
```

```python
import functools

import jax
import jax.numpy as jnp
import numpy as np
from jax import lax
from jax.experimental import pallas as pl
from jax.experimental.pallas import tpu as pltpu
from jax.sharding import PartitionSpec as P

NLON = 2560


advect_rate = 2.0


def wave_table(waves_total, points):
    wave_index = np.arange(waves_total)[:, None]
    angles = (wave_index * np.arange(points)[None, :] % points) * (2.0 * np.pi / points)
    return np.stack([np.cos(angles), -np.sin(angles)], axis=1)


def split_table(table):
    high = table.astype(jnp.bfloat16)
    low = (table - high.astype(np.float64)).astype(jnp.bfloat16)
    return high, low


def quadrature_points(waves_total):
    return (3 * (waves_total - 1)) // 128 * 128 + 128


def on_device(state, legendre, lat_weights, region, sources):
    wave_count = lax.axis_size("wave")
    waves_local = legendre.shape[0]
    waves_total = waves_local * wave_count
    degrees = legendre.shape[1]
    latitudes = legendre.shape[2]
    lat_rows = latitudes // wave_count
    state_rows = state.shape[2]
    level_count = state_rows // 4
    points = quadrature_points(waves_total)
    table_high, table_low = split_table(wave_table(waves_total, points))
    spectral = state[0]
    fourier_coef = jnp.einsum(
        "mrn,mnl->mrl", spectral.astype(jnp.bfloat16), legendre, preferred_element_type=jnp.float32
    )
    fourier_coef = fourier_coef.astype(jnp.bfloat16).reshape(
        waves_local, 2, 2 * level_count, latitudes
    )
    synthesis_scale = (2.0 * waves_total) ** (-0.5)
    coef = lax.all_to_all(fourier_coef, "wave", split_axis=3, concat_axis=0, tiled=True)
    gridded = synthesis_scale * jnp.einsum(
        "mckl,mcx->klx",
        jnp.concatenate([coef, coef], axis=1),
        jnp.concatenate([table_high, table_low], axis=1),
        preferred_element_type=jnp.float32,
    )
    lat_start = lax.axis_index("wave") * lat_rows
    local_weights = lax.dynamic_slice_in_dim(lat_weights, lat_start, lat_rows)
    wind_grid = gridded[:level_count]
    temper_grid = gridded[level_count:]
    fluxes = (
        jnp.concatenate([0.5 * wind_grid * wind_grid, wind_grid * temper_grid], axis=0)
        * local_weights[None, :, None]
    )
    fluxes = fluxes.astype(jnp.bfloat16)
    fourier = wave_table(waves_total, NLON).reshape(2 * waves_total, NLON).astype(jnp.bfloat16)
    lon_index = lax.broadcasted_iota(jnp.int32, (1, NLON), 1)
    lon_inside = (lon_index >= region[2]) & (lon_index < region[3])
    gram = jnp.einsum(
        "px,qx->pq",
        jnp.where(lon_inside, fourier, jnp.zeros((), jnp.bfloat16)),
        fourier,
        preferred_element_type=jnp.float32,
    )
    lowest = coef[:, :, -1].reshape(2 * waves_total, lat_rows).astype(jnp.float32)
    gram_lowest = jnp.dot(gram, lowest, precision=lax.Precision.HIGHEST)
    lat_index = lat_start + lax.broadcasted_iota(jnp.int32, (lat_rows,), 0)
    in_band = (lat_index >= region[0]) & (lat_index < region[1])
    region_part = jnp.sum(
        jnp.where(in_band, local_weights, 0.0)[None, :] * lowest * gram_lowest
    ) / (2.0 * waves_total)
    region_total = lax.psum(region_part, "wave")
    every_lat = lax.broadcasted_iota(jnp.int32, (latitudes,), 0)
    lat_inside = (every_lat >= region[0]) & (every_lat < region[1])
    region_weight = jnp.sum(jnp.where(lat_inside, lat_weights, 0.0)) * (
        region[3] - region[2]
    ).astype(jnp.float32)
    scores = (region_total / region_weight).reshape(1)
    analysis_scale = NLON ** (-0.5) * (NLON / points)
    flux_high = jnp.einsum("klx,mcx->mckl", fluxes, table_high, preferred_element_type=jnp.float32)
    flux_low = jnp.einsum("klx,mcx->mckl", fluxes, table_low, preferred_element_type=jnp.float32)
    flux_coef = (analysis_scale * (flux_high + flux_low)).astype(jnp.bfloat16)
    tendency = jnp.einsum(
        "mckl,mnl->mckn",
        lax.all_to_all(flux_coef, "wave", split_axis=0, concat_axis=3, tiled=True),
        legendre,
        preferred_element_type=jnp.float32,
    )
    wave_ids = lax.axis_index("wave") * waves_local + lax.broadcasted_iota(
        jnp.int32, (waves_local, 1, 1), 0
    )
    advection = advect_rate * wave_ids.astype(jnp.float32) / waves_total
    degree_ids = lax.broadcasted_iota(jnp.int32, (1, 1, degrees), 2).astype(jnp.float32)
    damping = 1.0 + ((degree_ids + 1.0) / degrees) ** 2
    spectral_split = spectral.reshape(waves_local, 2, 2 * level_count, degrees)
    real_part = (spectral_split[:, 0] + advection * tendency[:, 1]) / damping
    imag_part = (spectral_split[:, 1] - advection * tendency[:, 0]) / damping
    stepped = jnp.stack([real_part, imag_part], axis=1).reshape(1, waves_local, state_rows, degrees)
    source_member = sources[lax.axis_index("member")]
    shards = lax.all_gather(stepped.astype(jnp.bfloat16), "member", axis=0, tiled=True)
    cloned = lax.dynamic_slice_in_dim(shards, source_member, 1, axis=0).astype(jnp.float32)
    return (cloned, scores)


MESH = pl.DeviceIdType.MESH
WAVES = 4
CHUNKS = 2
PAIR = 4
ROWS = 32
SET_ROWS = ROWS // 2
LOCAL_WAVES = CHUNKS * PAIR
CHUNK_ROWS = PAIR * SET_ROWS
PART_ROWS = CHUNK_ROWS // WAVES
OWNED_ROWS = CHUNKS * PART_ROWS
STEPS = 4


def order_tables():
    forward = np.zeros((CHUNK_ROWS, CHUNK_ROWS))
    backward = np.zeros((CHUNK_ROWS, CHUNK_ROWS))
    for m in range(PAIR):
        for c in range(2):
            for f in range(2):
                for k in range(WAVES):
                    plain = ((m * 2 + c) * 2 + f) * WAVES + k
                    forward[((k * PAIR + m) * 2 + c) * 2 + f, plain] = 1.0
                    backward[plain, ((k * PAIR + m) * 2 + 1 - c) * 2 + f] = 1.0 - 2.0 * c
    return forward.astype(jnp.bfloat16), backward.astype(jnp.bfloat16)


def step_kernel(
    state_hbm, legendre_ref, weights_ref, region_ref, sources_ref, table_hbm,
    out_ref, score_ref,
    state_ref, set_ref, table_ref, synth_ref, analysis_ref, low_ref, low_sent, low_held,
    chosen, leg, sent, held, flux, back_sent, back, cross, crossed,
    *rest, scale, analysis_scale, waves_total, points,
):
    pools = rest[: 2 * STEPS]
    (
        state_sem, table_sem, leg_sem, go_send, go_recv, ret_send, ret_recv, score_send, score_recv,
        pass_send, pass_recv, cross_send, cross_recv,
    ) = rest[2 * STEPS :]
    me = lax.axis_index("wave")
    slot = lax.axis_index("member")
    z = slot // 2
    x = slot % 2
    half = z // 2
    inner = z % 2 != half % 2
    z_mate = (z + 1 - 2 * (z % 2)) * 2 + x
    x_mate = z * 2 + 1 - x
    far_inner = (2 - half) * 2 + x
    far_outer = (3 - 3 * half) * 2 + x
    here = slot - half * 4
    z_here = z_mate - half * 4
    degrees = state_ref.shape[1]
    lat_count = weights_ref.shape[0]
    f32 = jnp.float32
    bf16 = jnp.bfloat16
    levels = ROWS // 4

    loads = [
        pltpu.make_async_copy(legendre_ref.at[m], leg.at[m], leg_sem.at[m]) for m in range(LOCAL_WAVES)
    ]
    state_loads = [
        pltpu.make_async_copy(
            state_hbm.at[pl.ds(c * PAIR * ROWS, PAIR * ROWS)],
            state_ref.at[pl.ds(c * PAIR * ROWS, PAIR * ROWS)],
            state_sem.at[c],
        )
        for c in range(CHUNKS)
    ]
    table_load = pltpu.make_async_copy(table_hbm, table_ref, table_sem)
    for load in state_loads + [table_load] + loads:
        load.start()

    barrier = pltpu.get_barrier_semaphore()
    for d in range(1, WAVES):
        pl.semaphore_signal(
            barrier, inc=1, device_id={"wave": (me + d) % WAVES}, device_id_type=MESH
        )
    for mate in (z_mate, x_mate, far_inner):
        pl.semaphore_signal(barrier, inc=1, device_id={"member": mate}, device_id_type=MESH)

    @pl.when(inner)
    def _():
        pl.semaphore_signal(barrier, inc=1, device_id={"member": far_outer}, device_id_type=MESH)

    for c in range(CHUNKS):
        state_loads[c].wait()
        for m in range(c * PAIR, (c + 1) * PAIR):
            for group in range(4):
                for early in range(2):
                    first = m * SET_ROWS + group * WAVES
                    source = m * ROWS + group * levels + (1 - early) * WAVES
                    set_ref[1 - early, first : first + WAVES] = state_ref[source : source + WAVES]
        for g in range(c * 2, c * 2 + 2):
            pools[g][here] = set_ref[0, g * ROWS : (g + 1) * ROWS].astype(bf16)

    @pl.when(inner)
    def _():
        pl.semaphore_wait(barrier, 7)

    @pl.when(jnp.logical_not(inner))
    def _():
        pl.semaphore_wait(barrier, 6)

    def member_copy(source, target, to, send_sem, recv_sem):
        return pltpu.make_async_remote_copy(
            src_ref=source, dst_ref=target, send_sem=send_sem, recv_sem=recv_sem,
            device_id={"member": to}, device_id_type=MESH,
        )

    def pass_copy(c, kind):
        block = pools[c].at[z_here if kind == 2 else here]
        return member_copy(
            block, block, z_mate if kind == 0 else x_mate, pass_send.at[kind, c], pass_recv.at[kind, c]
        )

    def cross_copy(c, far):
        return member_copy(
            cross.at[c, far],
            crossed.at[c],
            far_outer if far else far_inner,
            cross_send.at[far, c],
            cross_recv.at[c],
        )

    def half_index(member_slot):
        return jnp.clip(sources_ref[member_slot] - half * 4, 0, 3)

    inner_pick = half_index(far_inner)
    outer_pick = half_index(far_outer)
    origin = sources_ref[slot] - half * 4
    near = (origin >= 0) & (origin < 4)
    choice = jnp.clip(origin, 0, 3)

    def begin_pass(c):
        pass_copy(c, 0).start()
        if c % STEPS < 2:
            pass_copy(c, 1).start()

    for c in range(STEPS):
        begin_pass(c)

    def forward_pass(c):
        pass_copy(c, 0).wait_recv()
        pass_copy(c, 2).start()
        if c % STEPS + 2 < STEPS:
            pass_copy(c + 2, 1).start()

    def send_across(c):
        pass_copy(c, 1).wait_recv()
        pass_copy(c, 2).wait_recv()

        @pl.when(inner)
        def _():
            cross[c, 1] = pools[c][outer_pick]
            cross_copy(c, 1).start()
            cross[c, 0] = pools[c][inner_pick]
            cross_copy(c, 0).start()

    def wave_copy(source, target, h, c, d, send_sem, recv_sem):
        to = (me + d) % WAVES
        return pltpu.make_async_remote_copy(
            src_ref=source.at[h, pl.ds(pl.multiple_of(to * OWNED_ROWS + c * PART_ROWS, PART_ROWS), PART_ROWS)],
            dst_ref=target.at[h, pl.ds(pl.multiple_of(me * OWNED_ROWS + c * PART_ROWS, PART_ROWS), PART_ROWS)],
            send_sem=send_sem.at[h, d - 1, c],
            recv_sem=recv_sem.at[h, d - 1, c],
            device_id={"wave": to},
            device_id_type=MESH,
        )

    def low_copy(d):
        return pltpu.make_async_remote_copy(
            src_ref=low_sent,
            dst_ref=low_held.at[pl.ds(pl.multiple_of(me * 16, 16), 16)],
            send_sem=score_send.at[d - 1],
            recv_sem=score_recv.at[d - 1],
            device_id={"wave": (me + d) % WAVES},
            device_id_type=MESH,
        )

    my_rows = me * OWNED_ROWS
    mine = pl.ds(pl.multiple_of(my_rows, OWNED_ROWS), OWNED_ROWS)
    columns = fourier_columns = table_ref.shape[1] - 4 * 128

    def go_copy(h, c, d):
        return wave_copy(sent, held, h, c, d, go_send, go_recv)

    def ret_copy(h, c, d):
        return wave_copy(back_sent, back, h, c, d, ret_send, ret_recv)

    def transform(h, c):
        parts = []
        for m in range(c * PAIR, (c + 1) * PAIR):
            rows = slice(m * SET_ROWS, (m + 1) * SET_ROWS)
            if h == 1:
                loads[m].wait()
                block = set_ref[1, rows].astype(bf16)
            else:
                block = chosen[rows]
            part = jnp.dot(block, leg[m], preferred_element_type=f32)
            parts.append(part)
            if h == 1:
                for real in range(2):
                    row = (real + 1) * (SET_ROWS // 2) - 1
                    low_ref[m * 2 + real : m * 2 + real + 1] = part[row : row + 1]
        coef = jnp.concatenate(parts, axis=0).astype(bf16)
        forward = table_ref[:, columns + 256 : columns + 256 + CHUNK_ROWS]
        ordered = jnp.dot(forward, coef, preferred_element_type=f32).astype(bf16)
        for w in range(WAVES):
            first = w * OWNED_ROWS + c * PART_ROWS
            sent[h, first : first + PART_ROWS] = ordered[w * PART_ROWS : (w + 1) * PART_ROWS]
        for d in (2, 1, 3):
            go_copy(h, c, d).start()

    def take_source(g):
        cross_copy(g, 0).wait_recv()
        return jnp.where(near, pools[g][choice], crossed[g])

    table_load.wait()
    transform(1, 0)
    forward_pass(0)
    transform(1, 1)
    low_sent[...] = low_ref[...].astype(bf16)
    low_held[pl.ds(pl.multiple_of(me * 16, 16), 16)] = low_sent[...]
    for d in range(1, WAVES):
        low_copy(d).start()
    held[1, mine] = sent[1, mine]
    forward_pass(1)
    forward_pass(2)
    send_across(0)

    coef_rows = 4 * waves_total
    owner_of = lax.broadcasted_iota(jnp.int32, (2 * waves_total, coef_rows), 0)
    column = lax.broadcasted_iota(jnp.int32, (2 * waves_total, coef_rows), 1)
    widen = jnp.where(column // 2 == owner_of, 1.0, 0.0).astype(bf16)
    tall_owner = lax.broadcasted_iota(jnp.int32, (coef_rows, 2 * waves_total), 1)
    tall_row = lax.broadcasted_iota(jnp.int32, (coef_rows, 2 * waves_total), 0)
    lengthen = jnp.where(tall_row // 2 == tall_owner, 1.0, 0.0).astype(bf16)
    synth_column = lax.broadcasted_iota(jnp.int32, (points, coef_rows), 1) % 2
    analysis_row = lax.broadcasted_iota(jnp.int32, (coef_rows, points), 0) % 2
    for part in range(2):
        waves = table_ref[:, columns + part * 128 : columns + part * 128 + points]
        wide = lax.dot_general(
            waves, widen, (((0,), (0,)), ((), ())), preferred_element_type=f32
        )
        tall = jnp.dot(lengthen, waves, preferred_element_type=f32)
        for f in range(2):
            at = slice(f * points, (f + 1) * points)
            synth_ref[at, part * coef_rows : (part + 1) * coef_rows] = jnp.where(
                synth_column == f, wide, 0.0
            ).astype(bf16)
            analysis_ref[part, :, at] = jnp.where(analysis_row == f, tall, 0.0).astype(bf16)
    forward_pass(3)
    send_across(1)

    low, high = region_ref[2], region_ref[3]
    lon = lax.broadcasted_iota(jnp.int32, (1, fourier_columns), 1)
    lon_inside = jnp.where((lon >= low) & (lon < high), 1.0, 0.0)
    fourier = table_ref[:, :fourier_columns]
    gram = lax.dot_general(
        (fourier.astype(f32) * lon_inside).astype(bf16),
        fourier,
        (((1,), (1,)), ((), ())),
        preferred_element_type=f32,
    )
    gram_high = gram.astype(bf16)
    gram_low = (gram - gram_high.astype(f32)).astype(bf16)
    lat = lax.broadcasted_iota(jnp.int32, (1, lat_count), 1)
    weights = weights_ref[...].reshape(1, lat_count)
    region_weights = jnp.where((lat >= region_ref[0]) & (lat < region_ref[1]), weights, 0.0)
    weight_sum = jnp.sum(region_weights, axis=1, keepdims=True) * (high - low).astype(f32)

    send_across(2)
    scaled = weights * (scale * scale)

    def grid_phase(h):
        for c in range(CHUNKS):
            for d in (2, 1, 3):
                go_copy(h, c, d).wait_recv()
        coefs = held[h]
        grid = jnp.dot(
            synth_ref[...], jnp.concatenate([coefs, coefs], axis=0), preferred_element_type=f32
        )
        wind = grid[:points]
        weighted = wind * scaled
        flux[h, :points] = (0.5 * weighted * wind).astype(bf16)
        flux[h, points:] = (weighted * grid[points:]).astype(bf16)
        fluxes = flux[h]
        back_sent[h] = (
            analysis_scale
            * (
                jnp.dot(analysis_ref[0], fluxes, preferred_element_type=f32)
                + jnp.dot(analysis_ref[1], fluxes, preferred_element_type=f32)
            )
        ).astype(bf16)
        for c in range(CHUNKS):
            for d in (2, 1, 3):
                ret_copy(h, c, d).start()
        back[h, mine] = back_sent[h, mine]

    grid_phase(1)
    send_across(3)

    def transform_sources(c):
        for g in range(c * 2, c * 2 + 2):
            chosen[g * ROWS : (g + 1) * ROWS] = take_source(g)
        transform(0, c)

    transform_sources(0)

    for d in range(1, WAVES):
        low_copy(d).wait()
    lowest = low_held[...]
    spread = jnp.dot(gram_high, lowest, preferred_element_type=f32) + jnp.dot(
        gram_low, lowest, preferred_element_type=f32
    )
    squares = jnp.sum(lowest.astype(f32) * spread, axis=0, keepdims=True) * (
        region_weights * (scale * scale)
    )
    score = jnp.sum(squares, axis=1, keepdims=True) / weight_sum
    score_ref[0] = jnp.sum(score)

    degree = lax.broadcasted_iota(jnp.int32, (1, degrees), 1).astype(f32)
    keep = 1.0 / (1.0 + ((degree + 1.0) / degrees) ** 2)
    backward = table_ref[:, columns + 384 : columns + 384 + CHUNK_ROWS]
    def tendencies(h, c):
        for d in (2, 1, 3):
            ret_copy(h, c, d).wait_recv()
        arrived = jnp.concatenate(
            [
                back[h, w * OWNED_ROWS + c * PART_ROWS : w * OWNED_ROWS + (c + 1) * PART_ROWS]
                for w in range(WAVES)
            ],
            axis=0,
        )
        plain = jnp.dot(backward, arrived, preferred_element_type=f32).astype(bf16)
        for i in range(PAIR):
            m = c * PAIR + i
            rows = slice(m * SET_ROWS, (m + 1) * SET_ROWS)
            tendency = lax.dot_general(
                plain[i * SET_ROWS : (i + 1) * SET_ROWS],
                leg[m],
                (((1,), (1,)), ((), ())),
                preferred_element_type=f32,
            )
            wave_id = (me * LOCAL_WAVES + m).astype(f32)
            advection = wave_id * (advect_rate / waves_total)
            source = set_ref[1, rows] if h == 1 else chosen[rows].astype(f32)
            stepped = (source + advection * tendency) * keep
            if h == 1:
                g = STEPS + m // 2
                pools[g][here, (m % 2) * SET_ROWS : (m % 2 + 1) * SET_ROWS] = stepped.astype(bf16)
                if m % 2 == 1:
                    begin_pass(g)
            else:
                put_rows(m, 0, stepped)

    def put_rows(m, late, values):
        for group in range(4):
            first = m * ROWS + group * levels + late * WAVES
            out_ref[first : first + WAVES] = values[group * WAVES : (group + 1) * WAVES]

    def put_cloned(g):
        block = take_source(g).astype(f32)
        for i in range(2):
            put_rows((g - STEPS) * 2 + i, 1, block[i * SET_ROWS : (i + 1) * SET_ROWS])

    tendencies(1, 0)
    tendencies(1, 1)
    forward_pass(STEPS)
    forward_pass(STEPS + 1)
    transform_sources(1)
    held[0, mine] = sent[0, mine]
    forward_pass(STEPS + 2)
    forward_pass(STEPS + 3)
    send_across(STEPS)
    send_across(STEPS + 1)
    grid_phase(0)
    send_across(STEPS + 2)
    send_across(STEPS + 3)
    tendencies(0, 0)
    put_cloned(STEPS)
    put_cloned(STEPS + 1)
    tendencies(0, 1)
    put_cloned(STEPS + 2)
    put_cloned(STEPS + 3)

    for h in range(2):
        for c in range(CHUNKS):
            for d in (2, 1, 3):
                go_copy(h, c, d).wait_send()
                ret_copy(h, c, d).wait_send()
    for c in range(2 * STEPS):
        for kind in range(3):
            pass_copy(c, kind).wait_send()

    @pl.when(inner)
    def _():
        for c in range(2 * STEPS):
            for far in range(2):
                cross_copy(c, far).wait_send()


def in_one_kernel(state, legendre, lat_weights, region, sources):
    waves_local, degrees, latitudes = legendre.shape
    waves_total = waves_local * WAVES
    points = quadrature_points(waves_total)
    table_high, table_low = split_table(wave_table(waves_total, points))
    fourier = wave_table(waves_total, NLON).astype(jnp.bfloat16)
    forward, backward = order_tables()
    unused = np.zeros((CHUNK_ROWS, 128 - CHUNK_ROWS), jnp.bfloat16)
    flat = [t.reshape(2 * waves_total, -1) for t in (fourier, table_high, table_low)]
    table = np.concatenate(flat + [forward, unused, backward, unused], axis=1)
    vmem = pl.BlockSpec(memory_space=pltpu.VMEM)
    smem = pl.BlockSpec(memory_space=pltpu.SMEM)
    hbm = pl.BlockSpec(memory_space=pl.ANY)
    rows = waves_local * ROWS
    block = (rows, degrees)
    grid_rows = (2, 4 * waves_total, latitudes)
    dma = pltpu.SemaphoreType.DMA
    bf16 = jnp.bfloat16
    stepped, scores = pl.pallas_call(
        functools.partial(
            step_kernel,
            scale=(2.0 * waves_total) ** -0.5,
            analysis_scale=NLON**-0.5 * (NLON / points),
            waves_total=waves_total,
            points=points,
        ),
        out_shape=(
            jax.ShapeDtypeStruct(block, jnp.float32),
            jax.ShapeDtypeStruct((1,), jnp.float32),
        ),
        in_specs=[hbm, hbm, vmem, smem, smem, hbm],
        out_specs=(vmem, smem),
        scratch_shapes=[
            pltpu.VMEM(block, jnp.float32),
            pltpu.VMEM((2, rows // 2, degrees), jnp.float32),
            pltpu.VMEM(table.shape, bf16),
            pltpu.VMEM((2 * points, 8 * waves_total), bf16),
            pltpu.VMEM((2, 4 * waves_total, 2 * points), bf16),
            pltpu.VMEM((2 * waves_local, latitudes), jnp.float32),
            pltpu.VMEM((2 * waves_local, latitudes), bf16),
            pltpu.VMEM((2 * waves_total, latitudes), bf16),
            pltpu.VMEM((rows // 2, degrees), bf16),
            pltpu.VMEM(legendre.shape, bf16),
            pltpu.VMEM(grid_rows, bf16),
            pltpu.VMEM(grid_rows, bf16),
            pltpu.VMEM((2, 2 * points, latitudes), bf16),
            pltpu.VMEM(grid_rows, bf16),
            pltpu.VMEM(grid_rows, bf16),
            pltpu.VMEM((2 * STEPS, 2, ROWS, degrees), bf16),
            pltpu.VMEM((2 * STEPS, ROWS, degrees), bf16),
        ]
        + [pltpu.VMEM((4, ROWS, degrees), bf16)] * (2 * STEPS)
        + [
            dma((CHUNKS,)),
            dma,
            dma((LOCAL_WAVES,)),
            dma((2, WAVES - 1, CHUNKS)),
            dma((2, WAVES - 1, CHUNKS)),
            dma((2, WAVES - 1, CHUNKS)),
            dma((2, WAVES - 1, CHUNKS)),
            dma((WAVES - 1,)),
            dma((WAVES - 1,)),
            dma((3, 2 * STEPS)),
            dma((3, 2 * STEPS)),
            dma((2, 2 * STEPS)),
            dma((2 * STEPS,)),
        ],
        compiler_params=pltpu.CompilerParams(
            collective_id=0, has_side_effects=True, vmem_limit_bytes=56 * 1024 * 1024
        ),
    )(state.reshape(block), legendre, lat_weights, region, sources, jnp.asarray(table))
    return (stepped.reshape(state.shape), scores)


def solution(mesh):
    in_specs = (P("member", "wave", None, None), P("wave", None, None), P(), P(), P())
    out_specs = (P("member", "wave", None, None), P("member"))

    def run(state, legendre, lat_weights, region, sources):
        shape = (state.shape[1] // mesh.shape["wave"], state.shape[2], state.shape[3], legendre.shape[2])
        fits = mesh.shape["wave"] == 4 and mesh.shape["member"] == 8 and shape == (8, 32, 640, 640)
        return jax.shard_map(
            in_one_kernel if fits else on_device,
            mesh=mesh,
            in_specs=in_specs,
            out_specs=out_specs,
            check_vma=False,
        )(state, legendre, lat_weights, region, sources)

    return run
```
